512 devices in a mesh: grp: 64 (over z, y_lo, core), mdl: 8 (over y_hi, x).
Axes of the slice: x: 4, y: 8 (y_hi: 2, y_lo: 4; y = y_hi * 4 + y_lo), z: 8, core: 2. Of those that a mesh axis runs over, the one named last changes fastest.
Arguments:
- model: float32 [4096, 8, 128], P(None, 'mdl'), may hold values from -1 to 1.5
- source: float32 [1024, 3, 8, 4096], P(('grp', 'mdl')), may hold values from -6 to 6
- observed: float32 [1024, 3, 8, 4096], P(('grp', 'mdl')), may hold values from -6 to 6
- owner_ids: int32 [1024, 8, 1], P(('grp', 'mdl')), may hold values from 0 to 7; in each aligned block of 16 rows (0 to 15, 16 to 31, ..., all dimensions but the last counted through in order) at most 4 rows name the same one
- offsets: int32 [1024, 8], P(('grp', 'mdl')), may hold values from 0 to 4064
- lengths: int32 [1024, 8], P(('grp', 'mdl')), may hold values from 1 to 32, 192 in all within a row
Outputs:
- gradient: float32 [4096, 8, 128], P('grp', 'mdl')
The draws below stay inside these ranges and needn't reach their ends.
Inputs may be any that keep to these rules, and one draw needn't show every extreme that they name: `owner_ids`: among the layers of the soundings of one device (aligned blocks of 16 layers), no owner is named by more than 4 layers; in some blocks one owner is named by exactly 4. A layer covers rows offsets to offsets + lengths - 1 of its owner's block. The first lengths rows of a layer lie in the earth, the others in the air; a sounding's 8 lengths sum to 192.
All inputs are finite; a program needn't handle non-finite values.
Results may differ from the reference program's by a relative error of at most 0.0003.
Values sent between devices are 32-bit elements; how exact they have to be, the bound alone decides.
A program may use at most 64 MiB of HBM per device.

```python
import math
import jax
import jax.numpy as jnp
import numpy as np
from jax import lax

LY = 64
LZ = 8
S_DEV = 2
STEPS_FWD = 4
STEPS_ADJ = 4
BLK_ROWS = 4096
LAYER = 4096
TILE = 32
OWNERS = 8
SOUNDINGS = 1024
CAP_T = 4


def place_ends(array, own_key, smallest, top_value):
    dims = array.shape
    spot = [jax.random.randint(jax.random.fold_in(own_key, axis), (), 0, dims[axis]) for axis in range(len(dims))]
    array = array.at[tuple(spot)].set(smallest)
    longest = dims.index(max(dims))
    spot[longest] = (spot[longest] + 1) % dims[longest]
    return array.at[tuple(spot)].set(top_value)


def shard_levels(stream_key, shape, cuts, least, high):
    level = 1.0
    for dim, shards_of in cuts:
        draws = jax.random.uniform(jax.random.fold_in(jax.random.fold_in(stream_key, 6), dim), (shards_of,), jnp.float32, least / len(cuts), high / len(cuts))
        level = level * jnp.repeat(jnp.exp(draws), shape[dim] // shards_of).reshape((-1,) + (1,) * (len(shape) - 1 - dim))
    return level


def profile(count, total, bound, skew):
    loads = [(1 << 20) // math.isqrt(standing ** skew) + 1 for standing in range(2, count + 1)]
    spare, holding = total - bound - (count - 1), [1] * (count - 1)
    while spare > 0:
        free = [i for i in range(count - 1) if holding[i] < bound]
        pool, budget = sum([loads[i] for i in free]), spare
        for i in free:
            addition = min(bound - holding[i], max(1, budget * loads[i] // pool), spare)
            holding[i] = holding[i] + addition
            spare = spare - addition
    return np.array([bound] + holding)


def ragged(own_key, number_of, total, reach, skew):
    if number_of == 2:
        one = jax.random.randint(own_key, (), max(1, total - reach), min(reach, total - 1) + 1)
        return jnp.stack([one, total - one])
    tallies = jnp.asarray(profile(number_of, total, reach, skew), jnp.int32)
    couples = (number_of - 1) // 2
    donor, receiver = tallies[1:1 + 2 * couples:2], tallies[2:2 + 2 * couples:2]
    margin = jnp.minimum(donor - 1, reach - receiver)
    moved = jax.random.randint(jax.random.fold_in(own_key, 1), (couples,), 0, 1 << 20) % (margin + 1)
    tallies = tallies.at[1:1 + 2 * couples:2].set(donor - moved).at[2:2 + 2 * couples:2].set(receiver + moved)
    return tallies[jax.random.permutation(jax.random.fold_in(own_key, 2), number_of)]


def shared_out(stream_key, own, number, rows, count, top, limit, skew):
    order = jax.random.permutation(stream_key, count)
    crowded, usual = shares(count, rows * top, limit, skew, True), shares(count, rows * top, limit, skew, False)
    places = jnp.arange(count)

    def named(sizes, offset_by):
        used = int((sizes > 0).sum())
        fixed = max(1, used // 4)
        shifted = fixed + (places - fixed + offset_by * (used - fixed)) % max(1, count - fixed)
        return jnp.zeros((count,), jnp.int32).at[order[jnp.where(places < fixed, places, shifted)]].set(jnp.asarray(sizes, jnp.int32))

    sizes = jnp.where(number % 4 == 0, named(crowded, number // 4), named(usual, number - number // 4 - 1))
    mixed = jax.random.permutation(jax.random.fold_in(own, 3), count)
    source_of, sink = mixed[0:count // 2 * 2:2], mixed[1:count // 2 * 2:2]
    slack = jnp.minimum(sizes[source_of] - 1, limit - sizes[sink]) // 2
    slack = jnp.where((source_of == order[0]) | (sink == order[0]) | (sizes[sink] == 0), 0, jnp.maximum(slack, 0))
    shifted = jax.random.randint(jax.random.fold_in(own, 4), (count // 2,), 0, 1 << 20) % (slack + 1)
    sizes = sizes.at[source_of].add(-shifted).at[sink].add(shifted)
    labels = jnp.searchsorted(jnp.cumsum(sizes), jnp.arange(rows * top), side="right").astype(jnp.int32)
    listing = labels.reshape(top, rows).T
    listing = listing[jax.random.permutation(jax.random.fold_in(own, 1), rows)]
    offset_by = jax.random.randint(jax.random.fold_in(own, 2), (rows, 1), 0, top)
    return jnp.take_along_axis(listing, (jnp.arange(top)[None, :] + offset_by) % top, axis=1)


def shares(amount, total, limit, lean, full):
    portions = [(1 << 20) // math.isqrt(rank ** lean) + 1 for rank in range(1, amount + 1)]
    largest = limit if full else min(limit, max(-(-total // amount), total * portions[0] // sum(portions)))
    least = 1 if total - largest >= amount - 1 else 0
    holding, rest = [largest] + [least] * (amount - 1), total - largest - least * (amount - 1)
    while rest > 0:
        candidates = [i for i in range(1, amount) if holding[i] < largest] or [i for i in range(1, amount) if holding[i] < limit]
        pool, budget = sum([portions[i] for i in candidates]), rest
        for i in candidates:
            extra = min(limit - holding[i], max(1, budget * portions[i] // pool), rest)
            holding[i] = holding[i] + extra
            rest = rest - extra
    return np.array(holding)


def gaussian(rng, shape, scale, limit, cuts=(), held_as=jnp.bfloat16):
    drawn = scale * jax.random.normal(rng, shape, jnp.float32)
    if cuts:
        drawn = drawn * shard_levels(rng, shape, cuts, -0.22, 0.18)
    return jnp.clip(drawn, -limit, limit).astype(held_as)


def setup_inputs(seed: int = 0) -> dict:
    key_of = jax.random.split(jax.random.key(seed), 7)
    model = jnp.clip(-1.0 + 2.5 * jax.random.uniform(key_of[0], (BLK_ROWS, OWNERS, 128), jnp.float32) ** shard_levels(key_of[0], (BLK_ROWS, OWNERS, 128), ((1, 8),), -0.2, 0.2), -1.0, 1.5)
    source = gaussian(key_of[1], (SOUNDINGS, 3, LZ, LAYER), 1.0, 6.0, ((0, 512),), jnp.float32)
    observed = gaussian(key_of[2], (SOUNDINGS, 3, LZ, LAYER), 1.0, 6.0, ((0, 512),), jnp.float32)
    owner_ids_keys = jax.random.split(jax.random.fold_in(key_of[3], 1), SOUNDINGS * LZ // (S_DEV * LZ))
    owner_ids_turns = jax.random.permutation(jax.random.fold_in(key_of[3], 3), SOUNDINGS * LZ // (S_DEV * LZ))
    owner_ids = jax.vmap(lambda own, number: shared_out(jax.random.fold_in(key_of[3], 2), own, number, S_DEV * LZ, OWNERS, 1, CAP_T, 2))(owner_ids_keys, owner_ids_turns).reshape((SOUNDINGS, LZ, 1))
    offsets = place_ends(jax.random.randint(key_of[4], (SOUNDINGS, LZ), 0, BLK_ROWS - TILE + 1), jax.random.fold_in(key_of[4], 1), 0, BLK_ROWS - TILE).astype(jnp.int32)
    lengths = jax.vmap(lambda own: ragged(own, LZ, LZ * TILE * 3 // 4, TILE, 2))(jax.random.split(key_of[5], SOUNDINGS)).reshape((SOUNDINGS, LZ)).astype(jnp.int32)
    return {"model": model, "source": source, "observed": observed, "owner_ids": owner_ids, "offsets": offsets, "lengths": lengths}


AIR = 0.05
OMEGA = 0.5
BETA = 0.5


def shift_next(field, count):
    filler = jnp.zeros(field.shape[:-1] + (count,), field.dtype)
    return jnp.concatenate([field[..., count:], filler], axis=-1)


def shift_prev(field, count):
    filler = jnp.zeros(field.shape[:-1] + (count,), field.dtype)
    return jnp.concatenate([filler, field[..., :-count]], axis=-1)


def layer_masks(width):
    column = jnp.arange(LAYER, dtype=jnp.int32) % width
    return (column != width - 1).astype(jnp.float32), (column != 0).astype(jnp.float32)


def forward_diff(field, which, masks):
    if which == 0:
        return shift_next(field, LY) - field
    if which == 1:
        return shift_next(field, 1) * masks[0] - field
    deeper = jnp.concatenate([field[:, 1:], jnp.zeros_like(field[:, :1])], axis=1)
    return deeper - field


def adjoint_diff(field, which, masks):
    if which == 0:
        return shift_prev(field, LY) - field
    if which == 1:
        return shift_prev(field, 1) * masks[1] - field
    upper = jnp.concatenate([jnp.zeros_like(field[:, :1]), field[:, :-1]], axis=1)
    return upper - field


def apply_operator(field, conduct, masks):
    east, north, vertical = field[:, 0], field[:, 1], field[:, 2]
    curl_x = forward_diff(vertical, 1, masks) - forward_diff(north, 2, masks)
    curl_y = forward_diff(east, 2, masks) - forward_diff(vertical, 0, masks)
    curl_z = forward_diff(north, 0, masks) - forward_diff(east, 1, masks)
    back_x = adjoint_diff(curl_y, 2, masks) - adjoint_diff(curl_z, 1, masks)
    back_y = adjoint_diff(curl_z, 0, masks) - adjoint_diff(curl_x, 2, masks)
    back_z = adjoint_diff(curl_x, 1, masks) - adjoint_diff(curl_y, 0, masks)
    return jnp.stack([back_x, back_y, back_z], axis=1) + conduct[:, None] * field


def relax(right_side, conduct, count, masks):
    state = jnp.zeros_like(right_side)
    scale = OMEGA / (4.0 + conduct[:, None])
    for sweep in range(count):
        state = state + scale * (right_side - apply_operator(state, conduct, masks))
    return state


def sounding_partial(source, observed, conduct, earth, masks):
    efield = relax(source, conduct, STEPS_FWD, masks)
    adjoint_field = relax(efield - observed, conduct, STEPS_ADJ, masks)
    return -conduct * jnp.sum(efield * adjoint_field, axis=1) * earth


def smoothing(values):
    left = jnp.concatenate([values[..., :1], values[..., :-1]], axis=-1)
    right = jnp.concatenate([values[..., 1:], values[..., -1:]], axis=-1)
    return BETA * (2.0 * values - left - right)


def reference(model, source, observed, owner_ids, offsets, lengths):
    masks = layer_masks(LY)
    flat_model = model.reshape(BLK_ROWS * OWNERS, 128)
    batches = SOUNDINGS // S_DEV
    within = jnp.arange(TILE, dtype=jnp.int32)

    def one_batch(total, pieces):
        batch_source, batch_observed, batch_owner, batch_start, batch_length = pieces
        rows = (batch_start[..., None] + within) * OWNERS + batch_owner[..., None]
        rows = rows.astype(jnp.int32)
        earth = (within < batch_length[..., None]).astype(jnp.float32)
        earth = jnp.broadcast_to(earth[..., None], (S_DEV, LZ, TILE, 128)).reshape(S_DEV, LZ, LAYER)
        values = jnp.exp(flat_model[rows]).reshape(S_DEV, LZ, LAYER)
        conduct = jnp.where(earth > 0.5, values, AIR)
        partial_value = sounding_partial(batch_source, batch_observed, conduct, earth, masks)
        total = total.at[rows.reshape(-1)].add(partial_value.reshape(-1, 128))
        return total, None

    initial = jnp.zeros((BLK_ROWS * OWNERS, 128), jnp.float32)
    pieces = (
        source.reshape(batches, S_DEV, 3, LZ, LAYER),
        observed.reshape(batches, S_DEV, 3, LZ, LAYER),
        owner_ids.reshape(batches, S_DEV, LZ),
        offsets.reshape(batches, S_DEV, LZ),
        lengths.reshape(batches, S_DEV, LZ),
    )
    total, unused = lax.scan(one_batch, initial, pieces)
    return total.reshape(BLK_ROWS, OWNERS, 128) + smoothing(model)
```

```python
import functools

import jax
import jax.numpy as jnp
from jax import lax
from jax.experimental import pallas as pl
from jax.experimental.pallas import tpu as pltpu
from jax.sharding import PartitionSpec as P

LZ = 8
S_DEV = 2
TILES = S_DEV * LZ
TILE = 32
ROWS = 4096
CAP = 4
AIR = 0.05
BETA = 0.5

NZ, NY, NX = 8, 4, 4
OWN = 2 * NX
SLOT_ROWS = CAP * TILE
SHARE = ROWS // (NZ * NY * 2)

MESH = pl.DeviceIdType.MESH
SMEM = pl.BlockSpec(memory_space=pltpu.SMEM)
VMEM = pl.BlockSpec(memory_space=pltpu.VMEM)
FAR_FIRST = [(1, 2), (1, 1), (1, 3), (1, 0), (0, 2), (0, 1), (0, 3)]


def here():
    g, m = lax.axis_index("grp"), lax.axis_index("mdl")
    return g // (2 * NY), (g // 2) % NY, g % 2, m // NX, m % NX


def partner(dh, dx):
    z, y, c, h, x = here()
    y = NY - 1 - y if dh % 2 else y
    m = ((h + dh) % 2) * NX + (x + dx) % NX
    return ((z * NY + y) * 2 + c, m), m


def other_core():
    z, y, c, h, x = here()
    return ((z * NY + y) * 2 + 1 - c, h * NX + x)


def meet(ids):
    barrier = pltpu.get_barrier_semaphore()
    for i in ids:
        pl.semaphore_signal(barrier, inc=1, device_id=i, device_id_type=MESH)
    pl.semaphore_wait(barrier, len(ids))


def remote(src, dst, send, recv, to):
    return pltpu.make_async_remote_copy(
        src_ref=src, dst_ref=dst, send_sem=send, recv_sem=recv, device_id=to, device_id_type=MESH
    )


def tables_kernel(owner, offset, place, request, counts):
    for o in range(OWN):
        counts[o] = 0
        for k in range(CAP):
            request[o, k] = 0
    for t in range(TILES):
        o = owner[t // LZ, t % LZ, 0]
        k = counts[o]
        counts[o] = k + 1
        place[t] = o * CAP + k
        request[o, k] = offset[t // LZ, t % LZ]


def fetch_kernel(request, block, values, starts, outbox, ask_send, ask_recv, row_send, row_recv, core_sem):
    me = lax.axis_index("mdl")
    meet([partner(*d)[0] for d in FAR_FIRST] + [other_core()])
    asks, answers = {}, {}
    for dh, dx in FAR_FIRST:
        to, m = partner(dh, dx)
        k = dh * NX + dx
        asks[dh, dx] = remote(request.at[m], starts.at[0, me], ask_send.at[k], ask_recv.at[k], to)
        asks[dh, dx].start()
    for k in range(CAP):
        starts[0, me, k] = request[me, k]
        values[me, pl.ds(k * TILE, TILE), :] = block[pl.ds(request[me, k], TILE), :]
    for dh, dx in FAR_FIRST:
        back = (-dh % 2, -dx % NX)
        asks[back].wait_recv()
        to, m = partner(dh, dx)
        k = dh * NX + dx
        for i in range(CAP):
            outbox[k, pl.ds(i * TILE, TILE), :] = block[pl.ds(starts[0, m, i], TILE), :]
        answers[dh, dx] = remote(outbox.at[k], values.at[me], row_send.at[k], row_recv.at[k], to)
        answers[dh, dx].start()
    pass_on = remote(starts.at[0], starts.at[1], core_sem.at[0], core_sem.at[1], other_core())
    pass_on.start()
    for d in FAR_FIRST:
        asks[d].wait_send()
        answers[d].wait()
    pass_on.wait()


def solve_kernel(place, lengths, values, source, observed, out, cond, weight, state, rhs, field, part):
    lane = lax.broadcasted_iota(jnp.int32, (8, 128), 1)
    layer = lax.broadcasted_iota(jnp.int32, (8, 128), 0)
    low = lane < 64
    y_next, y_prev = lane % 64 != 63, lane % 64 != 0
    z_next, z_prev = layer != LZ - 1, layer != 0
    row = lax.broadcasted_iota(jnp.int32, (TILE, 128), 0)
    zero = jnp.zeros((8, 128), jnp.float32)

    def half(v):
        return pltpu.roll(v, 64, 1)

    def y_up(v):
        return jnp.where(y_next, pltpu.roll(v, 127, 1), 0.0)

    def y_down(v):
        return jnp.where(y_prev, pltpu.roll(v, 1, 1), 0.0)

    def z_up(v):
        return jnp.where(z_next, pltpu.roll(v, 7, 0), 0.0)

    def z_down(v):
        return jnp.where(z_prev, pltpu.roll(v, 1, 0), 0.0)

    for t in range(TILES):
        s, z = t // LZ, t % LZ
        got = values[pl.ds(pl.multiple_of(place[t] * TILE, TILE), TILE), :]
        cond[s, pl.ds(z, TILE, stride=8), :] = jnp.where(row < lengths[s, z], jnp.exp(got), AIR)

    def split(a, b):
        return jnp.where(low, a, half(b)), jnp.where(low, half(a), b)

    def tile(k):
        return pl.ds(pl.multiple_of(k * 128, 128), 128)

    def weigh(k, carry):
        for s in range(S_DEV):
            here_, there = (cond[s, pl.ds(pl.multiple_of((k + d) * 8, 8), 8), :] for d in (0, 16))
            for i, c in enumerate(split(here_, there)):
                w = 0.5 / (4.0 + c)
                weight[s, 2 * k + i] = w
            for a in range(3):
                pair = split(source[s, a, :, tile(k)], source[s, a, :, tile(k + 16)])
                for i, v in enumerate(pair):
                    b = weight[s, 2 * k + i] * v
                    rhs[s, a, 2 * k + i] = b
                    state[s, a, 2 * k + i] = b
        return carry

    lax.fori_loop(0, 16, weigh, 0, unroll=2)

    def curl(e, e_x):
        ex, ey, ez = e
        hx = (y_up(ez) - ez) - (z_up(ey) - ey)
        hy = (z_up(ex) - ex) - (e_x[2] - ez)
        hz = (e_x[1] - ey) - (y_up(ex) - ex)
        return hx, hy, hz

    def sweep(state, step_rhs):
        def at(s, r):
            return [state[s, a, r] for a in range(3)]

        first, before = [], []
        for s in range(S_DEV):
            ends = [jnp.where(low, half(v), 0.0) for v in at(s, 0)]
            for a in range(3):
                state[s, a, TILE] = ends[a]
            _, hy, hz = curl(at(s, TILE - 1), ends)
            first.append(tuple(at(s, 0)))
            before.append(tuple(jnp.where(low, 0.0, half(v)) for v in (hy, hz)))

        def body(r, carry):
            now, last = carry
            nexts, lasts = [], []
            for s in range(S_DEV):
                e = now[s]
                e_x = tuple(at(s, r + 1))
                hx, hy, hz = curl(e, e_x)
                hy_x, hz_x = last[s]
                back = (
                    (z_down(hy) - hy) - (y_down(hz) - hz),
                    (hz_x - hz) - (z_down(hx) - hx),
                    (y_down(hx) - hx) - (hy_x - hy),
                )
                w = weight[s, r]
                keep = 0.5 + 4.0 * w
                for a in range(3):
                    state[s, a, r] = keep * e[a] + (step_rhs[s, a, r] - w * back[a])
                nexts.append(e_x)
                lasts.append((hy, hz))
            return tuple(nexts), tuple(lasts)

        lax.fori_loop(0, TILE, body, (tuple(first), tuple(before)), unroll=2)

    def sweeps(state):
        def one(i, carry):
            sweep(state, rhs)
            return carry

        lax.fori_loop(0, 3, one, 0)

    sweeps(state)

    def misfit(k, carry):
        for s in range(S_DEV):
            for a in range(3):
                pair = split(observed[s, a, :, tile(k)], observed[s, a, :, tile(k + 16)])
                for i, v in enumerate(pair):
                    b = weight[s, 2 * k + i] * (state[s, a, 2 * k + i] - v)
                    rhs[s, a, 2 * k + i] = b
                    field[s, a, 2 * k + i] = b
        return carry

    lax.fori_loop(0, 16, misfit, 0, unroll=2)
    sweeps(field)

    def products(k, carry):
        for s in range(S_DEV):
            p, q = (
                sum(state[s, a, 2 * k + i] * field[s, a, 2 * k + i] for a in range(3)) for i in range(2)
            )
            for d, v in ((0, jnp.where(low, p, half(q))), (16, jnp.where(low, half(p), q))):
                at = pl.ds(pl.multiple_of((k + d) * 8, 8), 8)
                part[s, at, :] = -cond[s, at, :] * v
        return carry

    lax.fori_loop(0, 16, products, 0, unroll=2)

    out[...] = jnp.zeros_like(out)
    for t in range(TILES):
        s, z = t // LZ, t % LZ
        got = part[s, pl.ds(z, TILE, stride=8), :]
        out[pl.ds(pl.multiple_of(place[t] * TILE, TILE), TILE), :] = jnp.where(row < lengths[s, z], got, 0.0)


def send_kernel(slots, arrived, send, recv, core_send, core_recv, own_sem):
    me = lax.axis_index("mdl")
    meet([partner(*d)[0] for d in FAR_FIRST] + [other_core()])
    copies, forwards = {}, []
    for dh, dx in FAR_FIRST:
        to, m = partner(dh, dx)
        k = dh * NX + dx
        copies[dh, dx] = remote(slots.at[m], arrived.at[0, me], send.at[k], recv.at[k], to)
        copies[dh, dx].start()
    own = pltpu.make_async_copy(slots.at[me], arrived.at[0, me], own_sem)
    own.start()
    forwards.append(remote(slots.at[me], arrived.at[1, me], core_send.at[0], core_recv.at[0], other_core()))
    forwards[0].start()
    for dh, dx in FAR_FIRST[::-1]:
        _, m = partner(dh, dx)
        back = (-dh % 2, -dx % NX)
        copies[back].wait_recv()
        k = dh * NX + dx
        forwards.append(
            remote(arrived.at[0, m], arrived.at[1, m], core_send.at[k], core_recv.at[k], other_core())
        )
        forwards[-1].start()
    own.wait()
    for d in FAR_FIRST:
        copies[d].wait_send()
    for f in forwards:
        f.wait()


def add_kernel(starts, arrived, total):
    total[...] = jnp.zeros_like(total)
    for side in range(2):
        for m in range(OWN):
            for k in range(CAP):
                at = pl.ds(starts[side, m, k], TILE)
                total[at, :] += arrived[side, m, pl.ds(k * TILE, TILE), :]


PIECE = SHARE // 2


def reduce_kernel(total, model, out, up, down, final, spread, up_sem, down_sem, y_send, y_recv):
    z, y, c, h, x = here()
    m = lax.axis_index("mdl")
    above = ((((z + 1) % NZ) * NY + y) * 2 + c, m)
    below = ((((z + NZ - 1) % NZ) * NY + y) * 2 + c, m)
    others = [((z * NY + (y + d) % NY) * 2 + c, m) for d in range(1, NY)]
    meet([above, below] + others)

    def own(d, way):
        return total.at[d, :, c, pl.ds(way * PIECE, PIECE), :]

    rings = (
        (up, up_sem, above, lambda s: (z + 2 * NZ - 1 - s) % NZ),
        (down, down_sem, below, lambda s: (z + 1 + s) % NZ),
    )
    flights = []
    for s in range(NZ):
        for way, (box, sem, to, chunk) in enumerate(rings):
            if s:
                flights[2 * (s - 1) + way].wait_recv()
            if s < NZ - 1:
                if s:
                    box[s - 1] += total[chunk(s), :, c, pl.ds(way * PIECE, PIECE), :]
                    src = box.at[s - 1]
                else:
                    src = own(chunk(0), way)
                flights.append(remote(src, box.at[s], sem.at[0, s], sem.at[1, s], to))
                flights[-1].start()
            else:
                final[:, pl.ds(way * PIECE, PIECE), :] = (
                    box[s - 1] + total[z, :, c, pl.ds(way * PIECE, PIECE), :]
                )
    sends = []
    for d in range(1, NY):
        sends.append(
            remote(final.at[(y + d) % NY], spread.at[d - 1], y_send.at[d - 1], y_recv.at[d - 1], others[d - 1])
        )
        sends[-1].start()
    mine = model[...]
    lane = lax.broadcasted_iota(jnp.int32, (SHARE, 128), 1)
    left = jnp.where(lane == 0, mine, pltpu.roll(mine, 1, 1))
    right = jnp.where(lane == 127, mine, pltpu.roll(mine, 127, 1))
    acc = final[y] + BETA * (2.0 * mine - left - right)
    for d in range(1, NY):
        sends[d - 1].wait()
        acc = acc + spread[d - 1]
    out[...] = acc
    for f in flights:
        f.wait_send()


def per_device(model, source, observed, owner_ids, offsets, lengths):
    block = model.reshape(ROWS, 128)
    f32, i32 = jnp.float32, jnp.int32
    dma = pltpu.SemaphoreType.DMA
    place, request = pl.pallas_call(
        tables_kernel,
        out_shape=(jax.ShapeDtypeStruct((TILES,), i32), jax.ShapeDtypeStruct((OWN, 128), i32)),
        in_specs=[SMEM, SMEM],
        out_specs=(SMEM, SMEM),
        scratch_shapes=[pltpu.SMEM((OWN,), i32)],
        name="tables",
    )(owner_ids, offsets)
    values, starts = pl.pallas_call(
        fetch_kernel,
        out_shape=(
            jax.ShapeDtypeStruct((OWN, SLOT_ROWS, 128), f32),
            jax.ShapeDtypeStruct((2, OWN, 128), i32),
        ),
        in_specs=[SMEM, VMEM],
        out_specs=(VMEM, SMEM),
        scratch_shapes=[pltpu.VMEM((OWN, SLOT_ROWS, 128), f32)] + [dma((OWN,))] * 4 + [dma((2,))],
        compiler_params=pltpu.CompilerParams(collective_id=0, has_side_effects=True),
        name="fetch",
    )(request, block)
    slots = pl.pallas_call(
        solve_kernel,
        out_shape=jax.ShapeDtypeStruct((OWN * SLOT_ROWS, 128), f32),
        in_specs=[SMEM, SMEM, VMEM, VMEM, VMEM],
        out_specs=VMEM,
        scratch_shapes=[
            pltpu.VMEM((S_DEV, TILE * 8, 128), f32),
            pltpu.VMEM((S_DEV, TILE, 8, 128), f32),
            pltpu.VMEM((S_DEV, 3, TILE + 1, 8, 128), f32),
            pltpu.VMEM((S_DEV, 3, TILE, 8, 128), f32),
            pltpu.VMEM((S_DEV, 3, TILE + 1, 8, 128), f32),
            pltpu.VMEM((S_DEV, TILE * 8, 128), f32),
        ],
        compiler_params=pltpu.CompilerParams(vmem_limit_bytes=32 << 20),
        name="solve",
    )(place, lengths, values.reshape(OWN * SLOT_ROWS, 128), source, observed)
    arrived = pl.pallas_call(
        send_kernel,
        out_shape=jax.ShapeDtypeStruct((2, OWN, SLOT_ROWS, 128), f32),
        in_specs=[VMEM],
        out_specs=VMEM,
        scratch_shapes=[dma((OWN,))] * 4 + [dma],
        compiler_params=pltpu.CompilerParams(collective_id=1, has_side_effects=True),
        name="send",
    )(slots.reshape(OWN, SLOT_ROWS, 128))
    total = pl.pallas_call(
        add_kernel,
        out_shape=jax.ShapeDtypeStruct((ROWS, 128), f32),
        in_specs=[SMEM, VMEM],
        out_specs=VMEM,
        compiler_params=pltpu.CompilerParams(vmem_limit_bytes=32 << 20),
        name="add",
    )(starts, arrived)
    mine = lax.dynamic_slice_in_dim(block, lax.axis_index("grp") * SHARE, SHARE, 0)
    gradient = pl.pallas_call(
        reduce_kernel,
        out_shape=jax.ShapeDtypeStruct((SHARE, 128), f32),
        in_specs=[VMEM, VMEM],
        out_specs=VMEM,
        scratch_shapes=[
            pltpu.VMEM((NZ - 1, NY, PIECE, 128), f32),
            pltpu.VMEM((NZ - 1, NY, PIECE, 128), f32),
            pltpu.VMEM((NY, SHARE, 128), f32),
            pltpu.VMEM((NY - 1, SHARE, 128), f32),
            dma((2, NZ - 1)),
            dma((2, NZ - 1)),
            dma((NY - 1,)),
            dma((NY - 1,)),
        ],
        compiler_params=pltpu.CompilerParams(
            collective_id=2, has_side_effects=True, vmem_limit_bytes=32 << 20
        ),
        name="reduce",
    )(total.reshape(NZ, NY, 2, SHARE, 128), mine)
    return gradient[:, None, :]


def solution(mesh):
    placed = (
        P(None, "mdl", None),
        P(("grp", "mdl"), None, None, None),
        P(("grp", "mdl"), None, None, None),
        P(("grp", "mdl"), None, None),
        P(("grp", "mdl"), None),
        P(("grp", "mdl"), None),
    )
    return jax.shard_map(
        per_device, mesh=mesh, in_specs=placed, out_specs=P("grp", "mdl", None), check_vma=False
    )
```

```python
import functools

import jax
import jax.numpy as jnp
from jax import lax
from jax.experimental import pallas as pl
from jax.experimental.pallas import tpu as pltpu
from jax.sharding import PartitionSpec as P

LZ = 8
S_DEV = 2
TILES = S_DEV * LZ
TILE = 32
ROWS = 4096
CAP = 4
AIR = 0.05
BETA = 0.5

NZ, NY, NX = 8, 4, 4
OWN = 2 * NX
SLOT_ROWS = CAP * TILE
SHARE = ROWS // (NZ * NY * 2)

MESH = pl.DeviceIdType.MESH
SMEM = pl.BlockSpec(memory_space=pltpu.SMEM)
VMEM = pl.BlockSpec(memory_space=pltpu.VMEM)
FAR_FIRST = [(1, 2), (1, 1), (1, 3), (1, 0), (0, 2), (0, 1), (0, 3)]


def here():
    g, m = lax.axis_index("grp"), lax.axis_index("mdl")
    return g // (2 * NY), (g // 2) % NY, g % 2, m // NX, m % NX


def partner(dh, dx):
    z, y, c, h, x = here()
    y = NY - 1 - y if dh % 2 else y
    m = ((h + dh) % 2) * NX + (x + dx) % NX
    return ((z * NY + y) * 2 + c, m), m


def other_core():
    z, y, c, h, x = here()
    return ((z * NY + y) * 2 + 1 - c, h * NX + x)


def meet(ids):
    barrier = pltpu.get_barrier_semaphore()
    for i in ids:
        pl.semaphore_signal(barrier, inc=1, device_id=i, device_id_type=MESH)
    pl.semaphore_wait(barrier, len(ids))


def remote(src, dst, send, recv, to):
    return pltpu.make_async_remote_copy(
        src_ref=src, dst_ref=dst, send_sem=send, recv_sem=recv, device_id=to, device_id_type=MESH
    )


def tables_kernel(owner, offset, place, request, counts):
    for o in range(OWN):
        counts[o] = 0
        for k in range(CAP):
            request[o, k] = 0
    for t in range(TILES):
        o = owner[t // LZ, 0, t % LZ]
        k = counts[o]
        counts[o] = k + 1
        place[t] = o * CAP + k
        request[o, k] = offset[t // LZ, t % LZ]


def fetch_kernel(request, block, values, starts, outbox, ask_send, ask_recv, row_send, row_recv, core_sem):
    me = lax.axis_index("mdl")
    meet([partner(*d)[0] for d in FAR_FIRST] + [other_core()])
    asks, answers = {}, {}
    for dh, dx in FAR_FIRST:
        to, m = partner(dh, dx)
        k = dh * NX + dx
        asks[dh, dx] = remote(request.at[m], starts.at[0, me], ask_send.at[k], ask_recv.at[k], to)
        asks[dh, dx].start()
    for k in range(CAP):
        starts[0, me, k] = request[me, k]
    for dh, dx in FAR_FIRST:
        back = (-dh % 2, -dx % NX)
        asks[back].wait_recv()
        to, m = partner(dh, dx)
        k = dh * NX + dx
        for i in range(CAP):
            outbox[k, pl.ds(i * TILE, TILE), :] = block[pl.ds(starts[0, m, i], TILE), :]
        answers[dh, dx] = remote(outbox.at[k], values.at[me], row_send.at[k], row_recv.at[k], to)
        answers[dh, dx].start()
    pass_on = remote(starts.at[0], starts.at[1], core_sem.at[0], core_sem.at[1], other_core())
    pass_on.start()
    for k in range(CAP):
        values[me, pl.ds(k * TILE, TILE), :] = block[pl.ds(starts[0, me, k], TILE), :]
    for d in FAR_FIRST:
        asks[d].wait_send()
        answers[d].wait()
    pass_on.wait()


BATCH = 4


def solve_kernel(place, lengths, values, source, observed, out, cond, weight, first, second, third, rhs, part):
    lane = lax.broadcasted_iota(jnp.int32, (8, 128), 1)
    layer = lax.broadcasted_iota(jnp.int32, (8, 128), 0)
    low = lane < 64
    y_next, y_prev = lane % 64 != 63, lane % 64 != 0
    z_next, z_prev = layer != LZ - 1, layer != 0
    row = lax.broadcasted_iota(jnp.int32, (TILE, 128), 0)

    def half(v):
        return pltpu.roll(v, 64, 1)

    def shift(mask, by, axis):
        def one(v):
            return jnp.where(mask, pltpu.roll(v, by, axis), 0.0)

        return lambda v: one(v) if v.ndim == 2 else jnp.stack([one(v[i]) for i in range(v.shape[0])])

    y_up, y_down = shift(y_next, 127, 1), shift(y_prev, 1, 1)
    z_up, z_down = shift(z_next, LZ - 1, 0), shift(z_prev, 1, 0)

    for t in range(TILES):
        s, z = t // LZ, t % LZ
        got = values[pl.ds(pl.multiple_of(place[t] * TILE, TILE), TILE), :]
        cond[s, pl.ds(z, TILE, stride=8), :] = jnp.where(row < lengths[s, z], jnp.exp(got), AIR)

    def split(a, b):
        return jnp.where(low, a, half(b)), jnp.where(low, half(a), b)

    def tile(k):
        return pl.ds(k * 128, 128)

    for k in range(TILE // 2):
        for s in range(S_DEV):
            pair = split(*[cond[s, pl.ds((k + d) * 8, 8), :] for d in (0, TILE // 2)])
            ws = [0.5 / (4.0 + c) for c in pair]
            for i in range(2):
                weight[s, 2 * k + i] = ws[i]
            for a in range(3):
                pair = split(source[s, a, :, tile(k)], source[s, a, :, tile(k + TILE // 2)])
                for i in range(2):
                    b = ws[i] * pair[i]
                    rhs[s, a, 2 * k + i] = b
                    first[s, a, 2 * k + i] = b

    def curl(e, e_x):
        ex, ey, ez = e
        hx = (y_up(ez) - ez) - (z_up(ey) - ey)
        hy = (z_up(ex) - ex) - (e_x[2] - ez)
        hz = (e_x[1] - ey) - (y_up(ex) - ex)
        return hx, hy, hz

    def sweep(src, dst):
        before = []
        for s in range(S_DEV):
            ends = [jnp.where(low, half(src[s, a, 0]), 0.0) for a in range(3)]
            for a in range(1, 3):
                src[s, a, TILE] = ends[a]
            _, hy, hz = curl([src[s, a, TILE - 1] for a in range(3)], ends)
            before.append(tuple(jnp.where(low, 0.0, half(v))[None] for v in (hy, hz)))

        def body(b, carry):
            at = pl.ds(b * BATCH, BATCH)
            lasts = []
            for s in range(S_DEV):
                e = [src[s, a, at] for a in range(3)]
                after = pl.ds(b * BATCH + BATCH, 1)
                e_x = [None] + [jnp.concatenate([e[a][1:], src[s, a, after]], 0) for a in (1, 2)]
                hx, hy, hz = curl(e, e_x)
                hy_x = jnp.concatenate([carry[s][0], hy[:-1]], 0)
                hz_x = jnp.concatenate([carry[s][1], hz[:-1]], 0)
                back = (
                    (z_down(hy) - hy) - (y_down(hz) - hz),
                    (hz_x - hz) - (z_down(hx) - hx),
                    (y_down(hx) - hx) - (hy_x - hy),
                )
                w = weight[s, at]
                keep = 0.5 + 4.0 * w
                for a in range(3):
                    dst[s, a, at] = keep * e[a] + (rhs[s, a, at] - w * back[a])
                lasts.append((hy[-1:], hz[-1:]))
            return tuple(lasts)

        lax.fori_loop(0, TILE // BATCH, body, tuple(before), unroll=4)

    sweep(first, second)
    sweep(second, first)
    sweep(first, second)

    for k in range(TILE // 2):
        for s in range(S_DEV):
            for a in range(3):
                pair = split(observed[s, a, :, tile(k)], observed[s, a, :, tile(k + TILE // 2)])
                for i in range(2):
                    b = weight[s, 2 * k + i] * (second[s, a, 2 * k + i] - pair[i])
                    rhs[s, a, 2 * k + i] = b
                    first[s, a, 2 * k + i] = b

    sweep(first, third)
    sweep(third, first)
    sweep(first, third)

    for k in range(TILE // 2):
        for s in range(S_DEV):
            p, q = (
                sum(second[s, a, 2 * k + i] * third[s, a, 2 * k + i] for a in range(3)) for i in range(2)
            )
            for d, v in ((0, jnp.where(low, p, half(q))), (TILE // 2, jnp.where(low, half(p), q))):
                at = pl.ds((k + d) * 8, 8)
                part[s, at, :] = -cond[s, at, :] * v

    out[...] = jnp.zeros_like(out)
    for t in range(TILES):
        s, z = t // LZ, t % LZ
        got = part[s, pl.ds(z, TILE, stride=8), :]
        out[pl.ds(pl.multiple_of(place[t] * TILE, TILE), TILE), :] = jnp.where(row < lengths[s, z], got, 0.0)


def send_kernel(slots, arrived, send, recv, core_send, core_recv, own_sem):
    me = lax.axis_index("mdl")
    meet([partner(*d)[0] for d in FAR_FIRST] + [other_core()])
    copies, forwards = {}, []
    for dh, dx in FAR_FIRST:
        to, m = partner(dh, dx)
        k = dh * NX + dx
        copies[dh, dx] = remote(slots.at[m], arrived.at[0, me], send.at[k], recv.at[k], to)
        copies[dh, dx].start()
    own = pltpu.make_async_copy(slots.at[me], arrived.at[0, me], own_sem)
    own.start()
    forwards.append(remote(slots.at[me], arrived.at[1, me], core_send.at[0], core_recv.at[0], other_core()))
    forwards[0].start()
    for dh, dx in FAR_FIRST[::-1]:
        _, m = partner(dh, dx)
        back = (-dh % 2, -dx % NX)
        copies[back].wait_recv()
        k = dh * NX + dx
        forwards.append(
            remote(arrived.at[0, m], arrived.at[1, m], core_send.at[k], core_recv.at[k], other_core())
        )
        forwards[-1].start()
    own.wait()
    for d in FAR_FIRST:
        copies[d].wait_send()
    for f in forwards:
        f.wait()


def add_kernel(starts, arrived, block, total):
    total[...] = jnp.zeros_like(total)
    at = pl.ds(pl.multiple_of(lax.axis_index("grp") * SHARE, SHARE), SHARE)
    mine = block[at, :]
    lane = lax.broadcasted_iota(jnp.int32, (SHARE, 128), 1)
    left = jnp.where(lane == 0, mine, pltpu.roll(mine, 1, 1))
    right = jnp.where(lane == 127, mine, pltpu.roll(mine, 127, 1))
    total[at, :] = BETA * (2.0 * mine - left - right)
    for side in range(2):
        for m in range(OWN):
            for k in range(CAP):
                at = pl.ds(starts[side, m, k], TILE)
                total[at, :] += arrived[side, m, pl.ds(k * TILE, TILE), :]


PIECE = SHARE // 2


def reduce_kernel(total, out, up, down, final, spread, up_sem, down_sem, y_send, y_recv):
    z, y, c, h, x = here()
    m = lax.axis_index("mdl")
    above = ((((z + 1) % NZ) * NY + y) * 2 + c, m)
    below = ((((z + NZ - 1) % NZ) * NY + y) * 2 + c, m)
    others = [((z * NY + (y + d) % NY) * 2 + c, m) for d in range(1, NY)]
    meet([above, below] + others)

    rings = (
        (up, up_sem, above, lambda s: (z + 2 * NZ - 1 - s) % NZ),
        (down, down_sem, below, lambda s: (z + 1 + s) % NZ),
    )
    order = list(range(1, NY)) + [0]
    flights, sends = {}, {}
    for s in range(NZ):
        for d in order:
            for way, (box, sem, to, chunk) in enumerate(rings):
                rows = pl.ds(way * PIECE, PIECE)
                j = (y + d) % NY
                if s:
                    flights[s - 1, d, way].wait_recv()
                if s == NZ - 1:
                    final[d, rows, :] = box[s - 1, d] + total[z, j, c, rows, :]
                    continue
                src = total.at[chunk(0), j, c, rows, :]
                if s:
                    box[s - 1, d] += total[chunk(s), j, c, rows, :]
                    src = box.at[s - 1, d]
                flights[s, d, way] = remote(src, box.at[s, d], sem.at[0, s, d], sem.at[1, s, d], to)
                flights[s, d, way].start()
            if s == NZ - 1 and d:
                sends[d] = remote(final.at[d], spread.at[d - 1], y_send.at[d - 1], y_recv.at[d - 1], others[d - 1])
                sends[d].start()
    acc = final[0]
    for d in range(1, NY):
        sends[d].wait()
        acc = acc + spread[d - 1]
    out[...] = acc
    for f in flights.values():
        f.wait_send()


def per_device(model, source, observed, owner_ids, offsets, lengths):
    block = model.reshape(ROWS, 128)
    f32, i32 = jnp.float32, jnp.int32
    dma = pltpu.SemaphoreType.DMA
    place, request = pl.pallas_call(
        tables_kernel,
        out_shape=(jax.ShapeDtypeStruct((TILES,), i32), jax.ShapeDtypeStruct((OWN, 128), i32)),
        in_specs=[SMEM, SMEM],
        out_specs=(SMEM, SMEM),
        scratch_shapes=[pltpu.SMEM((OWN,), i32)],
        name="tables",
    )(owner_ids.transpose(0, 2, 1), offsets)
    values, starts = pl.pallas_call(
        fetch_kernel,
        out_shape=(
            jax.ShapeDtypeStruct((OWN, SLOT_ROWS, 128), f32),
            jax.ShapeDtypeStruct((2, OWN, 128), i32),
        ),
        in_specs=[SMEM, VMEM],
        out_specs=(VMEM, SMEM),
        scratch_shapes=[pltpu.VMEM((OWN, SLOT_ROWS, 128), f32)] + [dma((OWN,))] * 4 + [dma((2,))],
        compiler_params=pltpu.CompilerParams(collective_id=0, has_side_effects=True),
        name="fetch",
    )(request, block)
    fields = pltpu.VMEM((S_DEV, 3, TILE + 1, 8, 128), f32)
    slots = pl.pallas_call(
        solve_kernel,
        out_shape=jax.ShapeDtypeStruct((OWN * SLOT_ROWS, 128), f32),
        in_specs=[SMEM, SMEM, VMEM, VMEM, VMEM],
        out_specs=VMEM,
        scratch_shapes=[
            pltpu.VMEM((S_DEV, TILE * 8, 128), f32),
            pltpu.VMEM((S_DEV, TILE, 8, 128), f32),
            fields,
            fields,
            fields,
            pltpu.VMEM((S_DEV, 3, TILE, 8, 128), f32),
            pltpu.VMEM((S_DEV, TILE * 8, 128), f32),
        ],
        compiler_params=pltpu.CompilerParams(vmem_limit_bytes=32 << 20),
        name="solve",
    )(place, lengths, values.reshape(OWN * SLOT_ROWS, 128), source, observed)
    arrived = pl.pallas_call(
        send_kernel,
        out_shape=jax.ShapeDtypeStruct((2, OWN, SLOT_ROWS, 128), f32),
        in_specs=[VMEM],
        out_specs=VMEM,
        scratch_shapes=[dma((OWN,))] * 4 + [dma],
        compiler_params=pltpu.CompilerParams(collective_id=1, has_side_effects=True),
        name="send",
    )(slots.reshape(OWN, SLOT_ROWS, 128))
    total = pl.pallas_call(
        add_kernel,
        out_shape=jax.ShapeDtypeStruct((ROWS, 128), f32),
        in_specs=[SMEM, VMEM, VMEM],
        out_specs=VMEM,
        compiler_params=pltpu.CompilerParams(vmem_limit_bytes=32 << 20),
        name="add",
    )(starts, arrived, block)
    box = pltpu.VMEM((NZ - 1, NY, PIECE, 128), f32)
    gradient = pl.pallas_call(
        reduce_kernel,
        out_shape=jax.ShapeDtypeStruct((SHARE, 128), f32),
        in_specs=[VMEM],
        out_specs=VMEM,
        scratch_shapes=[
            box,
            box,
            pltpu.VMEM((NY, SHARE, 128), f32),
            pltpu.VMEM((NY - 1, SHARE, 128), f32),
            dma((2, NZ - 1, NY)),
            dma((2, NZ - 1, NY)),
            dma((NY - 1,)),
            dma((NY - 1,)),
        ],
        compiler_params=pltpu.CompilerParams(
            collective_id=2, has_side_effects=True, vmem_limit_bytes=32 << 20
        ),
        name="reduce",
    )(total.reshape(NZ, NY, 2, SHARE, 128))
    return gradient[:, None, :]


def solution(mesh):
    placed = (
        P(None, "mdl", None),
        P(("grp", "mdl"), None, None, None),
        P(("grp", "mdl"), None, None, None),
        P(("grp", "mdl"), None, None),
        P(("grp", "mdl"), None),
        P(("grp", "mdl"), None),
    )
    return jax.shard_map(
        per_device, mesh=mesh, in_specs=placed, out_specs=P("grp", "mdl", None), check_vma=False
    )
```

```python
import functools

import jax
import jax.numpy as jnp
from jax import lax
from jax.experimental import pallas as pl
from jax.experimental.pallas import tpu as pltpu
from jax.sharding import PartitionSpec as P

LZ = 8
S_DEV = 2
TILES = S_DEV * LZ
TILE = 32
ROWS = 4096
CAP = 4
AIR = 0.05
BETA = 0.5

NZ, NY, NX = 8, 4, 4
OWN = 2 * NX
SLOT_ROWS = CAP * TILE
SHARE = ROWS // (NZ * NY * 2)

MESH = pl.DeviceIdType.MESH
SMEM = pl.BlockSpec(memory_space=pltpu.SMEM)
VMEM = pl.BlockSpec(memory_space=pltpu.VMEM)
FAR_FIRST = [(1, 2), (1, 1), (1, 3), (1, 0), (0, 2), (0, 1), (0, 3)]


def here():
    g, m = lax.axis_index("grp"), lax.axis_index("mdl")
    return g // (2 * NY), (g // 2) % NY, g % 2, m // NX, m % NX


def partner(dh, dx):
    z, y, c, h, x = here()
    y = NY - 1 - y if dh % 2 else y
    m = ((h + dh) % 2) * NX + (x + dx) % NX
    return ((z * NY + y) * 2 + c, m), m


def other_core():
    z, y, c, h, x = here()
    return ((z * NY + y) * 2 + 1 - c, h * NX + x)


def meet(ids):
    barrier = pltpu.get_barrier_semaphore()
    for i in ids:
        pl.semaphore_signal(barrier, inc=1, device_id=i, device_id_type=MESH)
    pl.semaphore_wait(barrier, len(ids))


def remote(src, dst, send, recv, to):
    return pltpu.make_async_remote_copy(
        src_ref=src, dst_ref=dst, send_sem=send, recv_sem=recv, device_id=to, device_id_type=MESH
    )


def tables_kernel(owner, offset, place, request, counts):
    for o in range(OWN):
        counts[o] = 0
        for k in range(CAP):
            request[o, k] = 0
    for t in range(TILES):
        o = owner[t // LZ, 0, t % LZ]
        k = counts[o]
        counts[o] = k + 1
        place[t] = o * CAP + k
        request[o, k] = offset[t // LZ, t % LZ]


def fetch_kernel(request, block, values, starts, outbox, ask_send, ask_recv, row_send, row_recv, core_sem):
    me = lax.axis_index("mdl")
    meet([partner(*d)[0] for d in FAR_FIRST] + [other_core()])
    asks, answers = {}, {}
    for dh, dx in FAR_FIRST:
        to, m = partner(dh, dx)
        k = dh * NX + dx
        asks[dh, dx] = remote(request.at[m], starts.at[0, me], ask_send.at[k], ask_recv.at[k], to)
        asks[dh, dx].start()
    for k in range(CAP):
        starts[0, me, k] = request[me, k]
    for dh, dx in FAR_FIRST:
        back = (-dh % 2, -dx % NX)
        asks[back].wait_recv()
        to, m = partner(dh, dx)
        k = dh * NX + dx
        for i in range(CAP):
            outbox[k, pl.ds(i * TILE, TILE), :] = block[pl.ds(starts[0, m, i], TILE), :]
        answers[dh, dx] = remote(outbox.at[k], values.at[me], row_send.at[k], row_recv.at[k], to)
        answers[dh, dx].start()
    pass_on = remote(starts.at[0], starts.at[1], core_sem.at[0], core_sem.at[1], other_core())
    pass_on.start()
    for k in range(CAP):
        values[me, pl.ds(k * TILE, TILE), :] = block[pl.ds(starts[0, me, k], TILE), :]
    for d in FAR_FIRST:
        asks[d].wait_send()
        answers[d].wait()
    pass_on.wait()


BATCH = 4


def solve_kernel(place, lengths, values, source, observed, out, cond, weight, first, second, third, rhs, part):
    lane = lax.broadcasted_iota(jnp.int32, (8, 128), 1)
    layer = lax.broadcasted_iota(jnp.int32, (8, 128), 0)
    low = lane < 64
    y_next, y_prev = lane % 64 != 63, lane % 64 != 0
    z_next, z_prev = layer != LZ - 1, layer != 0
    row = lax.broadcasted_iota(jnp.int32, (TILE, 128), 0)

    def half(v):
        return pltpu.roll(v, 64, 1)

    def shift(mask, by, axis):
        def one(v):
            return jnp.where(mask, pltpu.roll(v, by, axis), 0.0)

        return lambda v: one(v) if v.ndim == 2 else jnp.stack([one(v[i]) for i in range(v.shape[0])])

    y_up, y_down = shift(y_next, 127, 1), shift(y_prev, 1, 1)
    z_up, z_down = shift(z_next, LZ - 1, 0), shift(z_prev, 1, 0)

    for t in range(TILES):
        s, z = t // LZ, t % LZ
        got = values[pl.ds(pl.multiple_of(place[t] * TILE, TILE), TILE), :]
        cond[s, pl.ds(z, TILE, stride=8), :] = jnp.where(row < lengths[s, z], jnp.exp(got), AIR)

    def split(a, b):
        return jnp.where(low, a, half(b)), jnp.where(low, half(a), b)

    def tile(k):
        return pl.ds(k * 128, 128)

    for k in range(TILE // 2):
        for s in range(S_DEV):
            pair = split(*[cond[s, pl.ds((k + d) * 8, 8), :] for d in (0, TILE // 2)])
            ws = [0.5 / (4.0 + c) for c in pair]
            for i in range(2):
                weight[s, 2 * k + i] = ws[i]
            for a in range(3):
                pair = split(source[s, a, :, tile(k)], source[s, a, :, tile(k + TILE // 2)])
                for i in range(2):
                    b = ws[i] * pair[i]
                    rhs[s, a, 2 * k + i] = b
                    first[s, a, 2 * k + i] = b

    def curl(e, e_x):
        ex, ey, ez = e
        hx = (y_up(ez) - ez) - (z_up(ey) - ey)
        hy = (z_up(ex) - ex) - (e_x[2] - ez)
        hz = (e_x[1] - ey) - (y_up(ex) - ex)
        return hx, hy, hz

    def sweep(src, dst):
        before = []
        for s in range(S_DEV):
            ends = [jnp.where(low, half(src[s, a, 0]), 0.0) for a in range(3)]
            for a in range(1, 3):
                src[s, a, TILE] = ends[a]
            _, hy, hz = curl([src[s, a, TILE - 1] for a in range(3)], ends)
            before.append(tuple(jnp.where(low, 0.0, half(v))[None] for v in (hy, hz)))

        def body(b, carry):
            at = pl.ds(b * BATCH, BATCH)
            lasts = []
            for s in range(S_DEV):
                e = [src[s, a, at] for a in range(3)]
                after = pl.ds(b * BATCH + BATCH, 1)
                e_x = [None] + [jnp.concatenate([e[a][1:], src[s, a, after]], 0) for a in (1, 2)]
                hx, hy, hz = curl(e, e_x)
                hy_x = jnp.concatenate([carry[s][0], hy[:-1]], 0)
                hz_x = jnp.concatenate([carry[s][1], hz[:-1]], 0)
                back = (
                    (z_down(hy) - hy) - (y_down(hz) - hz),
                    (hz_x - hz) - (z_down(hx) - hx),
                    (y_down(hx) - hx) - (hy_x - hy),
                )
                w = weight[s, at]
                keep = 0.5 + 4.0 * w
                for a in range(3):
                    dst[s, a, at] = keep * e[a] + (rhs[s, a, at] - w * back[a])
                lasts.append((hy[-1:], hz[-1:]))
            return tuple(lasts)

        lax.fori_loop(0, TILE // BATCH, body, tuple(before), unroll=4)

    sweep(first, second)
    sweep(second, first)
    sweep(first, second)

    for k in range(TILE // 2):
        for s in range(S_DEV):
            for a in range(3):
                pair = split(observed[s, a, :, tile(k)], observed[s, a, :, tile(k + TILE // 2)])
                for i in range(2):
                    b = weight[s, 2 * k + i] * (second[s, a, 2 * k + i] - pair[i])
                    rhs[s, a, 2 * k + i] = b
                    first[s, a, 2 * k + i] = b

    sweep(first, third)
    sweep(third, first)
    sweep(first, third)

    for k in range(TILE // 2):
        for s in range(S_DEV):
            p, q = (
                sum(second[s, a, 2 * k + i] * third[s, a, 2 * k + i] for a in range(3)) for i in range(2)
            )
            for d, v in ((0, jnp.where(low, p, half(q))), (TILE // 2, jnp.where(low, half(p), q))):
                at = pl.ds((k + d) * 8, 8)
                part[s, at, :] = -cond[s, at, :] * v

    out[...] = jnp.zeros_like(out)
    for t in range(TILES):
        s, z = t // LZ, t % LZ
        got = part[s, pl.ds(z, TILE, stride=8), :]
        out[pl.ds(pl.multiple_of(place[t] * TILE, TILE), TILE), :] = jnp.where(row < lengths[s, z], got, 0.0)


def send_kernel(slots, arrived, send, recv, core_send, core_recv, own_sem):
    me = lax.axis_index("mdl")
    meet([partner(*d)[0] for d in FAR_FIRST] + [other_core()])
    copies, forwards = {}, []
    for dh, dx in FAR_FIRST:
        to, m = partner(dh, dx)
        k = dh * NX + dx
        copies[dh, dx] = remote(slots.at[m], arrived.at[0, me], send.at[k], recv.at[k], to)
        copies[dh, dx].start()
    own = pltpu.make_async_copy(slots.at[me], arrived.at[0, me], own_sem)
    own.start()
    forwards.append(remote(slots.at[me], arrived.at[1, me], core_send.at[0], core_recv.at[0], other_core()))
    forwards[0].start()
    for dh, dx in FAR_FIRST[::-1]:
        _, m = partner(dh, dx)
        back = (-dh % 2, -dx % NX)
        copies[back].wait_recv()
        k = dh * NX + dx
        forwards.append(
            remote(arrived.at[0, m], arrived.at[1, m], core_send.at[k], core_recv.at[k], other_core())
        )
        forwards[-1].start()
    own.wait()
    for d in FAR_FIRST:
        copies[d].wait_send()
    for f in forwards:
        f.wait()


def add_kernel(starts, arrived, block, total):
    total[...] = jnp.zeros_like(total)
    at = pl.ds(pl.multiple_of(lax.axis_index("grp") * SHARE, SHARE), SHARE)
    mine = block[at, :]
    lane = lax.broadcasted_iota(jnp.int32, (SHARE, 128), 1)
    left = jnp.where(lane == 0, mine, pltpu.roll(mine, 1, 1))
    right = jnp.where(lane == 127, mine, pltpu.roll(mine, 127, 1))
    total[at, :] = BETA * (2.0 * mine - left - right)
    for side in range(2):
        for m in range(OWN):
            for k in range(CAP):
                at = pl.ds(starts[side, m, k], TILE)
                total[at, :] += arrived[side, m, pl.ds(k * TILE, TILE), :]


CUT = SHARE // 2
Z_ORDER = [4, 3, 5, 2, 6, 1, 7]


def reduce_kernel(total, out, z_box, y_box, z_sum, y_sum, zy_box, yz_box, z_sem, y_sem, zy_sem, yz_sem):
    z, y, c, h, x = here()
    m = lax.axis_index("mdl")

    def chip(dz, dy):
        return ((((z + dz) % NZ) * NY + (y + dy) % NY) * 2 + c, m)

    def send(src, dst, sem, i, to):
        copy = remote(src, dst, sem.at[0, i], sem.at[1, i], to)
        copy.start()
        return copy

    meet([chip(d, 0) for d in Z_ORDER] + [chip(0, d) for d in range(1, NY)])
    low, high = pl.ds(0, CUT), pl.ds(CUT, SHARE - CUT)
    along_z, along_y, then_y, then_z = {}, {}, {}, {}
    for i, d in enumerate(Z_ORDER):
        if i < NY - 1:
            e = i + 1
            along_y[e] = send(total.at[:, (y + e) % NY, c, high, :], y_box.at[e - 1], y_sem, e - 1, chip(0, e))
        along_z[d] = send(total.at[(z + d) % NZ, :, c, low, :], z_box.at[d - 1], z_sem, d - 1, chip(d, 0))
    for copy in along_y.values():
        copy.wait_recv()
    for d in Z_ORDER + [0]:
        j = (z + d) % NZ
        y_sum[d] = total[j, y, c, high, :] + sum(y_box[k, j] for k in range(NY - 1))
        if d:
            then_z[d] = send(y_sum.at[d], yz_box.at[d - 1], yz_sem, d - 1, chip(d, 0))
    for copy in along_z.values():
        copy.wait_recv()
    for d in (2, 1, 3, 0):
        j = (y + d) % NY
        z_sum[d] = total[z, j, c, low, :] + sum(z_box[k, j] for k in range(NZ - 1))
        if d:
            then_y[d] = send(z_sum.at[d], zy_box.at[d - 1], zy_sem, d - 1, chip(0, d))
    for copy in then_z.values():
        copy.wait()
    out[high, :] = y_sum[0] + sum(yz_box[k] for k in range(NZ - 1))
    for copy in then_y.values():
        copy.wait()
    out[low, :] = z_sum[0] + sum(zy_box[k] for k in range(NY - 1))
    for copy in list(along_z.values()) + list(along_y.values()):
        copy.wait_send()


def per_device(model, source, observed, owner_ids, offsets, lengths):
    block = model.reshape(ROWS, 128)
    f32, i32 = jnp.float32, jnp.int32
    dma = pltpu.SemaphoreType.DMA
    place, request = pl.pallas_call(
        tables_kernel,
        out_shape=(jax.ShapeDtypeStruct((TILES,), i32), jax.ShapeDtypeStruct((OWN, 128), i32)),
        in_specs=[SMEM, SMEM],
        out_specs=(SMEM, SMEM),
        scratch_shapes=[pltpu.SMEM((OWN,), i32)],
        name="tables",
    )(owner_ids.transpose(0, 2, 1), offsets)
    values, starts = pl.pallas_call(
        fetch_kernel,
        out_shape=(
            jax.ShapeDtypeStruct((OWN, SLOT_ROWS, 128), f32),
            jax.ShapeDtypeStruct((2, OWN, 128), i32),
        ),
        in_specs=[SMEM, VMEM],
        out_specs=(VMEM, SMEM),
        scratch_shapes=[pltpu.VMEM((OWN, SLOT_ROWS, 128), f32)] + [dma((OWN,))] * 4 + [dma((2,))],
        compiler_params=pltpu.CompilerParams(collective_id=0, has_side_effects=True),
        name="fetch",
    )(request, block)
    fields = pltpu.VMEM((S_DEV, 3, TILE + 1, 8, 128), f32)
    slots = pl.pallas_call(
        solve_kernel,
        out_shape=jax.ShapeDtypeStruct((OWN * SLOT_ROWS, 128), f32),
        in_specs=[SMEM, SMEM, VMEM, VMEM, VMEM],
        out_specs=VMEM,
        scratch_shapes=[
            pltpu.VMEM((S_DEV, TILE * 8, 128), f32),
            pltpu.VMEM((S_DEV, TILE, 8, 128), f32),
            fields,
            fields,
            fields,
            pltpu.VMEM((S_DEV, 3, TILE, 8, 128), f32),
            pltpu.VMEM((S_DEV, TILE * 8, 128), f32),
        ],
        compiler_params=pltpu.CompilerParams(vmem_limit_bytes=32 << 20),
        name="solve",
    )(place, lengths, values.reshape(OWN * SLOT_ROWS, 128), source, observed)
    arrived = pl.pallas_call(
        send_kernel,
        out_shape=jax.ShapeDtypeStruct((2, OWN, SLOT_ROWS, 128), f32),
        in_specs=[VMEM],
        out_specs=VMEM,
        scratch_shapes=[dma((OWN,))] * 4 + [dma],
        compiler_params=pltpu.CompilerParams(collective_id=1, has_side_effects=True),
        name="send",
    )(slots.reshape(OWN, SLOT_ROWS, 128))
    total = pl.pallas_call(
        add_kernel,
        out_shape=jax.ShapeDtypeStruct((ROWS, 128), f32),
        in_specs=[SMEM, VMEM, VMEM],
        out_specs=VMEM,
        compiler_params=pltpu.CompilerParams(vmem_limit_bytes=32 << 20),
        name="add",
    )(starts, arrived, block)
    gradient = pl.pallas_call(
        reduce_kernel,
        out_shape=jax.ShapeDtypeStruct((SHARE, 128), f32),
        in_specs=[VMEM],
        out_specs=VMEM,
        scratch_shapes=[
            pltpu.VMEM((NZ - 1, NY, CUT, 128), f32),
            pltpu.VMEM((NY - 1, NZ, SHARE - CUT, 128), f32),
            pltpu.VMEM((NY, CUT, 128), f32),
            pltpu.VMEM((NZ, SHARE - CUT, 128), f32),
            pltpu.VMEM((NY - 1, CUT, 128), f32),
            pltpu.VMEM((NZ - 1, SHARE - CUT, 128), f32),
            dma((2, NZ - 1)),
            dma((2, NY - 1)),
            dma((2, NY - 1)),
            dma((2, NZ - 1)),
        ],
        compiler_params=pltpu.CompilerParams(
            collective_id=2, has_side_effects=True, vmem_limit_bytes=32 << 20
        ),
        name="reduce",
    )(total.reshape(NZ, NY, 2, SHARE, 128))
    return gradient[:, None, :]


def solution(mesh):
    placed = (
        P(None, "mdl", None),
        P(("grp", "mdl"), None, None, None),
        P(("grp", "mdl"), None, None, None),
        P(("grp", "mdl"), None, None),
        P(("grp", "mdl"), None),
        P(("grp", "mdl"), None),
    )
    return jax.shard_map(
        per_device, mesh=mesh, in_specs=placed, out_specs=P("grp", "mdl", None), check_vma=False
    )
```

```python
import functools

import jax
import jax.numpy as jnp
from jax import lax
from jax.experimental import pallas as pl
from jax.experimental.pallas import tpu as pltpu
from jax.sharding import PartitionSpec as P

LZ = 8
S_DEV = 2
TILES = S_DEV * LZ
TILE = 32
ROWS = 4096
CAP = 4
AIR = 0.05
BETA = 0.5

NZ, NY, NX = 8, 4, 4
OWN = 2 * NX
SLOT_ROWS = CAP * TILE
SHARE = ROWS // (NZ * NY * 2)

MESH = pl.DeviceIdType.MESH
SMEM = pl.BlockSpec(memory_space=pltpu.SMEM)
VMEM = pl.BlockSpec(memory_space=pltpu.VMEM)
FAR_FIRST = [(1, 2), (1, 1), (1, 3), (1, 0), (0, 2), (0, 1), (0, 3)]
Z_ORDER = [4, 3, 5, 2, 6, 1, 7]


def here():
    g, m = lax.axis_index("grp"), lax.axis_index("mdl")
    return g // (2 * NY), (g // 2) % NY, g % 2, m // NX, m % NX


def partner(dh, dx, dz=0):
    z, y, c, h, x = here()
    y = NY - 1 - y if dh % 2 else y
    m = ((h + dh) % 2) * NX + (x + dx) % NX
    return ((((z + dz) % NZ) * NY + y) * 2 + c, m), m


def other_core():
    z, y, c, h, x = here()
    return ((z * NY + y) * 2 + 1 - c, h * NX + x)


def meet(ids):
    barrier = pltpu.get_barrier_semaphore()
    for i in ids:
        pl.semaphore_signal(barrier, inc=1, device_id=i, device_id_type=MESH)
    pl.semaphore_wait(barrier, len(ids))


def remote(src, dst, send, recv, to):
    return pltpu.make_async_remote_copy(
        src_ref=src, dst_ref=dst, send_sem=send, recv_sem=recv, device_id=to, device_id_type=MESH
    )


def tables_kernel(owner, offset, place, request, counts):
    for o in range(OWN):
        counts[o] = 0
        for k in range(CAP):
            request[o, k] = 0
    for t in range(TILES):
        o = owner[t // LZ, 0, t % LZ]
        k = counts[o]
        counts[o] = k + 1
        place[t] = o * CAP + k
        request[o, k] = offset[t // LZ, t % LZ]


def fetch_kernel(
    request, block, values, starts, outbox, ask_send, ask_recv, row_send, row_recv, core_sem, z_send, z_recv
):
    me = lax.axis_index("mdl")
    z = here()[0]
    z_ids = {d: partner(0, 0, d)[0] for d in Z_ORDER}
    meet([partner(*d)[0] for d in FAR_FIRST] + [other_core()] + list(z_ids.values()))
    asks, answers = {}, {}
    for dh, dx in FAR_FIRST:
        to, m = partner(dh, dx)
        k = dh * NX + dx
        asks[dh, dx] = remote(request.at[m], starts.at[z, 0, me], ask_send.at[k], ask_recv.at[k], to)
        asks[dh, dx].start()
    for k in range(CAP):
        starts[z, 0, me, k] = request[me, k]
    for dh, dx in FAR_FIRST:
        back = (-dh % 2, -dx % NX)
        asks[back].wait_recv()
        to, m = partner(dh, dx)
        k = dh * NX + dx
        for i in range(CAP):
            outbox[k, pl.ds(i * TILE, TILE), :] = block[pl.ds(starts[z, 0, m, i], TILE), :]
        answers[dh, dx] = remote(outbox.at[k], values.at[me], row_send.at[k], row_recv.at[k], to)
        answers[dh, dx].start()
    pass_on = remote(starts.at[z, 0], starts.at[z, 1], core_sem.at[0], core_sem.at[1], other_core())
    pass_on.start()
    for k in range(CAP):
        values[me, pl.ds(k * TILE, TILE), :] = block[pl.ds(starts[z, 0, me, k], TILE), :]
    pass_on.wait()
    tables = [remote(starts.at[z], starts.at[z], z_send.at[d], z_recv.at[d], z_ids[d]) for d in Z_ORDER]
    for copy in tables:
        copy.start()
    for d in FAR_FIRST:
        asks[d].wait_send()
        answers[d].wait()
    for copy in tables:
        copy.wait()


BATCH = 4


def solve_kernel(
    place, lengths, values, source, observed, out, cond, weight, first, second, third, rhs, part, by_row
):
    lane = lax.broadcasted_iota(jnp.int32, (8, 128), 1)
    layer = lax.broadcasted_iota(jnp.int32, (8, 128), 0)
    low = lane < 64
    y_next, y_prev = lane % 64 != 63, lane % 64 != 0
    z_next, z_prev = layer != LZ - 1, layer != 0
    row = lax.broadcasted_iota(jnp.int32, (TILE, 128), 0)

    def half(v):
        return pltpu.roll(v, 64, 1)

    def shift(mask, by, axis):
        def one(v):
            return jnp.where(mask, pltpu.roll(v, by, axis), 0.0)

        return lambda v: one(v) if v.ndim == 2 else jnp.stack([one(v[i]) for i in range(v.shape[0])])

    y_up, y_down = shift(y_next, 127, 1), shift(y_prev, 1, 1)
    z_up, z_down = shift(z_next, LZ - 1, 0), shift(z_prev, 1, 0)

    for t in range(TILES):
        s, z = t // LZ, t % LZ
        got = values[pl.ds(pl.multiple_of(place[t] * TILE, TILE), TILE), :]
        cond[s, pl.ds(z, TILE, stride=8), :] = jnp.where(row < lengths[s, z], jnp.exp(got), AIR)

    def split(a, b):
        return jnp.where(low, a, half(b)), jnp.where(low, half(a), b)

    def tile(k):
        return pl.ds(k * 128, 128)

    for k in range(TILE // 2):
        for s in range(S_DEV):
            pair = split(*[cond[s, pl.ds((k + d) * 8, 8), :] for d in (0, TILE // 2)])
            ws = [0.5 / (4.0 + c) for c in pair]
            for i in range(2):
                weight[s, 2 * k + i] = ws[i]
            for a in range(3):
                pair = split(source[s, a, :, tile(k)], source[s, a, :, tile(k + TILE // 2)])
                for i in range(2):
                    b = ws[i] * pair[i]
                    rhs[s, a, 2 * k + i] = b
                    first[s, a, 2 * k + i] = b

    def curl(e, e_x):
        ex, ey, ez = e
        hx = (y_up(ez) - ez) - (z_up(ey) - ey)
        hy = (z_up(ex) - ex) - (e_x[2] - ez)
        hz = (e_x[1] - ey) - (y_up(ex) - ex)
        return hx, hy, hz

    def sweep(src, dst):
        before = []
        for s in range(S_DEV):
            ends = [jnp.where(low, half(src[s, a, 0]), 0.0) for a in range(3)]
            for a in range(1, 3):
                src[s, a, TILE] = ends[a]
            _, hy, hz = curl([src[s, a, TILE - 1] for a in range(3)], ends)
            before.append(tuple(jnp.where(low, 0.0, half(v))[None] for v in (hy, hz)))

        def body(b, carry):
            at = pl.ds(b * BATCH, BATCH)
            lasts = []
            for s in range(S_DEV):
                e = [src[s, a, at] for a in range(3)]
                after = pl.ds(b * BATCH + BATCH, 1)
                e_x = [None] + [jnp.concatenate([e[a][1:], src[s, a, after]], 0) for a in (1, 2)]
                hx, hy, hz = curl(e, e_x)
                hy_x = jnp.concatenate([carry[s][0], hy[:-1]], 0)
                hz_x = jnp.concatenate([carry[s][1], hz[:-1]], 0)
                back = (
                    (z_down(hy) - hy) - (y_down(hz) - hz),
                    (hz_x - hz) - (z_down(hx) - hx),
                    (y_down(hx) - hx) - (hy_x - hy),
                )
                w = weight[s, at]
                keep = 0.5 + 4.0 * w
                for a in range(3):
                    dst[s, a, at] = keep * e[a] + (rhs[s, a, at] - w * back[a])
                lasts.append((hy[-1:], hz[-1:]))
            return tuple(lasts)

        lax.fori_loop(0, TILE // BATCH, body, tuple(before), unroll=4)

    sweep(first, second)
    sweep(second, first)
    sweep(first, second)

    for k in range(TILE // 2):
        for s in range(S_DEV):
            for a in range(3):
                pair = split(observed[s, a, :, tile(k)], observed[s, a, :, tile(k + TILE // 2)])
                for i in range(2):
                    b = weight[s, 2 * k + i] * (second[s, a, 2 * k + i] - pair[i])
                    rhs[s, a, 2 * k + i] = b
                    first[s, a, 2 * k + i] = b

    sweep(first, third)
    sweep(third, first)
    sweep(first, third)

    for k in range(TILE // 2):
        for s in range(S_DEV):
            p, q = (
                sum(second[s, a, 2 * k + i] * third[s, a, 2 * k + i] for a in range(3)) for i in range(2)
            )
            for d, v in ((0, jnp.where(low, p, half(q))), (TILE // 2, jnp.where(low, half(p), q))):
                at = pl.ds((k + d) * 8, 8)
                part[s, at, :] = -cond[s, at, :] * v

    by_row[...] = jnp.zeros_like(by_row)
    for t in range(TILES):
        s, z = t // LZ, t % LZ
        got = part[s, pl.ds(z, TILE, stride=8), :]
        by_row[pl.ds(pl.multiple_of(place[t] * TILE, TILE), TILE), :] = jnp.where(row < lengths[s, z], got, 0.0)
    for o in range(OWN):
        cells = by_row[pl.ds(o * SLOT_ROWS, SLOT_ROWS), :].T.reshape(NZ, 2, 8, 128)
        for k in range(2):
            out[k, o] = cells[:, k]


SPREAD = [(dh, dx, dz) for dz in Z_ORDER + [0] for dh, dx in FAR_FIRST + [(0, 0)] if (dh, dx, dz) != (0, 0, 0)]


def send_kernel(slots, arrived, pair, send, recv, core_send, core_recv, own_sem):
    me = lax.axis_index("mdl")
    z, y, c, h, x = here()
    meet([partner(*d)[0] for d in SPREAD] + [other_core()])
    swap = remote(slots.at[1 - c], pair.at[1], core_send, core_recv, other_core())
    swap.start()
    keep = pltpu.make_async_copy(slots.at[c], pair.at[0], own_sem)
    keep.start()
    keep.wait()
    swap.wait()
    copies = []
    for dh, dx, dz in SPREAD:
        to, m = partner(dh, dx, dz)
        k = (dh * NX + dx) * NZ + dz
        copies.append(remote(pair.at[:, m, (z + dz) % NZ], arrived.at[k], send, recv, to))
        copies[-1].start()
    own = pltpu.make_async_copy(pair.at[:, me, z], arrived.at[0], own_sem)
    own.start()
    own.wait()
    others = pl.ds(1, OWN * NZ - 1)
    pltpu.make_async_copy(arrived.at[others], arrived.at[others], recv).wait()
    pltpu.make_async_copy(arrived.at[others], arrived.at[others], send).wait()


PARTS = 2 * CAP


def add_kernel(starts, arrived, block, total, smooth, sums):
    z, y, c, h, x = here()
    at = pl.ds(pl.multiple_of(lax.axis_index("grp") * SHARE, SHARE), SHARE)
    mine = block[at, :]
    lane = lax.broadcasted_iota(jnp.int32, (SHARE, 128), 1)
    left = jnp.where(lane == 0, mine, pltpu.roll(mine, 1, 1))
    right = jnp.where(lane == 127, mine, pltpu.roll(mine, 127, 1))
    smooth[...] = BETA * (2.0 * mine - left - right)

    sums[...] = jnp.zeros_like(sums)
    lane = lax.broadcasted_iota(jnp.int32, (8, 128), 1)

    def one(k, carry):
        dz, dx, dh = k % NZ, (k // NZ) % NX, k // (NZ * NX)
        zs = (z + NZ - dz) % NZ
        ms = ((h + 2 - dh) % 2) * NX + (x + NX - dx) % NX
        for side in range(2):
            v = arrived[k, side]
            for i in range(CAP):
                start = starts[zs, side, ms, i]
                a, r = start // 128, start % 128
                moved = pltpu.roll(v, (r + 128 - i * TILE) % 128, 1)
                moved = jnp.where(((lane - r) & 127) < TILE, moved, 0.0)
                p = side * CAP + i
                sums[p, a] += jnp.where(lane >= r, moved, 0.0)
                sums[p, a + 1] += jnp.where(lane >= r, 0.0, moved)
        return carry

    lax.fori_loop(0, OWN * NZ, one, 0, unroll=2)
    total[...] = sum(sums[p, pl.ds(0, TILE)] for p in range(PARTS))


PLANE = [(dz, dy) for dz in Z_ORDER + [0] for dy in (2, 1, 3, 0) if (dz, dy) != (0, 0)]


def reduce_kernel(total, smooth, out, box, cells, turned, send, recv, core_send, core_recv):
    z, y, c, h, x = here()
    m = lax.axis_index("mdl")

    def chip(dz, dy):
        return ((((z + dz) % NZ) * NY + (y + dy) % NY) * 2 + c, m)

    meet([chip(*d) for d in PLANE] + [other_core()])
    for dz, dy in PLANE:
        src = total.at[((z + dz) % NZ) * NY + (y + dy) % NY]
        remote(src, box.at[dz * NY + dy], send, recv, chip(dz, dy)).start()
    others = pl.ds(1, NZ * NY - 1)
    pltpu.make_async_copy(box.at[others], box.at[others], recv).wait()
    box[0] = total[z * NY + y]
    for dz in range(NZ):
        cells[(z + NZ - dz) % NZ, c] = sum(box[dz * NY + dy] for dy in range(NY))
    swap = remote(cells.at[:, c], cells.at[:, c], core_send, core_recv, other_core())
    swap.start()
    swap.wait()
    turned[...] = cells[...].reshape(128, 128).T.reshape(2, SHARE, 128)
    out[...] = turned[c] + smooth[...]
    pltpu.make_async_copy(box.at[others], box.at[others], send).wait()


def per_device(model, source, observed, owner_ids, offsets, lengths):
    block = model.reshape(ROWS, 128)
    f32, i32 = jnp.float32, jnp.int32
    dma = pltpu.SemaphoreType.DMA
    place, request = pl.pallas_call(
        tables_kernel,
        out_shape=(jax.ShapeDtypeStruct((TILES,), i32), jax.ShapeDtypeStruct((OWN, 128), i32)),
        in_specs=[SMEM, SMEM],
        out_specs=(SMEM, SMEM),
        scratch_shapes=[pltpu.SMEM((OWN,), i32)],
        name="tables",
    )(owner_ids.transpose(0, 2, 1), offsets)
    values, starts = pl.pallas_call(
        fetch_kernel,
        out_shape=(
            jax.ShapeDtypeStruct((OWN, SLOT_ROWS, 128), f32),
            jax.ShapeDtypeStruct((NZ, 2, OWN, 128), i32),
        ),
        in_specs=[SMEM, VMEM],
        out_specs=(VMEM, SMEM),
        scratch_shapes=[pltpu.VMEM((OWN, SLOT_ROWS, 128), f32)]
        + [dma((OWN,))] * 4
        + [dma((2,)), dma((NZ,)), dma((NZ,))],
        compiler_params=pltpu.CompilerParams(collective_id=0, has_side_effects=True),
        name="fetch",
    )(request, block)
    fields = pltpu.VMEM((S_DEV, 3, TILE + 1, 8, 128), f32)
    slots = pl.pallas_call(
        solve_kernel,
        out_shape=jax.ShapeDtypeStruct((2, OWN, NZ, 8, 128), f32),
        in_specs=[SMEM, SMEM, VMEM, VMEM, VMEM],
        out_specs=VMEM,
        scratch_shapes=[
            pltpu.VMEM((S_DEV, TILE * 8, 128), f32),
            pltpu.VMEM((S_DEV, TILE, 8, 128), f32),
            fields,
            fields,
            fields,
            pltpu.VMEM((S_DEV, 3, TILE, 8, 128), f32),
            pltpu.VMEM((S_DEV, TILE * 8, 128), f32),
            pltpu.VMEM((OWN * SLOT_ROWS, 128), f32),
        ],
        compiler_params=pltpu.CompilerParams(vmem_limit_bytes=32 << 20),
        name="solve",
    )(place, lengths, values.reshape(OWN * SLOT_ROWS, 128), source, observed)
    arrived = pl.pallas_call(
        send_kernel,
        out_shape=jax.ShapeDtypeStruct((OWN * NZ, 2, 8, 128), f32),
        in_specs=[VMEM],
        out_specs=VMEM,
        scratch_shapes=[pltpu.VMEM((2, OWN, NZ, 8, 128), f32)] + [dma] * 5,
        compiler_params=pltpu.CompilerParams(collective_id=1, has_side_effects=True),
        name="send",
    )(slots)
    total, smooth = pl.pallas_call(
        add_kernel,
        out_shape=(
            jax.ShapeDtypeStruct((NZ * NY, 8, 128), f32),
            jax.ShapeDtypeStruct((SHARE, 128), f32),
        ),
        in_specs=[SMEM, VMEM, VMEM],
        out_specs=(VMEM, VMEM),
        scratch_shapes=[pltpu.VMEM((PARTS, TILE + 1, 8, 128), f32)],
        compiler_params=pltpu.CompilerParams(vmem_limit_bytes=32 << 20),
        name="add",
    )(starts, arrived, block)
    gradient = pl.pallas_call(
        reduce_kernel,
        out_shape=jax.ShapeDtypeStruct((SHARE, 128), f32),
        in_specs=[VMEM, VMEM],
        out_specs=VMEM,
        scratch_shapes=[
            pltpu.VMEM((NZ * NY, 8, 128), f32),
            pltpu.VMEM((NZ, 2, 8, 128), f32),
            pltpu.VMEM((2, SHARE, 128), f32),
        ]
        + [dma] * 4,
        compiler_params=pltpu.CompilerParams(
            collective_id=2, has_side_effects=True, vmem_limit_bytes=32 << 20
        ),
        name="reduce",
    )(total, smooth)
    return gradient[:, None, :]


def solution(mesh):
    placed = (
        P(None, "mdl", None),
        P(("grp", "mdl"), None, None, None),
        P(("grp", "mdl"), None, None, None),
        P(("grp", "mdl"), None, None),
        P(("grp", "mdl"), None),
        P(("grp", "mdl"), None),
    )
    return jax.shard_map(
        per_device, mesh=mesh, in_specs=placed, out_specs=P("grp", "mdl", None), check_vma=False
    )
```

```python
import functools

import jax
import jax.numpy as jnp
from jax import lax
from jax.experimental import pallas as pl
from jax.experimental.pallas import tpu as pltpu
from jax.sharding import PartitionSpec as P

LZ = 8
S_DEV = 2
TILES = S_DEV * LZ
TILE = 32
ROWS = 4096
CAP = 4
AIR = 0.05
BETA = 0.5

NZ, NY, NX = 8, 4, 4
OWN = 2 * NX
SLOT_ROWS = CAP * TILE
SHARE = ROWS // (NZ * NY * 2)

MESH = pl.DeviceIdType.MESH
SMEM = pl.BlockSpec(memory_space=pltpu.SMEM)
VMEM = pl.BlockSpec(memory_space=pltpu.VMEM)
HBM = pl.BlockSpec(memory_space=pl.ANY)
FAR_FIRST = [(1, 2), (1, 1), (1, 3), (1, 0), (0, 2), (0, 1), (0, 3)]


def here():
    g, m = lax.axis_index("grp"), lax.axis_index("mdl")
    return g // (2 * NY), (g // 2) % NY, g % 2, m // NX, m % NX


def partner(dh, dx):
    z, y, c, h, x = here()
    y = NY - 1 - y if dh % 2 else y
    m = ((h + dh) % 2) * NX + (x + dx) % NX
    return ((z * NY + y) * 2 + c, m), m


def other_core():
    z, y, c, h, x = here()
    return ((z * NY + y) * 2 + 1 - c, h * NX + x)


def meet(ids):
    barrier = pltpu.get_barrier_semaphore()
    for i in ids:
        pl.semaphore_signal(barrier, inc=1, device_id=i, device_id_type=MESH)
    pl.semaphore_wait(barrier, len(ids))


def remote(src, dst, send, recv, to):
    return pltpu.make_async_remote_copy(
        src_ref=src, dst_ref=dst, send_sem=send, recv_sem=recv, device_id=to, device_id_type=MESH
    )


def tables_kernel(owner, offset, place, holds, request, counts):
    for o in range(OWN):
        counts[o] = 0
        for k in range(CAP):
            request[o, k] = 0
            holds[o * CAP + k] = TILES * TILE
    for t in range(TILES):
        o = owner[t // LZ, 0, t % LZ]
        k = counts[o]
        counts[o] = k + 1
        place[t] = (o * CAP + k) * TILE
        holds[o * CAP + k] = t * TILE
        request[o, k] = offset[t // LZ, t % LZ]


BATCH = 4


def solve(place, lengths, values, source, observed, by_layer, cond, weight, first, second, third, rhs, part):
    lane = lax.broadcasted_iota(jnp.int32, (8, 128), 1)
    layer = lax.broadcasted_iota(jnp.int32, (8, 128), 0)
    low = lane < 64
    y_next, y_prev = lane % 64 != 63, lane % 64 != 0
    z_next, z_prev = layer != LZ - 1, layer != 0
    row = lax.broadcasted_iota(jnp.int32, (TILE, 128), 0)

    def half(v):
        return pltpu.roll(v, 64, 1)

    def shift(mask, by, axis):
        def one(v):
            return jnp.where(mask, pltpu.roll(v, by, axis), 0.0)

        return lambda v: one(v) if v.ndim == 2 else jnp.stack([one(v[i]) for i in range(v.shape[0])])

    y_up, y_down = shift(y_next, 127, 1), shift(y_prev, 1, 1)
    z_up, z_down = shift(z_next, LZ - 1, 0), shift(z_prev, 1, 0)

    for t in range(TILES):
        s, z = t // LZ, t % LZ
        got = values[pl.ds(place[t], TILE), :]
        cond[s, pl.ds(z, TILE, stride=8), :] = jnp.where(row < lengths[s, z], jnp.exp(got), AIR)

    def split(a, b):
        return jnp.where(low, a, half(b)), jnp.where(low, half(a), b)

    def tile(k):
        return pl.ds(k * 128, 128)

    for k in range(TILE // 2):
        for s in range(S_DEV):
            pair = split(*[cond[s, pl.ds((k + d) * 8, 8), :] for d in (0, TILE // 2)])
            ws = [0.5 / (4.0 + c) for c in pair]
            for i in range(2):
                weight[s, 2 * k + i] = ws[i]
            for a in range(3):
                pair = split(source[s, a, :, tile(k)], source[s, a, :, tile(k + TILE // 2)])
                for i in range(2):
                    b = ws[i] * pair[i]
                    rhs[s, a, 2 * k + i] = b
                    first[s, a, 2 * k + i] = b

    def curl(e, e_x):
        ex, ey, ez = e
        hx = (y_up(ez) - ez) - (z_up(ey) - ey)
        hy = (z_up(ex) - ex) - (e_x[2] - ez)
        hz = (e_x[1] - ey) - (y_up(ex) - ex)
        return hx, hy, hz

    def sweep(src, dst):
        before = []
        for s in range(S_DEV):
            ends = [jnp.where(low, half(src[s, a, 0]), 0.0) for a in range(3)]
            for a in range(1, 3):
                src[s, a, TILE] = ends[a]
            _, hy, hz = curl([src[s, a, TILE - 1] for a in range(3)], ends)
            before.append(tuple(jnp.where(low, 0.0, half(v))[None] for v in (hy, hz)))

        def body(b, carry):
            at = pl.ds(b * BATCH, BATCH)
            lasts = []
            for s in range(S_DEV):
                e = [src[s, a, at] for a in range(3)]
                after = pl.ds(b * BATCH + BATCH, 1)
                e_x = [None] + [jnp.concatenate([e[a][1:], src[s, a, after]], 0) for a in (1, 2)]
                hx, hy, hz = curl(e, e_x)
                hy_x = jnp.concatenate([carry[s][0], hy[:-1]], 0)
                hz_x = jnp.concatenate([carry[s][1], hz[:-1]], 0)
                back = (
                    (z_down(hy) - hy) - (y_down(hz) - hz),
                    (hz_x - hz) - (z_down(hx) - hx),
                    (y_down(hx) - hx) - (hy_x - hy),
                )
                w = weight[s, at]
                keep = 0.5 + 4.0 * w
                for a in range(3):
                    dst[s, a, at] = keep * e[a] + (rhs[s, a, at] - w * back[a])
                lasts.append((hy[-1:], hz[-1:]))
            return tuple(lasts)

        lax.fori_loop(0, TILE // BATCH, body, tuple(before), unroll=4)

    sweep(first, second)
    sweep(second, first)
    sweep(first, second)

    for k in range(TILE // 2):
        for s in range(S_DEV):
            for a in range(3):
                pair = split(observed[s, a, :, tile(k)], observed[s, a, :, tile(k + TILE // 2)])
                for i in range(2):
                    b = weight[s, 2 * k + i] * (second[s, a, 2 * k + i] - pair[i])
                    rhs[s, a, 2 * k + i] = b
                    first[s, a, 2 * k + i] = b

    sweep(first, third)
    sweep(third, first)
    sweep(first, third)

    for k in range(TILE // 2):
        for s in range(S_DEV):
            p, q = (
                sum(second[s, a, 2 * k + i] * third[s, a, 2 * k + i] for a in range(3)) for i in range(2)
            )
            for d, v in ((0, jnp.where(low, p, half(q))), (TILE // 2, jnp.where(low, half(p), q))):
                at = pl.ds((k + d) * 8, 8)
                part[s, at, :] = -cond[s, at, :] * v

    for t in range(TILES):
        s, z = t // LZ, t % LZ
        got = part[s, pl.ds(z, TILE, stride=8), :]
        by_layer[pl.ds(t * TILE, TILE), :] = jnp.where(row < lengths[s, z], got, 0.0)
    by_layer[pl.ds(TILES * TILE, TILE), :] = jnp.zeros((TILE, 128), jnp.float32)


def front_kernel(
    place,
    holds,
    request,
    lengths,
    block_hbm,
    source_hbm,
    observed_hbm,
    arrived,
    starts,
    block,
    source,
    observed,
    values,
    outbox,
    slots,
    by_layer,
    *rest,
):
    fields, (load_sem, ask_send, ask_recv, row_send, row_recv, send, recv, core_send, core_recv, core_sem) = (
        rest[:7],
        rest[7:],
    )
    me = lax.axis_index("mdl")
    barrier = pltpu.get_barrier_semaphore()
    greeted = [partner(*d)[0] for d in FAR_FIRST] + [other_core()]
    for i in greeted:
        pl.semaphore_signal(barrier, inc=1, device_id=i, device_id_type=MESH)
    pairs = ((block_hbm, block), (source_hbm, source), (observed_hbm, observed))
    loads = [pltpu.make_async_copy(a, b, load_sem.at[i]) for i, (a, b) in enumerate(pairs)]
    for copy in loads:
        copy.start()
    pl.semaphore_wait(barrier, len(greeted))

    asks, answers = {}, {}
    for dh, dx in FAR_FIRST:
        to, m = partner(dh, dx)
        k = dh * NX + dx
        asks[dh, dx] = remote(request.at[m], starts.at[0, me], ask_send.at[k], ask_recv.at[k], to)
        asks[dh, dx].start()
    for k in range(CAP):
        starts[0, me, k] = request[me, k]
    loads[0].wait()
    for dh, dx in FAR_FIRST:
        back = (-dh % 2, -dx % NX)
        asks[back].wait_recv()
        to, m = partner(dh, dx)
        k = dh * NX + dx
        for i in range(CAP):
            outbox[k, pl.ds(i * TILE, TILE), :] = block[pl.ds(starts[0, m, i], TILE), :]
        answers[dh, dx] = remote(
            outbox.at[k], values.at[pl.ds(me * SLOT_ROWS, SLOT_ROWS)], row_send.at[k], row_recv.at[k], to
        )
        answers[dh, dx].start()
    pass_on = remote(starts.at[0], starts.at[1], core_sem.at[0], core_sem.at[1], other_core())
    pass_on.start()
    for k in range(CAP):
        at = pl.ds(me * SLOT_ROWS + k * TILE, TILE)
        values[at, :] = block[pl.ds(starts[0, me, k], TILE), :]
    for copy in loads[1:]:
        copy.wait()
    for d in FAR_FIRST:
        answers[d].wait_recv()

    solve(place, lengths, values, source, observed, by_layer, *fields)

    def fill(m):
        for k in range(CAP):
            slots[m, pl.ds(k * TILE, TILE), :] = by_layer[pl.ds(holds[m * CAP + k], TILE), :]

    copies, forwards = {}, []
    for dh, dx in FAR_FIRST:
        to, m = partner(dh, dx)
        k = dh * NX + dx
        fill(m)
        copies[dh, dx] = remote(slots.at[m], arrived.at[0, me], send.at[k], recv.at[k], to)
        copies[dh, dx].start()
    fill(me)
    own = pltpu.make_async_copy(slots.at[me], arrived.at[0, me], load_sem.at[0])
    own.start()
    forwards.append(remote(slots.at[me], arrived.at[1, me], core_send.at[0], core_recv.at[0], other_core()))
    forwards[0].start()
    for dh, dx in FAR_FIRST[::-1]:
        _, m = partner(dh, dx)
        back = (-dh % 2, -dx % NX)
        copies[back].wait_recv()
        k = dh * NX + dx
        forwards.append(
            remote(arrived.at[0, m], arrived.at[1, m], core_send.at[k], core_recv.at[k], other_core())
        )
        forwards[-1].start()
    for d in FAR_FIRST:
        asks[d].wait_send()
        answers[d].wait_send()
        copies[d].wait_send()
    for copy in [own, pass_on] + forwards:
        copy.wait()


def add_kernel(starts, arrived_hbm, block, total, arrived, mine, sems):
    at = pl.ds(pl.multiple_of(lax.axis_index("grp") * SHARE, SHARE), SHARE)
    rows = pltpu.make_async_copy(block.at[at], mine, sems.at[2])
    rows.start()
    sides = [pltpu.make_async_copy(arrived_hbm.at[i], arrived.at[i], sems.at[i]) for i in range(2)]
    for copy in sides:
        copy.start()
    total[...] = jnp.zeros_like(total)
    rows.wait()
    v = mine[...]
    lane = lax.broadcasted_iota(jnp.int32, (SHARE, 128), 1)
    left = jnp.where(lane == 0, v, pltpu.roll(v, 1, 1))
    right = jnp.where(lane == 127, v, pltpu.roll(v, 127, 1))
    total[at, :] = BETA * (2.0 * v - left - right)
    for side in range(2):
        sides[side].wait()
        for m in range(OWN):
            for k in range(CAP):
                at = pl.ds(starts[side, m, k], TILE)
                total[at, :] += arrived[side, m, pl.ds(k * TILE, TILE), :]


CUT = SHARE // 2
Z_ORDER = [4, 3, 5, 2, 6, 1, 7]


def reduce_kernel(total, out, z_box, y_box, z_sum, y_sum, zy_box, yz_box, z_sem, y_sem, zy_sem, yz_sem):
    z, y, c, h, x = here()
    m = lax.axis_index("mdl")

    def chip(dz, dy):
        return ((((z + dz) % NZ) * NY + (y + dy) % NY) * 2 + c, m)

    def send(src, dst, sem, i, to):
        copy = remote(src, dst, sem.at[0, i], sem.at[1, i], to)
        copy.start()
        return copy

    meet([chip(d, 0) for d in Z_ORDER] + [chip(0, d) for d in range(1, NY)])
    low, high = pl.ds(0, CUT), pl.ds(CUT, SHARE - CUT)
    along_z, along_y, then_y, then_z = {}, {}, {}, {}
    for i, d in enumerate(Z_ORDER):
        if i < NY - 1:
            e = i + 1
            along_y[e] = send(total.at[:, (y + e) % NY, c, high, :], y_box.at[e - 1], y_sem, e - 1, chip(0, e))
        along_z[d] = send(total.at[(z + d) % NZ, :, c, low, :], z_box.at[d - 1], z_sem, d - 1, chip(d, 0))
    for copy in along_y.values():
        copy.wait_recv()
    for d in Z_ORDER + [0]:
        j = (z + d) % NZ
        y_sum[d] = total[j, y, c, high, :] + sum(y_box[k, j] for k in range(NY - 1))
        if d:
            then_z[d] = send(y_sum.at[d], yz_box.at[d - 1], yz_sem, d - 1, chip(d, 0))
    for copy in along_z.values():
        copy.wait_recv()
    for d in (2, 1, 3, 0):
        j = (y + d) % NY
        z_sum[d] = total[z, j, c, low, :] + sum(z_box[k, j] for k in range(NZ - 1))
        if d:
            then_y[d] = send(z_sum.at[d], zy_box.at[d - 1], zy_sem, d - 1, chip(0, d))
    for copy in then_z.values():
        copy.wait()
    out[high, :] = y_sum[0] + sum(yz_box[k] for k in range(NZ - 1))
    for copy in then_y.values():
        copy.wait()
    out[low, :] = z_sum[0] + sum(zy_box[k] for k in range(NY - 1))
    for copy in list(along_z.values()) + list(along_y.values()):
        copy.wait_send()


def per_device(model, source, observed, owner_ids, offsets, lengths):
    block = model.reshape(ROWS, 128)
    f32, i32 = jnp.float32, jnp.int32
    dma = pltpu.SemaphoreType.DMA
    place, holds, request = pl.pallas_call(
        tables_kernel,
        out_shape=(
            jax.ShapeDtypeStruct((TILES,), i32),
            jax.ShapeDtypeStruct((OWN * CAP,), i32),
            jax.ShapeDtypeStruct((OWN, 128), i32),
        ),
        in_specs=[SMEM, SMEM],
        out_specs=(SMEM, SMEM, SMEM),
        scratch_shapes=[pltpu.SMEM((OWN,), i32)],
        name="tables",
    )(owner_ids.transpose(0, 2, 1), offsets)
    fields = pltpu.VMEM((S_DEV, 3, TILE + 1, 8, 128), f32)
    plain = pltpu.VMEM((S_DEV, TILE * 8, 128), f32)
    arrived, starts = pl.pallas_call(
        front_kernel,
        out_shape=(
            jax.ShapeDtypeStruct((2, OWN, SLOT_ROWS, 128), f32),
            jax.ShapeDtypeStruct((2, OWN, 128), i32),
        ),
        in_specs=[SMEM, SMEM, SMEM, SMEM, HBM, HBM, HBM],
        out_specs=(HBM, SMEM),
        scratch_shapes=[
            pltpu.VMEM((ROWS, 128), f32),
            pltpu.VMEM((S_DEV, 3, LZ, TILE * 128), f32),
            pltpu.VMEM((S_DEV, 3, LZ, TILE * 128), f32),
            pltpu.VMEM((OWN * SLOT_ROWS, 128), f32),
            pltpu.VMEM((OWN, SLOT_ROWS, 128), f32),
            pltpu.VMEM((OWN, SLOT_ROWS, 128), f32),
            pltpu.VMEM(((TILES + 1) * TILE, 128), f32),
            plain,
            pltpu.VMEM((S_DEV, TILE, 8, 128), f32),
            fields,
            fields,
            fields,
            pltpu.VMEM((S_DEV, 3, TILE, 8, 128), f32),
            plain,
            dma((3,)),
        ]
        + [dma((OWN,))] * 8
        + [dma((2,))],
        compiler_params=pltpu.CompilerParams(
            collective_id=0, has_side_effects=True, vmem_limit_bytes=60 << 20
        ),
        name="front",
    )(place, holds, request, lengths, block, source, observed)
    total = pl.pallas_call(
        add_kernel,
        out_shape=jax.ShapeDtypeStruct((ROWS, 128), f32),
        in_specs=[SMEM, HBM, HBM],
        out_specs=VMEM,
        scratch_shapes=[
            pltpu.VMEM((2, OWN, SLOT_ROWS, 128), f32),
            pltpu.VMEM((SHARE, 128), f32),
            dma((3,)),
        ],
        compiler_params=pltpu.CompilerParams(vmem_limit_bytes=58 << 20),
        name="add",
    )(starts, arrived, block)
    gradient = pl.pallas_call(
        reduce_kernel,
        out_shape=jax.ShapeDtypeStruct((SHARE, 128), f32),
        in_specs=[VMEM],
        out_specs=VMEM,
        scratch_shapes=[
            pltpu.VMEM((NZ - 1, NY, CUT, 128), f32),
            pltpu.VMEM((NY - 1, NZ, SHARE - CUT, 128), f32),
            pltpu.VMEM((NY, CUT, 128), f32),
            pltpu.VMEM((NZ, SHARE - CUT, 128), f32),
            pltpu.VMEM((NY - 1, CUT, 128), f32),
            pltpu.VMEM((NZ - 1, SHARE - CUT, 128), f32),
            dma((2, NZ - 1)),
            dma((2, NY - 1)),
            dma((2, NY - 1)),
            dma((2, NZ - 1)),
        ],
        compiler_params=pltpu.CompilerParams(
            collective_id=2, has_side_effects=True, vmem_limit_bytes=32 << 20
        ),
        name="reduce",
    )(total.reshape(NZ, NY, 2, SHARE, 128))
    return gradient[:, None, :]


def solution(mesh):
    placed = (
        P(None, "mdl", None),
        P(("grp", "mdl"), None, None, None),
        P(("grp", "mdl"), None, None, None),
        P(("grp", "mdl"), None, None),
        P(("grp", "mdl"), None),
        P(("grp", "mdl"), None),
    )
    return jax.shard_map(
        per_device, mesh=mesh, in_specs=placed, out_specs=P("grp", "mdl", None), check_vma=False
    )
```

```python
import functools

import jax
import jax.numpy as jnp
from jax import lax
from jax.experimental import pallas as pl
from jax.experimental.pallas import tpu as pltpu
from jax.sharding import PartitionSpec as P

LZ = 8
S_DEV = 2
TILES = S_DEV * LZ
TILE = 32
ROWS = 4096
CAP = 4
AIR = 0.05
BETA = 0.5

NZ, NY, NX = 8, 4, 4
OWN = 2 * NX
SLOT_ROWS = CAP * TILE
SHARE = ROWS // (NZ * NY * 2)

MESH = pl.DeviceIdType.MESH
SMEM = pl.BlockSpec(memory_space=pltpu.SMEM)
VMEM = pl.BlockSpec(memory_space=pltpu.VMEM)
HBM = pl.BlockSpec(memory_space=pl.ANY)
FAR_FIRST = [(1, 2), (1, 1), (1, 3), (1, 0), (0, 2), (0, 1), (0, 3)]


def here():
    g, m = lax.axis_index("grp"), lax.axis_index("mdl")
    return g // (2 * NY), (g // 2) % NY, g % 2, m // NX, m % NX


def partner(dh, dx):
    z, y, c, h, x = here()
    y = NY - 1 - y if dh % 2 else y
    m = ((h + dh) % 2) * NX + (x + dx) % NX
    return ((z * NY + y) * 2 + c, m), m


def other_core():
    z, y, c, h, x = here()
    return ((z * NY + y) * 2 + 1 - c, h * NX + x)


def meet(ids):
    barrier = pltpu.get_barrier_semaphore()
    for i in ids:
        pl.semaphore_signal(barrier, inc=1, device_id=i, device_id_type=MESH)
    pl.semaphore_wait(barrier, len(ids))


def remote(src, dst, send, recv, to):
    return pltpu.make_async_remote_copy(
        src_ref=src, dst_ref=dst, send_sem=send, recv_sem=recv, device_id=to, device_id_type=MESH
    )


def tables_kernel(owner, offset, place, holds, request, counts):
    for o in range(OWN):
        counts[o] = 0
        for k in range(CAP):
            request[o, k] = 0
            holds[o * CAP + k] = TILES * TILE
    for t in range(TILES):
        o = owner[t // LZ, 0, t % LZ]
        k = counts[o]
        counts[o] = k + 1
        place[t] = (o * CAP + k) * TILE
        holds[o * CAP + k] = t * TILE
        request[o, k] = offset[t // LZ, t % LZ]


BATCH = 4


def solve(place, lengths, values, source, observed, by_layer, cond, weight, first, second, third, rhs, part):
    lane = lax.broadcasted_iota(jnp.int32, (8, 128), 1)
    layer = lax.broadcasted_iota(jnp.int32, (8, 128), 0)
    low = lane < 64
    y_next, y_prev = lane % 64 != 63, lane % 64 != 0
    z_next, z_prev = layer != LZ - 1, layer != 0
    row = lax.broadcasted_iota(jnp.int32, (TILE, 128), 0)

    def half(v):
        return pltpu.roll(v, 64, 1)

    def shift(mask, by, axis):
        def one(v):
            return jnp.where(mask, pltpu.roll(v, by, axis), 0.0)

        return lambda v: one(v) if v.ndim == 2 else jnp.stack([one(v[i]) for i in range(v.shape[0])])

    y_up, y_down = shift(y_next, 127, 1), shift(y_prev, 1, 1)
    z_up, z_down = shift(z_next, LZ - 1, 0), shift(z_prev, 1, 0)

    for t in range(TILES):
        s, z = t // LZ, t % LZ
        got = values[pl.ds(place[t], TILE), :]
        cond[s, pl.ds(z, TILE, stride=8), :] = jnp.where(row < lengths[s, z], jnp.exp(got), AIR)

    def split(a, b):
        return jnp.where(low, a, half(b)), jnp.where(low, half(a), b)

    def tile(k):
        return pl.ds(k * 128, 128)

    for k in range(TILE // 2):
        for s in range(S_DEV):
            pair = split(*[cond[s, pl.ds((k + d) * 8, 8), :] for d in (0, TILE // 2)])
            ws = [0.5 / (4.0 + c) for c in pair]
            for i in range(2):
                weight[s, 2 * k + i] = ws[i]
            for a in range(3):
                pair = split(source[s, a, :, tile(k)], source[s, a, :, tile(k + TILE // 2)])
                for i in range(2):
                    b = ws[i] * pair[i]
                    rhs[s, a, 2 * k + i] = b
                    first[s, a, 2 * k + i] = b

    def curl(e, e_x):
        ex, ey, ez = e
        hx = (y_up(ez) - ez) - (z_up(ey) - ey)
        hy = (z_up(ex) - ex) - (e_x[2] - ez)
        hz = (e_x[1] - ey) - (y_up(ex) - ex)
        return hx, hy, hz

    def sweep(src, dst):
        before = []
        for s in range(S_DEV):
            ends = [jnp.where(low, half(src[s, a, 0]), 0.0) for a in range(3)]
            for a in range(1, 3):
                src[s, a, TILE] = ends[a]
            _, hy, hz = curl([src[s, a, TILE - 1] for a in range(3)], ends)
            before.append(tuple(jnp.where(low, 0.0, half(v))[None] for v in (hy, hz)))

        def body(b, carry):
            at = pl.ds(b * BATCH, BATCH)
            lasts = []
            for s in range(S_DEV):
                e = [src[s, a, at] for a in range(3)]
                after = pl.ds(b * BATCH + BATCH, 1)
                e_x = [None] + [jnp.concatenate([e[a][1:], src[s, a, after]], 0) for a in (1, 2)]
                hx, hy, hz = curl(e, e_x)
                hy_x = jnp.concatenate([carry[s][0], hy[:-1]], 0)
                hz_x = jnp.concatenate([carry[s][1], hz[:-1]], 0)
                back = (
                    (z_down(hy) - hy) - (y_down(hz) - hz),
                    (hz_x - hz) - (z_down(hx) - hx),
                    (y_down(hx) - hx) - (hy_x - hy),
                )
                w = weight[s, at]
                keep = 0.5 + 4.0 * w
                for a in range(3):
                    dst[s, a, at] = keep * e[a] + (rhs[s, a, at] - w * back[a])
                lasts.append((hy[-1:], hz[-1:]))
            return tuple(lasts)

        lax.fori_loop(0, TILE // BATCH, body, tuple(before), unroll=4)

    sweep(first, second)
    sweep(second, first)
    sweep(first, second)

    for k in range(TILE // 2):
        for s in range(S_DEV):
            for a in range(3):
                pair = split(observed[s, a, :, tile(k)], observed[s, a, :, tile(k + TILE // 2)])
                for i in range(2):
                    b = weight[s, 2 * k + i] * (second[s, a, 2 * k + i] - pair[i])
                    rhs[s, a, 2 * k + i] = b
                    first[s, a, 2 * k + i] = b

    sweep(first, third)
    sweep(third, first)
    sweep(first, third)

    for k in range(TILE // 2):
        for s in range(S_DEV):
            p, q = (
                sum(second[s, a, 2 * k + i] * third[s, a, 2 * k + i] for a in range(3)) for i in range(2)
            )
            for d, v in ((0, jnp.where(low, p, half(q))), (TILE // 2, jnp.where(low, half(p), q))):
                at = pl.ds((k + d) * 8, 8)
                part[s, at, :] = -cond[s, at, :] * v

    for t in range(TILES):
        s, z = t // LZ, t % LZ
        got = part[s, pl.ds(z, TILE, stride=8), :]
        by_layer[pl.ds(t * TILE, TILE), :] = jnp.where(row < lengths[s, z], got, 0.0)
    by_layer[pl.ds(TILES * TILE, TILE), :] = jnp.zeros((TILE, 128), jnp.float32)


def front_kernel(
    place,
    holds,
    request,
    lengths,
    block_hbm,
    source_hbm,
    observed_hbm,
    arrived,
    starts,
    smooth,
    block,
    source,
    observed,
    values,
    outbox,
    slots,
    by_layer,
    *rest,
):
    fields, (load_sem, ask_send, ask_recv, row_send, row_recv, send, recv, core_send, core_recv, core_sem) = (
        rest[:7],
        rest[7:],
    )
    me = lax.axis_index("mdl")
    barrier = pltpu.get_barrier_semaphore()
    greeted = [partner(*d)[0] for d in FAR_FIRST] + [other_core()]
    for i in greeted:
        pl.semaphore_signal(barrier, inc=1, device_id=i, device_id_type=MESH)
    pairs = ((block_hbm, block), (source_hbm, source), (observed_hbm, observed))
    loads = [pltpu.make_async_copy(a, b, load_sem.at[i]) for i, (a, b) in enumerate(pairs)]
    for copy in loads:
        copy.start()
    pl.semaphore_wait(barrier, len(greeted))

    asks, answers = {}, {}
    for dh, dx in FAR_FIRST:
        to, m = partner(dh, dx)
        k = dh * NX + dx
        asks[dh, dx] = remote(request.at[m], starts.at[0, me], ask_send.at[k], ask_recv.at[k], to)
        asks[dh, dx].start()
    for k in range(CAP):
        starts[0, me, k] = request[me, k]
    loads[0].wait()
    for dh, dx in FAR_FIRST:
        back = (-dh % 2, -dx % NX)
        asks[back].wait_recv()
        to, m = partner(dh, dx)
        k = dh * NX + dx
        for i in range(CAP):
            outbox[k, pl.ds(i * TILE, TILE), :] = block[pl.ds(starts[0, m, i], TILE), :]
        answers[dh, dx] = remote(
            outbox.at[k], values.at[pl.ds(me * SLOT_ROWS, SLOT_ROWS)], row_send.at[k], row_recv.at[k], to
        )
        answers[dh, dx].start()
    pass_on = remote(starts.at[0], starts.at[1], core_sem.at[0], core_sem.at[1], other_core())
    pass_on.start()
    for k in range(CAP):
        at = pl.ds(me * SLOT_ROWS + k * TILE, TILE)
        values[at, :] = block[pl.ds(starts[0, me, k], TILE), :]
    mine = block[pl.ds(lax.axis_index("grp") * SHARE, SHARE), :]
    lane = lax.broadcasted_iota(jnp.int32, (SHARE, 128), 1)
    left = jnp.where(lane == 0, mine, pltpu.roll(mine, 1, 1))
    right = jnp.where(lane == 127, mine, pltpu.roll(mine, 127, 1))
    smooth[...] = BETA * (2.0 * mine - left - right)
    for copy in loads[1:]:
        copy.wait()
    for d in FAR_FIRST:
        answers[d].wait_recv()

    solve(place, lengths, values, source, observed, by_layer, *fields)

    def fill(m):
        for k in range(CAP):
            slots[m, pl.ds(k * TILE, TILE), :] = by_layer[pl.ds(holds[m * CAP + k], TILE), :]

    copies, forwards = {}, []
    for dh, dx in FAR_FIRST:
        to, m = partner(dh, dx)
        k = dh * NX + dx
        fill(m)
        copies[dh, dx] = remote(slots.at[m], arrived.at[0, me], send.at[k], recv.at[k], to)
        copies[dh, dx].start()
    fill(me)
    own = pltpu.make_async_copy(slots.at[me], arrived.at[0, me], load_sem.at[0])
    own.start()
    forwards.append(remote(slots.at[me], arrived.at[1, me], core_send.at[0], core_recv.at[0], other_core()))
    forwards[0].start()
    for dh, dx in FAR_FIRST[::-1]:
        _, m = partner(dh, dx)
        back = (-dh % 2, -dx % NX)
        copies[back].wait_recv()
        k = dh * NX + dx
        forwards.append(
            remote(arrived.at[0, m], arrived.at[1, m], core_send.at[k], core_recv.at[k], other_core())
        )
        forwards[-1].start()
    for d in FAR_FIRST:
        asks[d].wait_send()
        answers[d].wait_send()
        copies[d].wait_send()
    for copy in [own, pass_on] + forwards:
        copy.wait()


def add_kernel(starts, arrived, smooth, total):
    total[...] = jnp.zeros_like(total)
    at = pl.ds(pl.multiple_of(lax.axis_index("grp") * SHARE, SHARE), SHARE)
    total[at, :] = smooth[...]
    for side in range(2):
        for m in range(OWN):
            for k in range(CAP):
                at = pl.ds(starts[side, m, k], TILE)
                total[at, :] += arrived[side, m, pl.ds(k * TILE, TILE), :]


CUT = SHARE // 2
Z_ORDER = [4, 3, 5, 2, 6, 1, 7]


def reduce_kernel(total, out, z_box, y_box, z_sum, y_sum, zy_box, yz_box, z_sem, y_sem, zy_sem, yz_sem):
    z, y, c, h, x = here()
    m = lax.axis_index("mdl")

    def chip(dz, dy):
        return ((((z + dz) % NZ) * NY + (y + dy) % NY) * 2 + c, m)

    def send(src, dst, sem, i, to):
        copy = remote(src, dst, sem.at[0, i], sem.at[1, i], to)
        copy.start()
        return copy

    meet([chip(d, 0) for d in Z_ORDER] + [chip(0, d) for d in range(1, NY)])
    low, high = pl.ds(0, CUT), pl.ds(CUT, SHARE - CUT)
    along_z, along_y, then_y, then_z = {}, {}, {}, {}
    for i, d in enumerate(Z_ORDER):
        if i < NY - 1:
            e = i + 1
            along_y[e] = send(total.at[:, (y + e) % NY, c, high, :], y_box.at[e - 1], y_sem, e - 1, chip(0, e))
        along_z[d] = send(total.at[(z + d) % NZ, :, c, low, :], z_box.at[d - 1], z_sem, d - 1, chip(d, 0))
    for copy in along_y.values():
        copy.wait_recv()
    for d in Z_ORDER + [0]:
        j = (z + d) % NZ
        y_sum[d] = total[j, y, c, high, :] + sum(y_box[k, j] for k in range(NY - 1))
        if d:
            then_z[d] = send(y_sum.at[d], yz_box.at[d - 1], yz_sem, d - 1, chip(d, 0))
    for copy in along_z.values():
        copy.wait_recv()
    for d in (2, 1, 3, 0):
        j = (y + d) % NY
        z_sum[d] = total[z, j, c, low, :] + sum(z_box[k, j] for k in range(NZ - 1))
        if d:
            then_y[d] = send(z_sum.at[d], zy_box.at[d - 1], zy_sem, d - 1, chip(0, d))
    for copy in then_z.values():
        copy.wait()
    out[high, :] = y_sum[0] + sum(yz_box[k] for k in range(NZ - 1))
    for copy in then_y.values():
        copy.wait()
    out[low, :] = z_sum[0] + sum(zy_box[k] for k in range(NY - 1))
    for copy in list(along_z.values()) + list(along_y.values()):
        copy.wait_send()


def per_device(model, source, observed, owner_ids, offsets, lengths):
    block = model.reshape(ROWS, 128)
    f32, i32 = jnp.float32, jnp.int32
    dma = pltpu.SemaphoreType.DMA
    place, holds, request = pl.pallas_call(
        tables_kernel,
        out_shape=(
            jax.ShapeDtypeStruct((TILES,), i32),
            jax.ShapeDtypeStruct((OWN * CAP,), i32),
            jax.ShapeDtypeStruct((OWN, 128), i32),
        ),
        in_specs=[SMEM, SMEM],
        out_specs=(SMEM, SMEM, SMEM),
        scratch_shapes=[pltpu.SMEM((OWN,), i32)],
        name="tables",
    )(owner_ids.transpose(0, 2, 1), offsets)
    fields = pltpu.VMEM((S_DEV, 3, TILE + 1, 8, 128), f32)
    plain = pltpu.VMEM((S_DEV, TILE * 8, 128), f32)
    arrived, starts, smooth = pl.pallas_call(
        front_kernel,
        out_shape=(
            jax.ShapeDtypeStruct((2, OWN, SLOT_ROWS, 128), f32),
            jax.ShapeDtypeStruct((2, OWN, 128), i32),
            jax.ShapeDtypeStruct((SHARE, 128), f32),
        ),
        in_specs=[SMEM, SMEM, SMEM, SMEM, HBM, HBM, HBM],
        out_specs=(HBM, SMEM, VMEM),
        scratch_shapes=[
            pltpu.VMEM((ROWS, 128), f32),
            pltpu.VMEM((S_DEV, 3, LZ, TILE * 128), f32),
            pltpu.VMEM((S_DEV, 3, LZ, TILE * 128), f32),
            pltpu.VMEM((OWN * SLOT_ROWS, 128), f32),
            pltpu.VMEM((OWN, SLOT_ROWS, 128), f32),
            pltpu.VMEM((OWN, SLOT_ROWS, 128), f32),
            pltpu.VMEM(((TILES + 1) * TILE, 128), f32),
            plain,
            pltpu.VMEM((S_DEV, TILE, 8, 128), f32),
            fields,
            fields,
            fields,
            pltpu.VMEM((S_DEV, 3, TILE, 8, 128), f32),
            plain,
            dma((3,)),
        ]
        + [dma((OWN,))] * 8
        + [dma((2,))],
        compiler_params=pltpu.CompilerParams(
            collective_id=0, has_side_effects=True, vmem_limit_bytes=60 << 20
        ),
        name="front",
    )(place, holds, request, lengths, block, source, observed)
    total = pl.pallas_call(
        add_kernel,
        out_shape=jax.ShapeDtypeStruct((ROWS, 128), f32),
        in_specs=[SMEM, VMEM, VMEM],
        out_specs=VMEM,
        compiler_params=pltpu.CompilerParams(vmem_limit_bytes=32 << 20),
        name="add",
    )(starts, arrived, smooth)
    gradient = pl.pallas_call(
        reduce_kernel,
        out_shape=jax.ShapeDtypeStruct((SHARE, 128), f32),
        in_specs=[VMEM],
        out_specs=VMEM,
        scratch_shapes=[
            pltpu.VMEM((NZ - 1, NY, CUT, 128), f32),
            pltpu.VMEM((NY - 1, NZ, SHARE - CUT, 128), f32),
            pltpu.VMEM((NY, CUT, 128), f32),
            pltpu.VMEM((NZ, SHARE - CUT, 128), f32),
            pltpu.VMEM((NY - 1, CUT, 128), f32),
            pltpu.VMEM((NZ - 1, SHARE - CUT, 128), f32),
            dma((2, NZ - 1)),
            dma((2, NY - 1)),
            dma((2, NY - 1)),
            dma((2, NZ - 1)),
        ],
        compiler_params=pltpu.CompilerParams(
            collective_id=2, has_side_effects=True, vmem_limit_bytes=32 << 20
        ),
        name="reduce",
    )(total.reshape(NZ, NY, 2, SHARE, 128))
    return gradient[:, None, :]


def solution(mesh):
    placed = (
        P(None, "mdl", None),
        P(("grp", "mdl"), None, None, None),
        P(("grp", "mdl"), None, None, None),
        P(("grp", "mdl"), None, None),
        P(("grp", "mdl"), None),
        P(("grp", "mdl"), None),
    )
    return jax.shard_map(
        per_device, mesh=mesh, in_specs=placed, out_specs=P("grp", "mdl", None), check_vma=False
    )
```

```python
import functools

import jax
import jax.numpy as jnp
from jax import lax
from jax.experimental import pallas as pl
from jax.experimental.pallas import tpu as pltpu
from jax.sharding import PartitionSpec as P

LZ = 8
S_DEV = 2
TILES = S_DEV * LZ
TILE = 32
ROWS = 4096
CAP = 4
AIR = 0.05
BETA = 0.5

NZ, NY, NX = 8, 4, 4
OWN = 2 * NX
SLOT_ROWS = CAP * TILE
SHARE = ROWS // (NZ * NY * 2)

MESH = pl.DeviceIdType.MESH
SMEM = pl.BlockSpec(memory_space=pltpu.SMEM)
VMEM = pl.BlockSpec(memory_space=pltpu.VMEM)
HBM = pl.BlockSpec(memory_space=pl.ANY)
FAR_FIRST = [(1, 2), (1, 1), (1, 3), (1, 0), (0, 2), (0, 1), (0, 3)]


def here():
    g, m = lax.axis_index("grp"), lax.axis_index("mdl")
    return g // (2 * NY), (g // 2) % NY, g % 2, m // NX, m % NX


def partner(dh, dx):
    z, y, c, h, x = here()
    y = NY - 1 - y if dh % 2 else y
    m = ((h + dh) % 2) * NX + (x + dx) % NX
    return ((z * NY + y) * 2 + c, m), m


def other_core():
    z, y, c, h, x = here()
    return ((z * NY + y) * 2 + 1 - c, h * NX + x)


def meet(ids):
    barrier = pltpu.get_barrier_semaphore()
    for i in ids:
        pl.semaphore_signal(barrier, inc=1, device_id=i, device_id_type=MESH)
    pl.semaphore_wait(barrier, len(ids))


def remote(src, dst, send, recv, to):
    return pltpu.make_async_remote_copy(
        src_ref=src, dst_ref=dst, send_sem=send, recv_sem=recv, device_id=to, device_id_type=MESH
    )


def tables_kernel(owner, offset, place, holds, request, counts):
    for o in range(OWN):
        counts[o] = 0
        for k in range(CAP):
            request[o, k] = 0
            holds[o * CAP + k] = TILES * TILE
    for t in range(TILES):
        o = owner[t // LZ, 0, t % LZ]
        k = counts[o]
        counts[o] = k + 1
        place[t] = (o * CAP + k) * TILE
        holds[o * CAP + k] = t * TILE
        request[o, k] = offset[t // LZ, t % LZ]


BATCH = 4


def solve(place, lengths, values, source, observed, by_layer, cond, weight, first, second, third, rhs, part):
    lane = lax.broadcasted_iota(jnp.int32, (8, 128), 1)
    layer = lax.broadcasted_iota(jnp.int32, (8, 128), 0)
    low = lane < 64
    y_next, y_prev = lane % 64 != 63, lane % 64 != 0
    z_next, z_prev = layer != LZ - 1, layer != 0
    row = lax.broadcasted_iota(jnp.int32, (TILE, 128), 0)

    def half(v):
        return pltpu.roll(v, 64, 1)

    def shift(mask, by, axis):
        def one(v):
            return jnp.where(mask, pltpu.roll(v, by, axis), 0.0)

        return lambda v: one(v) if v.ndim == 2 else jnp.stack([one(v[i]) for i in range(v.shape[0])])

    y_up, y_down = shift(y_next, 127, 1), shift(y_prev, 1, 1)
    z_up, z_down = shift(z_next, LZ - 1, 0), shift(z_prev, 1, 0)

    for t in range(TILES):
        s, z = t // LZ, t % LZ
        got = values[pl.ds(place[t], TILE), :]
        cond[s, pl.ds(z, TILE, stride=8), :] = jnp.where(row < lengths[s, z], jnp.exp(got), AIR)

    def split(a, b):
        return jnp.where(low, a, half(b)), jnp.where(low, half(a), b)

    def tile(k):
        return pl.ds(k * 128, 128)

    for k in range(TILE // 2):
        for s in range(S_DEV):
            pair = split(*[cond[s, pl.ds((k + d) * 8, 8), :] for d in (0, TILE // 2)])
            ws = [0.5 / (4.0 + c) for c in pair]
            for i in range(2):
                weight[s, 2 * k + i] = ws[i]
            for a in range(3):
                pair = split(source[s, a, :, tile(k)], source[s, a, :, tile(k + TILE // 2)])
                for i in range(2):
                    b = ws[i] * pair[i]
                    rhs[s, a, 2 * k + i] = b
                    first[s, a, 2 * k + i] = b

    def curl(e, e_x):
        ex, ey, ez = e
        hx = (y_up(ez) - ez) - (z_up(ey) - ey)
        hy = (z_up(ex) - ex) - (e_x[2] - ez)
        hz = (e_x[1] - ey) - (y_up(ex) - ex)
        return hx, hy, hz

    def sweep(src, dst):
        before = []
        for s in range(S_DEV):
            ends = [jnp.where(low, half(src[s, a, 0]), 0.0) for a in range(3)]
            for a in range(1, 3):
                src[s, a, TILE] = ends[a]
            _, hy, hz = curl([src[s, a, TILE - 1] for a in range(3)], ends)
            before.append(tuple(jnp.where(low, 0.0, half(v))[None] for v in (hy, hz)))

        def body(b, carry):
            at = pl.ds(b * BATCH, BATCH)
            lasts = []
            for s in range(S_DEV):
                e = [src[s, a, at] for a in range(3)]
                after = pl.ds(b * BATCH + BATCH, 1)
                e_x = [None] + [jnp.concatenate([e[a][1:], src[s, a, after]], 0) for a in (1, 2)]
                hx, hy, hz = curl(e, e_x)
                hy_x = jnp.concatenate([carry[s][0], hy[:-1]], 0)
                hz_x = jnp.concatenate([carry[s][1], hz[:-1]], 0)
                back = (
                    (z_down(hy) - hy) - (y_down(hz) - hz),
                    (hz_x - hz) - (z_down(hx) - hx),
                    (y_down(hx) - hx) - (hy_x - hy),
                )
                w = weight[s, at]
                keep = 0.5 + 4.0 * w
                for a in range(3):
                    dst[s, a, at] = keep * e[a] + (rhs[s, a, at] - w * back[a])
                lasts.append((hy[-1:], hz[-1:]))
            return tuple(lasts)

        lax.fori_loop(0, TILE // BATCH, body, tuple(before), unroll=4)

    sweep(first, second)
    sweep(second, first)
    sweep(first, second)

    for k in range(TILE // 2):
        for s in range(S_DEV):
            for a in range(3):
                pair = split(observed[s, a, :, tile(k)], observed[s, a, :, tile(k + TILE // 2)])
                for i in range(2):
                    b = weight[s, 2 * k + i] * (second[s, a, 2 * k + i] - pair[i])
                    rhs[s, a, 2 * k + i] = b
                    first[s, a, 2 * k + i] = b

    sweep(first, third)
    sweep(third, first)
    sweep(first, third)

    for k in range(TILE // 2):
        for s in range(S_DEV):
            p, q = (
                sum(second[s, a, 2 * k + i] * third[s, a, 2 * k + i] for a in range(3)) for i in range(2)
            )
            for d, v in ((0, jnp.where(low, p, half(q))), (TILE // 2, jnp.where(low, half(p), q))):
                at = pl.ds((k + d) * 8, 8)
                part[s, at, :] = -cond[s, at, :] * v

    for t in range(TILES):
        s, z = t // LZ, t % LZ
        got = part[s, pl.ds(z, TILE, stride=8), :]
        by_layer[pl.ds(t * TILE, TILE), :] = jnp.where(row < lengths[s, z], got, 0.0)
    by_layer[pl.ds(TILES * TILE, TILE), :] = jnp.zeros((TILE, 128), jnp.float32)


NEAR = [(0, 0)] + [d for d in FAR_FIRST if d[0] == 0]
FAR = [d for d in FAR_FIRST if d[0] == 1]
OWN_ROWS = NY * SHARE
BLOCKS = 2 * NX


def targets(starts, arrived, vals, senders):
    lane = lax.broadcasted_iota(jnp.int32, (8, 128), 1)
    found = []
    for i, (side, m) in enumerate([(side, m) for m in senders for side in range(2)]):
        v = arrived[side, m]
        head = v.astype(jnp.bfloat16)
        at = pl.ds(i * SLOT_ROWS, SLOT_ROWS)
        vals[at, pl.ds(0, 128)] = head
        vals[at, pl.ds(128, 128)] = (v - head.astype(jnp.float32)).astype(jnp.bfloat16)
        s = [starts[side, m, k] for k in range(CAP)]
        t = jnp.where(lane < 2 * TILE, jnp.where(lane < TILE, s[0], s[1]), jnp.where(lane < 3 * TILE, s[2], s[3]))
        found.append(t + lane % TILE)
    return found


def placed_rows(found, vals, rows, j):
    picked = [
        jnp.where(rows == (t - j * (2 * OWN_ROWS))[None], 1.0, 0.0).astype(jnp.bfloat16).reshape(OWN_ROWS, 128)
        for t in found
    ]
    d = jnp.dot(jnp.concatenate(picked, 1), vals[...], preferred_element_type=jnp.float32)
    return (d[:, :128] + d[:, 128:]).reshape(NY, SHARE, 128)


CUT = SHARE // 2
Z_ORDER = [4, 3, 5, 2, 6, 1, 7]


def whole_kernel(
    place,
    holds,
    request,
    lengths,
    block_hbm,
    source_hbm,
    observed_hbm,
    out,
    starts,
    arrived,
    smooth,
    block,
    source,
    observed,
    values,
    outbox,
    slots,
    by_layer,
    vals,
    dense,
    *rest,
):
    fields, boxes, sems = rest[:7], rest[7:13], rest[13:]
    z_box, y_box, z_sum, y_sum, zy_box, yz_box = boxes
    (load_sem, ask_send, ask_recv, row_send, row_recv, send, recv, core_send, core_recv, core_sem) = sems[:10]
    z_sem, y_sem, zy_sem, yz_sem = sems[10:]
    z, y, c, h, x = here()
    me = lax.axis_index("mdl")

    def chip(dz, dy):
        return ((((z + dz) % NZ) * NY + (y + dy) % NY) * 2 + c, me)

    barrier = pltpu.get_barrier_semaphore()
    greeted = [partner(*d)[0] for d in FAR_FIRST] + [other_core()]
    greeted += [chip(d, 0) for d in Z_ORDER] + [chip(0, d) for d in range(1, NY)]
    for i in greeted:
        pl.semaphore_signal(barrier, inc=1, device_id=i, device_id_type=MESH)
    pairs = ((block_hbm, block), (source_hbm, source), (observed_hbm, observed))
    loads = [pltpu.make_async_copy(a, b, load_sem.at[i]) for i, (a, b) in enumerate(pairs)]
    for copy in loads:
        copy.start()
    pl.semaphore_wait(barrier, len(greeted))

    asks, answers = {}, {}
    for dh, dx in FAR_FIRST:
        to, m = partner(dh, dx)
        k = dh * NX + dx
        asks[dh, dx] = remote(request.at[m], starts.at[0, me], ask_send.at[k], ask_recv.at[k], to)
        asks[dh, dx].start()
    for k in range(CAP):
        starts[0, me, k] = request[me, k]
    loads[0].wait()
    for dh, dx in FAR_FIRST:
        back = (-dh % 2, -dx % NX)
        asks[back].wait_recv()
        to, m = partner(dh, dx)
        k = dh * NX + dx
        for i in range(CAP):
            outbox[k, pl.ds(i * TILE, TILE), :] = block[pl.ds(starts[0, m, i], TILE), :]
        answers[dh, dx] = remote(
            outbox.at[k], values.at[pl.ds(me * SLOT_ROWS, SLOT_ROWS)], row_send.at[k], row_recv.at[k], to
        )
        answers[dh, dx].start()
    pass_on = remote(starts.at[0], starts.at[1], core_sem.at[0], core_sem.at[1], other_core())
    pass_on.start()
    for k in range(CAP):
        at = pl.ds(me * SLOT_ROWS + k * TILE, TILE)
        values[at, :] = block[pl.ds(starts[0, me, k], TILE), :]
    mine = block[pl.ds(lax.axis_index("grp") * SHARE, SHARE), :]
    lane = lax.broadcasted_iota(jnp.int32, (SHARE, 128), 1)
    left = jnp.where(lane == 0, mine, pltpu.roll(mine, 1, 1))
    right = jnp.where(lane == 127, mine, pltpu.roll(mine, 127, 1))
    smooth[...] = BETA * (2.0 * mine - left - right)
    for copy in loads[1:]:
        copy.wait()
    for d in FAR_FIRST:
        answers[d].wait_recv()

    solve(place, lengths, values, source, observed, by_layer, *fields)

    def fill(m, ref):
        for k in range(CAP):
            ref[m, pl.ds(k * TILE, TILE), :] = by_layer[pl.ds(holds[m * CAP + k], TILE), :]

    copies, forwards = {}, {}
    for dh, dx in FAR_FIRST:
        to, m = partner(dh, dx)
        k = dh * NX + dx
        fill(m, slots)
        copies[dh, dx] = remote(slots.at[m], arrived.at[0, me], send.at[k], recv.at[k], to)
        copies[dh, dx].start()
    fill(me, arrived.at[0])
    pass_on.wait()

    def take(steps):
        for dh, dx in steps:
            _, m = partner(dh, dx)
            if (dh, dx) != (0, 0):
                copies[-dh % 2, -dx % NX].wait_recv()
            k = dh * NX + dx
            forwards[dh, dx] = remote(
                arrived.at[0, m], arrived.at[1, m], core_send.at[k], core_recv.at[k], other_core()
            )
            forwards[dh, dx].start()
        for d in steps:
            forwards[d].wait_recv()
        return [partner(*d)[1] for d in steps]

    shape = (OWN_ROWS // 8, 8, 128)
    at = lax.broadcasted_iota(jnp.int32, shape, 0) * 8 + lax.broadcasted_iota(jnp.int32, shape, 1)
    rows = (at // SHARE) * (2 * SHARE) + at % SHARE + c * SHARE
    found = targets(starts, arrived, vals, take(NEAR))

    def near(j, carry):
        dense[j] = placed_rows(found, vals, rows, j)
        return carry

    lax.fori_loop(0, NZ, near, 0, unroll=4)
    found_far = targets(starts, arrived, vals, take(FAR))

    def push(src, dst, sem, i, to):
        copy = remote(src, dst, sem.at[0, i], sem.at[1, i], to)
        copy.start()
        return copy

    low, high = pl.ds(0, CUT), pl.ds(CUT, SHARE - CUT)
    along_z, along_y, then_y, then_z = {}, {}, {}, {}
    for d in Z_ORDER + [0]:
        j = (z + d) % NZ
        dense[j] = dense[j] + placed_rows(found_far, vals, rows, j)
        if d:
            along_z[d] = push(dense.at[j, :, low, :], z_box.at[d - 1], z_sem, d - 1, chip(d, 0))
    for d in (2, 1, 3):
        along_y[d] = push(dense.at[:, (y + d) % NY, high, :], y_box.at[d - 1], y_sem, d - 1, chip(0, d))
    for copy in along_y.values():
        copy.wait_recv()
    for d in Z_ORDER + [0]:
        j = (z + d) % NZ
        y_sum[d] = dense[j, y, high, :] + sum(y_box[k, j] for k in range(NY - 1))
        if d:
            then_z[d] = push(y_sum.at[d], yz_box.at[d - 1], yz_sem, d - 1, chip(d, 0))
    for copy in along_z.values():
        copy.wait_recv()
    for d in (2, 1, 3, 0):
        j = (y + d) % NY
        z_sum[d] = dense[z, j, low, :] + sum(z_box[k, j] for k in range(NZ - 1))
        if d:
            then_y[d] = push(z_sum.at[d], zy_box.at[d - 1], zy_sem, d - 1, chip(0, d))
    for copy in then_z.values():
        copy.wait_recv()
    out[high, :] = smooth[high, :] + y_sum[0] + sum(yz_box[k] for k in range(NZ - 1))
    for copy in then_y.values():
        copy.wait_recv()
    out[low, :] = smooth[low, :] + z_sum[0] + sum(zy_box[k] for k in range(NY - 1))
    for sent in (asks, answers, copies, forwards, along_z, along_y, then_z, then_y):
        for copy in sent.values():
            copy.wait_send()


def per_device(model, source, observed, owner_ids, offsets, lengths):
    block = model.reshape(ROWS, 128)
    f32, i32 = jnp.float32, jnp.int32
    dma = pltpu.SemaphoreType.DMA
    place, holds, request = pl.pallas_call(
        tables_kernel,
        out_shape=(
            jax.ShapeDtypeStruct((TILES,), i32),
            jax.ShapeDtypeStruct((OWN * CAP,), i32),
            jax.ShapeDtypeStruct((OWN, 128), i32),
        ),
        in_specs=[SMEM, SMEM],
        out_specs=(SMEM, SMEM, SMEM),
        scratch_shapes=[pltpu.SMEM((OWN,), i32)],
        name="tables",
    )(owner_ids.transpose(0, 2, 1), offsets)
    fields = pltpu.VMEM((S_DEV, 3, TILE + 1, 8, 128), f32)
    plain = pltpu.VMEM((S_DEV, TILE * 8, 128), f32)
    gradient = pl.pallas_call(
        whole_kernel,
        out_shape=jax.ShapeDtypeStruct((SHARE, 128), f32),
        in_specs=[SMEM, SMEM, SMEM, SMEM, HBM, HBM, HBM],
        out_specs=VMEM,
        scratch_shapes=[
            pltpu.SMEM((2, OWN, 128), i32),
            pltpu.VMEM((2, OWN, SLOT_ROWS, 128), f32),
            pltpu.VMEM((SHARE, 128), f32),
            pltpu.VMEM((ROWS, 128), f32),
            pltpu.VMEM((S_DEV, 3, LZ, TILE * 128), f32),
            pltpu.VMEM((S_DEV, 3, LZ, TILE * 128), f32),
            pltpu.VMEM((OWN * SLOT_ROWS, 128), f32),
            pltpu.VMEM((OWN, SLOT_ROWS, 128), f32),
            pltpu.VMEM((OWN, SLOT_ROWS, 128), f32),
            pltpu.VMEM(((TILES + 1) * TILE, 128), f32),
            pltpu.VMEM((BLOCKS * SLOT_ROWS, 256), jnp.bfloat16),
            pltpu.VMEM((NZ, NY, SHARE, 128), f32),
            plain,
            pltpu.VMEM((S_DEV, TILE, 8, 128), f32),
            fields,
            fields,
            fields,
            pltpu.VMEM((S_DEV, 3, TILE, 8, 128), f32),
            plain,
            pltpu.VMEM((NZ - 1, NY, CUT, 128), f32),
            pltpu.VMEM((NY - 1, NZ, SHARE - CUT, 128), f32),
            pltpu.VMEM((NY, CUT, 128), f32),
            pltpu.VMEM((NZ, SHARE - CUT, 128), f32),
            pltpu.VMEM((NY - 1, CUT, 128), f32),
            pltpu.VMEM((NZ - 1, SHARE - CUT, 128), f32),
            dma((3,)),
        ]
        + [dma((OWN,))] * 8
        + [dma((2,)), dma((2, NZ - 1)), dma((2, NY - 1)), dma((2, NY - 1)), dma((2, NZ - 1))],
        compiler_params=pltpu.CompilerParams(
            collective_id=0, has_side_effects=True, vmem_limit_bytes=60 << 20
        ),
        name="whole",
    )(place, holds, request, lengths, block, source, observed)
    return gradient[:, None, :]


def solution(mesh):
    placed = (
        P(None, "mdl", None),
        P(("grp", "mdl"), None, None, None),
        P(("grp", "mdl"), None, None, None),
        P(("grp", "mdl"), None, None),
        P(("grp", "mdl"), None),
        P(("grp", "mdl"), None),
    )
    return jax.shard_map(
        per_device, mesh=mesh, in_specs=placed, out_specs=P("grp", "mdl", None), check_vma=False
    )
```

```python
import functools

import jax
import jax.numpy as jnp
from jax import lax
from jax.experimental import pallas as pl
from jax.experimental.pallas import tpu as pltpu
from jax.sharding import PartitionSpec as P

LZ = 8
S_DEV = 2
TILES = S_DEV * LZ
TILE = 32
ROWS = 4096
CAP = 4
AIR = 0.05
BETA = 0.5

NZ, NY, NX = 8, 4, 4
OWN = 2 * NX
SLOT_ROWS = CAP * TILE
SHARE = ROWS // (NZ * NY * 2)

MESH = pl.DeviceIdType.MESH
SMEM = pl.BlockSpec(memory_space=pltpu.SMEM)
VMEM = pl.BlockSpec(memory_space=pltpu.VMEM)
HBM = pl.BlockSpec(memory_space=pl.ANY)
FAR_FIRST = [(1, 2), (1, 1), (1, 3), (1, 0), (0, 2), (0, 1), (0, 3)]


def here():
    g, m = lax.axis_index("grp"), lax.axis_index("mdl")
    return g // (2 * NY), (g // 2) % NY, g % 2, m // NX, m % NX


def partner(dh, dx):
    z, y, c, h, x = here()
    y = NY - 1 - y if dh % 2 else y
    m = ((h + dh) % 2) * NX + (x + dx) % NX
    return ((z * NY + y) * 2 + c, m), m


def other_core():
    z, y, c, h, x = here()
    return ((z * NY + y) * 2 + 1 - c, h * NX + x)


def meet(ids):
    barrier = pltpu.get_barrier_semaphore()
    for i in ids:
        pl.semaphore_signal(barrier, inc=1, device_id=i, device_id_type=MESH)
    pl.semaphore_wait(barrier, len(ids))


def remote(src, dst, send, recv, to):
    return pltpu.make_async_remote_copy(
        src_ref=src, dst_ref=dst, send_sem=send, recv_sem=recv, device_id=to, device_id_type=MESH
    )


HALF = TILE // 2


def half(v):
    return pltpu.roll(v, 64, 1)


def split(a, b):
    low = lax.broadcasted_iota(jnp.int32, (8, 128), 1) < 64
    return jnp.where(low, a, half(b)), jnp.where(low, half(a), b)


def arrange(source, observed, given):
    def one(k, carry):
        places = [pl.ds(pl.multiple_of((k + d) * 128, 128), 128) for d in (0, HALF)]
        for s in range(S_DEV):
            for a in range(3):
                p, q = split(*[source[s, a, :, at] for at in places])
                given[0, s, a, 2 * k] = -p
                given[0, s, a, 2 * k + 1] = -q
                p, q = split(*[observed[s, a, :, at] for at in places])
                given[1, s, a, 2 * k] = p
                given[1, s, a, 2 * k + 1] = q
        return carry

    lax.fori_loop(0, HALF, one, 0, unroll=4)


def solve(place, lengths, values, given, by_layer, cond, weight, keeps, state, rhs, part):
    lane = lax.broadcasted_iota(jnp.int32, (8, 128), 1)
    layer = lax.broadcasted_iota(jnp.int32, (8, 128), 0)
    row = lax.broadcasted_iota(jnp.int32, (TILE, 128), 0)
    low = lane < 64

    def shift(mask, by, axis):
        def all_of(v):
            return jnp.stack([jnp.where(mask, pltpu.roll(v[i], by, axis), 0.0) for i in range(v.shape[0])])

        return all_of

    y_up, y_down = shift(lane % 64 != 63, 127, 1), shift(lane % 64 != 0, 1, 1)
    z_up, z_down = shift(layer != LZ - 1, LZ - 1, 0), shift(layer != 0, 1, 0)

    for t in range(TILES):
        s, z = t // LZ, t % LZ
        got = values[pl.ds(place[t], TILE), :]
        cond[s, pl.ds(z, TILE, stride=8), :] = jnp.where(row < lengths[s, z], jnp.exp(got), AIR)

    for k in range(HALF):
        for s in range(S_DEV):
            pair = split(*[cond[s, pl.ds((k + d) * 8, 8), :] for d in (0, HALF)])
            for i in range(2):
                w = 0.5 / (4.0 + pair[i])
                weight[s, 2 * k + i] = w
                keeps[s, 2 * k + i] = 0.5 + 4.0 * w

    state[0] = jnp.zeros_like(state[0])

    def phase(p, carry):
        for r in range(TILE):
            for s in range(S_DEV):
                for a in range(3):
                    b = weight[s, r] * (state[p, s, a, r] - given[p, s, a, r])
                    rhs[s, a, r] = b
                    state[p + 1, s, a, r] = b

        def sweep(i, carry):
            for s in range(S_DEV):
                ex, ey, ez = e = [state[p + 1, s, a] for a in range(3)]
                ey_x, ez_x = (jnp.concatenate([v[1:], jnp.where(low, half(v[0]), 0.0)[None]], 0) for v in (ey, ez))
                hx = (y_up(ez) - ez) - (z_up(ey) - ey)
                hy = (z_up(ex) - ex) - (ez_x - ez)
                hz = (ey_x - ey) - (y_up(ex) - ex)
                hy_x, hz_x = (
                    jnp.concatenate([jnp.where(low, 0.0, half(v[TILE - 1]))[None], v[:-1]], 0) for v in (hy, hz)
                )
                back = (
                    (z_down(hy) - hy) - (y_down(hz) - hz),
                    (hz_x - hz) - (z_down(hx) - hx),
                    (y_down(hx) - hx) - (hy_x - hy),
                )
                w, keep = weight[s], keeps[s]
                for a in range(3):
                    state[p + 1, s, a] = keep * e[a] + (rhs[s, a] - w * back[a])
            return carry

        lax.fori_loop(0, 3, sweep, 0)
        return carry

    lax.fori_loop(0, 2, phase, 0)

    for k in range(HALF):
        for s in range(S_DEV):
            pair = [sum(state[1, s, a, 2 * k + i] * state[2, s, a, 2 * k + i] for a in range(3)) for i in range(2)]
            for d, v in zip((0, HALF), split(*pair)):
                at = pl.ds((k + d) * 8, 8)
                part[s, at, :] = -cond[s, at, :] * v

    for t in range(TILES):
        s, z = t // LZ, t % LZ
        got = part[s, pl.ds(z, TILE, stride=8), :]
        by_layer[pl.ds(t * TILE, TILE), :] = jnp.where(row < lengths[s, z], got, 0.0)
    by_layer[pl.ds(TILES * TILE, TILE), :] = jnp.zeros((TILE, 128), jnp.float32)


NEAR = [(0, 0)] + [d for d in FAR_FIRST if d[0] == 0]
FAR = [d for d in FAR_FIRST if d[0] == 1]
OWN_ROWS = NY * SHARE
BLOCKS = 2 * NX


def targets(starts, arrived, vals, senders):
    lane = lax.broadcasted_iota(jnp.int32, (8, 128), 1)
    found = []
    for i, (side, m) in enumerate([(side, m) for m in senders for side in range(2)]):
        v = arrived[side, m]
        head = v.astype(jnp.bfloat16)
        at = pl.ds(i * SLOT_ROWS, SLOT_ROWS)
        vals[at, pl.ds(0, 128)] = head
        vals[at, pl.ds(128, 128)] = (v - head.astype(jnp.float32)).astype(jnp.bfloat16)
        s = [starts[side, m, k] for k in range(CAP)]
        t = jnp.where(lane < 2 * TILE, jnp.where(lane < TILE, s[0], s[1]), jnp.where(lane < 3 * TILE, s[2], s[3]))
        found.append(t + lane % TILE)
    return found


def placed_rows(found, vals, rows, j):
    picked = [
        jnp.where(rows == (t - j * (2 * OWN_ROWS))[None], 1.0, 0.0).astype(jnp.bfloat16).reshape(OWN_ROWS, 128)
        for t in found
    ]
    d = jnp.dot(jnp.concatenate(picked, 1), vals[...], preferred_element_type=jnp.float32)
    return (d[:, :128] + d[:, 128:]).reshape(NY, SHARE, 128)


CUT = SHARE // 2
Z_ORDER = [4, 3, 5, 2, 6, 1, 7]


def whole_kernel(
    owner,
    offset,
    lengths,
    block_hbm,
    source_hbm,
    observed_hbm,
    out,
    place,
    holds,
    request,
    starts,
    arrived,
    smooth,
    given,
    block,
    source,
    observed,
    values,
    outbox,
    slots,
    by_layer,
    vals,
    dense,
    *rest,
):
    fields, boxes, sems = rest[:6], rest[6:12], rest[12:]
    z_box, y_box, z_sum, y_sum, zy_box, yz_box = boxes
    (load_sem, ask_send, ask_recv, row_send, row_recv, send, recv, core_send, core_recv, core_sem) = sems[:10]
    z_sem, y_sem, zy_sem, yz_sem = sems[10:]
    z, y, c, h, x = here()
    me = lax.axis_index("mdl")

    def chip(dz, dy):
        return ((((z + dz) % NZ) * NY + (y + dy) % NY) * 2 + c, me)

    barrier = pltpu.get_barrier_semaphore()
    greeted = [partner(*d)[0] for d in FAR_FIRST] + [other_core()]
    greeted += [chip(d, 0) for d in Z_ORDER] + [chip(0, d) for d in range(1, NY)]
    for i in greeted:
        pl.semaphore_signal(barrier, inc=1, device_id=i, device_id_type=MESH)
    pairs = ((block_hbm, block), (source_hbm, source), (observed_hbm, observed))
    loads = [pltpu.make_async_copy(a, b, load_sem.at[i]) for i, (a, b) in enumerate(pairs)]
    for copy in loads:
        copy.start()

    owners = [owner[t // LZ, 0, t % LZ] for t in range(TILES)]
    firsts = [offset[t // LZ, t % LZ] for t in range(TILES)]
    slot_of = []
    for t in range(TILES):
        slot = owners[t] * CAP
        for i in range(t):
            slot = jnp.where(owners[i] == owners[t], slot + 1, slot)
        slot_of.append(slot)
        place[t] = slot * TILE

    def table(j, carry):
        first, held = jnp.int32(0), jnp.int32(TILES * TILE)
        for t in range(TILES):
            first = jnp.where(slot_of[t] == j, firsts[t], first)
            held = jnp.where(slot_of[t] == j, t * TILE, held)
        request[j // CAP, j % CAP] = first
        holds[j] = held
        return carry

    lax.fori_loop(0, OWN * CAP, table, 0)
    pl.semaphore_wait(barrier, len(greeted))

    asks, answers = {}, {}
    for dh, dx in FAR_FIRST:
        to, m = partner(dh, dx)
        k = dh * NX + dx
        asks[dh, dx] = remote(request.at[m], starts.at[0, me], ask_send.at[k], ask_recv.at[k], to)
        asks[dh, dx].start()
    for k in range(CAP):
        starts[0, me, k] = request[me, k]
    loads[0].wait()
    for dh, dx in FAR_FIRST:
        back = (-dh % 2, -dx % NX)
        asks[back].wait_recv()
        to, m = partner(dh, dx)
        k = dh * NX + dx
        for i in range(CAP):
            outbox[k, pl.ds(i * TILE, TILE), :] = block[pl.ds(starts[0, m, i], TILE), :]
        answers[dh, dx] = remote(
            outbox.at[k], values.at[pl.ds(me * SLOT_ROWS, SLOT_ROWS)], row_send.at[k], row_recv.at[k], to
        )
        answers[dh, dx].start()
    pass_on = remote(starts.at[0], starts.at[1], core_sem.at[0], core_sem.at[1], other_core())
    pass_on.start()
    for k in range(CAP):
        at = pl.ds(me * SLOT_ROWS + k * TILE, TILE)
        values[at, :] = block[pl.ds(starts[0, me, k], TILE), :]
    mine = block[pl.ds(lax.axis_index("grp") * SHARE, SHARE), :]
    lane = lax.broadcasted_iota(jnp.int32, (SHARE, 128), 1)
    left = jnp.where(lane == 0, mine, pltpu.roll(mine, 1, 1))
    right = jnp.where(lane == 127, mine, pltpu.roll(mine, 127, 1))
    smooth[...] = BETA * (2.0 * mine - left - right)
    for copy in loads[1:]:
        copy.wait()
    arrange(source, observed, given)
    for d in FAR_FIRST:
        answers[d].wait_recv()

    solve(place, lengths, values, given, by_layer, *fields)

    def fill(m, ref):
        for k in range(CAP):
            ref[m, pl.ds(k * TILE, TILE), :] = by_layer[pl.ds(holds[m * CAP + k], TILE), :]

    copies, forwards = {}, {}
    for dh, dx in FAR_FIRST:
        to, m = partner(dh, dx)
        k = dh * NX + dx
        fill(m, slots)
        copies[dh, dx] = remote(slots.at[m], arrived.at[0, me], send.at[k], recv.at[k], to)
        copies[dh, dx].start()
    fill(me, arrived.at[0])
    pass_on.wait()

    def take(steps):
        for dh, dx in steps:
            _, m = partner(dh, dx)
            if (dh, dx) != (0, 0):
                copies[-dh % 2, -dx % NX].wait_recv()
            k = dh * NX + dx
            forwards[dh, dx] = remote(
                arrived.at[0, m], arrived.at[1, m], core_send.at[k], core_recv.at[k], other_core()
            )
            forwards[dh, dx].start()
        for d in steps:
            forwards[d].wait_recv()
        return [partner(*d)[1] for d in steps]

    shape = (OWN_ROWS // 8, 8, 128)
    at = lax.broadcasted_iota(jnp.int32, shape, 0) * 8 + lax.broadcasted_iota(jnp.int32, shape, 1)
    rows = (at // SHARE) * (2 * SHARE) + at % SHARE + c * SHARE
    found = targets(starts, arrived, vals, take(NEAR))

    def near(j, carry):
        dense[j] = placed_rows(found, vals, rows, j)
        return carry

    lax.fori_loop(0, NZ, near, 0, unroll=4)
    found_far = targets(starts, arrived, vals, take(FAR))

    def push(src, dst, sem, i, to):
        copy = remote(src, dst, sem.at[0, i], sem.at[1, i], to)
        copy.start()
        return copy

    low, high = pl.ds(0, CUT), pl.ds(CUT, SHARE - CUT)
    along_z, along_y, then_y, then_z = {}, {}, {}, {}
    for d in Z_ORDER + [0]:
        j = (z + d) % NZ
        dense[j] = dense[j] + placed_rows(found_far, vals, rows, j)
        if d:
            along_z[d] = push(dense.at[j, :, low, :], z_box.at[d - 1], z_sem, d - 1, chip(d, 0))
    for d in (2, 1, 3):
        along_y[d] = push(dense.at[:, (y + d) % NY, high, :], y_box.at[d - 1], y_sem, d - 1, chip(0, d))
    for copy in along_y.values():
        copy.wait_recv()
    for d in Z_ORDER + [0]:
        j = (z + d) % NZ
        y_sum[d] = dense[j, y, high, :] + sum(y_box[k, j] for k in range(NY - 1))
        if d:
            then_z[d] = push(y_sum.at[d], yz_box.at[d - 1], yz_sem, d - 1, chip(d, 0))
    for copy in along_z.values():
        copy.wait_recv()
    for d in (2, 1, 3, 0):
        j = (y + d) % NY
        z_sum[d] = dense[z, j, low, :] + sum(z_box[k, j] for k in range(NZ - 1))
        if d:
            then_y[d] = push(z_sum.at[d], zy_box.at[d - 1], zy_sem, d - 1, chip(0, d))
    for copy in then_z.values():
        copy.wait_recv()
    out[high, :] = smooth[high, :] + y_sum[0] + sum(yz_box[k] for k in range(NZ - 1))
    for copy in then_y.values():
        copy.wait_recv()
    out[low, :] = smooth[low, :] + z_sum[0] + sum(zy_box[k] for k in range(NY - 1))
    for sent in (asks, answers, copies, forwards, along_z, along_y, then_z, then_y):
        for copy in sent.values():
            copy.wait_send()


def per_device(model, source, observed, owner_ids, offsets, lengths):
    block = model.reshape(ROWS, 128)
    f32, i32 = jnp.float32, jnp.int32
    dma = pltpu.SemaphoreType.DMA
    field = (S_DEV, 3, TILE, 8, 128)
    plain = pltpu.VMEM((S_DEV, TILE * 8, 128), f32)
    gradient = pl.pallas_call(
        whole_kernel,
        out_shape=jax.ShapeDtypeStruct((SHARE, 128), f32),
        in_specs=[SMEM, SMEM, SMEM, HBM, HBM, HBM],
        out_specs=VMEM,
        scratch_shapes=[
            pltpu.SMEM((TILES,), i32),
            pltpu.SMEM((OWN * CAP,), i32),
            pltpu.SMEM((OWN, 128), i32),
            pltpu.SMEM((2, OWN, 128), i32),
            pltpu.VMEM((2, OWN, SLOT_ROWS, 128), f32),
            pltpu.VMEM((SHARE, 128), f32),
            pltpu.VMEM((2,) + field, f32),
            pltpu.VMEM((ROWS, 128), f32),
            pltpu.VMEM((S_DEV, 3, LZ, TILE * 128), f32),
            pltpu.VMEM((S_DEV, 3, LZ, TILE * 128), f32),
            pltpu.VMEM((OWN * SLOT_ROWS, 128), f32),
            pltpu.VMEM((OWN, SLOT_ROWS, 128), f32),
            pltpu.VMEM((OWN, SLOT_ROWS, 128), f32),
            pltpu.VMEM(((TILES + 1) * TILE, 128), f32),
            pltpu.VMEM((BLOCKS * SLOT_ROWS, 256), jnp.bfloat16),
            pltpu.VMEM((NZ, NY, SHARE, 128), f32),
            plain,
            pltpu.VMEM((S_DEV, TILE, 8, 128), f32),
            pltpu.VMEM((S_DEV, TILE, 8, 128), f32),
            pltpu.VMEM((3,) + field, f32),
            pltpu.VMEM(field, f32),
            plain,
            pltpu.VMEM((NZ - 1, NY, CUT, 128), f32),
            pltpu.VMEM((NY - 1, NZ, SHARE - CUT, 128), f32),
            pltpu.VMEM((NY, CUT, 128), f32),
            pltpu.VMEM((NZ, SHARE - CUT, 128), f32),
            pltpu.VMEM((NY - 1, CUT, 128), f32),
            pltpu.VMEM((NZ - 1, SHARE - CUT, 128), f32),
            dma((3,)),
        ]
        + [dma((OWN,))] * 8
        + [dma((2,)), dma((2, NZ - 1)), dma((2, NY - 1)), dma((2, NY - 1)), dma((2, NZ - 1))],
        compiler_params=pltpu.CompilerParams(
            collective_id=0, has_side_effects=True, vmem_limit_bytes=60 << 20
        ),
        name="whole",
    )(owner_ids.transpose(0, 2, 1), offsets, lengths, block, source, observed)
    return gradient[:, None, :]


def solution(mesh):
    placed = (
        P(None, "mdl", None),
        P(("grp", "mdl"), None, None, None),
        P(("grp", "mdl"), None, None, None),
        P(("grp", "mdl"), None, None),
        P(("grp", "mdl"), None),
        P(("grp", "mdl"), None),
    )
    return jax.shard_map(
        per_device, mesh=mesh, in_specs=placed, out_specs=P("grp", "mdl", None), check_vma=False
    )
```

```python
import functools

import jax
import jax.numpy as jnp
from jax import lax
from jax.experimental import pallas as pl
from jax.experimental.pallas import tpu as pltpu
from jax.sharding import PartitionSpec as P

LZ = 8
S_DEV = 2
TILES = S_DEV * LZ
TILE = 32
ROWS = 4096
CAP = 4
AIR = 0.05
BETA = 0.5

NZ, NY, NX = 8, 4, 4
OWN = 2 * NX
SLOT_ROWS = CAP * TILE
SHARE = ROWS // (NZ * NY * 2)

MESH = pl.DeviceIdType.MESH
SMEM = pl.BlockSpec(memory_space=pltpu.SMEM)
VMEM = pl.BlockSpec(memory_space=pltpu.VMEM)
HBM = pl.BlockSpec(memory_space=pl.ANY)
NEAR_FIRST = [(0, 2), (0, 1), (0, 3), (1, 2), (1, 1), (1, 3), (1, 0)]


def here():
    g, m = lax.axis_index("grp"), lax.axis_index("mdl")
    return g // (2 * NY), (g // 2) % NY, g % 2, m // NX, m % NX


def partner(dh, dx):
    z, y, c, h, x = here()
    y = NY - 1 - y if dh % 2 else y
    m = ((h + dh) % 2) * NX + (x + dx) % NX
    return ((z * NY + y) * 2 + c, m), m


def other_core():
    z, y, c, h, x = here()
    return ((z * NY + y) * 2 + 1 - c, h * NX + x)


def meet(ids):
    barrier = pltpu.get_barrier_semaphore()
    for i in ids:
        pl.semaphore_signal(barrier, inc=1, device_id=i, device_id_type=MESH)
    pl.semaphore_wait(barrier, len(ids))


def remote(src, dst, send, recv, to):
    return pltpu.make_async_remote_copy(
        src_ref=src, dst_ref=dst, send_sem=send, recv_sem=recv, device_id=to, device_id_type=MESH
    )


HALF = TILE // 2


def half(v):
    return pltpu.roll(v, 64, 1)


def split(a, b):
    low = lax.broadcasted_iota(jnp.int32, (8, 128), 1) < 64
    return jnp.where(low, a, half(b)), jnp.where(low, half(a), b)


def arrange(source, observed, given):
    def one(k, carry):
        places = [pl.ds(pl.multiple_of((k + d) * 128, 128), 128) for d in (0, HALF)]
        for s in range(S_DEV):
            for a in range(3):
                p, q = split(*[source[s, a, :, at] for at in places])
                given[0, s, a, 2 * k] = -p
                given[0, s, a, 2 * k + 1] = -q
                p, q = split(*[observed[s, a, :, at] for at in places])
                given[1, s, a, 2 * k] = p
                given[1, s, a, 2 * k + 1] = q
        return carry

    lax.fori_loop(0, HALF, one, 0, unroll=4)


def solve(place, lengths, values, given, by_layer, cond, weight, keeps, state, rhs, part):
    lane = lax.broadcasted_iota(jnp.int32, (8, 128), 1)
    layer = lax.broadcasted_iota(jnp.int32, (8, 128), 0)
    row = lax.broadcasted_iota(jnp.int32, (TILE, 128), 0)
    low = lane < 64

    def shift(mask, by, axis):
        def all_of(v):
            return jnp.stack([jnp.where(mask, pltpu.roll(v[i], by, axis), 0.0) for i in range(v.shape[0])])

        return all_of

    y_up, y_down = shift(lane % 64 != 63, 127, 1), shift(lane % 64 != 0, 1, 1)
    z_up, z_down = shift(layer != LZ - 1, LZ - 1, 0), shift(layer != 0, 1, 0)

    for t in range(TILES):
        s, z = t // LZ, t % LZ
        got = values[pl.ds(place[t], TILE), :]
        cond[s, pl.ds(z, TILE, stride=8), :] = jnp.where(row < lengths[s, z], jnp.exp(got), AIR)

    for k in range(HALF):
        for s in range(S_DEV):
            pair = split(*[cond[s, pl.ds((k + d) * 8, 8), :] for d in (0, HALF)])
            for i in range(2):
                w = 0.5 / (4.0 + pair[i])
                weight[s, 2 * k + i] = w
                keeps[s, 2 * k + i] = 0.5 + 4.0 * w

    state[0] = jnp.zeros_like(state[0])

    def phase(p, carry):
        for r in range(TILE):
            for s in range(S_DEV):
                for a in range(3):
                    b = weight[s, r] * (state[p, s, a, r] - given[p, s, a, r])
                    rhs[s, a, r] = b
                    state[p + 1, s, a, r] = b

        def sweep(i, carry):
            for s in range(S_DEV):
                ex, ey, ez = e = [state[p + 1, s, a] for a in range(3)]
                ey_x, ez_x = (jnp.concatenate([v[1:], jnp.where(low, half(v[0]), 0.0)[None]], 0) for v in (ey, ez))
                hx = (y_up(ez) - ez) - (z_up(ey) - ey)
                hy = (z_up(ex) - ex) - (ez_x - ez)
                hz = (ey_x - ey) - (y_up(ex) - ex)
                hy_x, hz_x = (
                    jnp.concatenate([jnp.where(low, 0.0, half(v[TILE - 1]))[None], v[:-1]], 0) for v in (hy, hz)
                )
                back = (
                    (z_down(hy) - hy) - (y_down(hz) - hz),
                    (hz_x - hz) - (z_down(hx) - hx),
                    (y_down(hx) - hx) - (hy_x - hy),
                )
                w, keep = weight[s], keeps[s]
                for a in range(3):
                    state[p + 1, s, a] = keep * e[a] + (rhs[s, a] - w * back[a])
            return carry

        lax.fori_loop(0, 3, sweep, 0)
        return carry

    lax.fori_loop(0, 2, phase, 0)

    for k in range(HALF):
        for s in range(S_DEV):
            pair = [sum(state[1, s, a, 2 * k + i] * state[2, s, a, 2 * k + i] for a in range(3)) for i in range(2)]
            for d, v in zip((0, HALF), split(*pair)):
                at = pl.ds((k + d) * 8, 8)
                part[s, at, :] = -cond[s, at, :] * v

    for t in range(TILES):
        s, z = t // LZ, t % LZ
        got = part[s, pl.ds(z, TILE, stride=8), :]
        by_layer[pl.ds(t * TILE, TILE), :] = jnp.where(row < lengths[s, z], got, 0.0)
    by_layer[pl.ds(TILES * TILE, TILE), :] = jnp.zeros((TILE, 128), jnp.float32)


NEAR = [(0, 0)] + [d for d in NEAR_FIRST if d[0] == 0]
FAR = [d for d in NEAR_FIRST if d[0] == 1]
OWN_ROWS = NY * SHARE
BLOCKS = 2 * NX


def targets(starts, arrived, vals, senders):
    lane = lax.broadcasted_iota(jnp.int32, (8, 128), 1)
    found = []
    for i, (side, m) in enumerate([(side, m) for m in senders for side in range(2)]):
        v = arrived[side, m]
        head = v.astype(jnp.bfloat16)
        at = pl.ds(i * SLOT_ROWS, SLOT_ROWS)
        vals[at, pl.ds(0, 128)] = head
        vals[at, pl.ds(128, 128)] = (v - head.astype(jnp.float32)).astype(jnp.bfloat16)
        s = [starts[side, m, k] for k in range(CAP)]
        t = jnp.where(lane < 2 * TILE, jnp.where(lane < TILE, s[0], s[1]), jnp.where(lane < 3 * TILE, s[2], s[3]))
        found.append(t + lane % TILE)
    return found


def placed_rows(found, vals, rows, j):
    picked = [
        jnp.where(rows == (t - j * (2 * OWN_ROWS))[None], 1.0, 0.0).astype(jnp.bfloat16).reshape(OWN_ROWS, 128)
        for t in found
    ]
    d = jnp.dot(jnp.concatenate(picked, 1), vals[...], preferred_element_type=jnp.float32)
    return (d[:, :128] + d[:, 128:]).reshape(NY, SHARE, 128)


CUT = SHARE // 2
Z_ORDER = [4, 3, 5, 2, 6, 1, 7]


def whole_kernel(
    owner,
    offset,
    lengths,
    block_hbm,
    source_hbm,
    observed_hbm,
    out,
    place,
    holds,
    request,
    starts,
    arrived,
    smooth,
    given,
    block,
    source,
    observed,
    values,
    outbox,
    slots,
    by_layer,
    vals,
    dense,
    *rest,
):
    fields, boxes, sems = rest[:6], rest[6:12], rest[12:]
    z_box, y_box, z_sum, y_sum, zy_box, yz_box = boxes
    (load_sem, ask_send, ask_recv, row_send, row_recv, send, recv, core_send, core_recv, core_sem) = sems[:10]
    z_sem, y_sem, zy_sem, yz_sem = sems[10:]
    z, y, c, h, x = here()
    me = lax.axis_index("mdl")

    def chip(dz, dy):
        return ((((z + dz) % NZ) * NY + (y + dy) % NY) * 2 + c, me)

    barrier = pltpu.get_barrier_semaphore()
    greeted = [partner(*d)[0] for d in NEAR_FIRST] + [other_core()]
    greeted += [chip(d, 0) for d in Z_ORDER] + [chip(0, d) for d in range(1, NY)]
    for i in greeted:
        pl.semaphore_signal(barrier, inc=1, device_id=i, device_id_type=MESH)
    pairs = ((block_hbm, block), (source_hbm, source), (observed_hbm, observed))
    loads = [pltpu.make_async_copy(a, b, load_sem.at[i]) for i, (a, b) in enumerate(pairs)]
    for copy in loads:
        copy.start()

    owners = [owner[t // LZ, 0, t % LZ] for t in range(TILES)]
    firsts = [offset[t // LZ, t % LZ] for t in range(TILES)]
    slot_of = []
    for t in range(TILES):
        slot = owners[t] * CAP
        for i in range(t):
            slot = jnp.where(owners[i] == owners[t], slot + 1, slot)
        slot_of.append(slot)
        place[t] = slot * TILE

    def table(j, carry):
        first, held = jnp.int32(0), jnp.int32(TILES * TILE)
        for t in range(TILES):
            first = jnp.where(slot_of[t] == j, firsts[t], first)
            held = jnp.where(slot_of[t] == j, t * TILE, held)
        request[j // CAP, j % CAP] = first
        holds[j] = held
        return carry

    lax.fori_loop(0, OWN * CAP, table, 0)
    pl.semaphore_wait(barrier, len(greeted))

    asks, answers = {}, {}
    for dh, dx in NEAR_FIRST:
        to, m = partner(dh, dx)
        k = dh * NX + dx
        asks[dh, dx] = remote(request.at[m], starts.at[0, me], ask_send.at[k], ask_recv.at[k], to)
        asks[dh, dx].start()
    for k in range(CAP):
        starts[0, me, k] = request[me, k]
    loads[0].wait()
    for dh, dx in NEAR_FIRST:
        back = (-dh % 2, -dx % NX)
        asks[back].wait_recv()
        to, m = partner(dh, dx)
        k = dh * NX + dx
        for i in range(CAP):
            outbox[k, pl.ds(i * TILE, TILE), :] = block[pl.ds(starts[0, m, i], TILE), :]
        answers[dh, dx] = remote(
            outbox.at[k], values.at[pl.ds(me * SLOT_ROWS, SLOT_ROWS)], row_send.at[k], row_recv.at[k], to
        )
        answers[dh, dx].start()
    pass_on = remote(starts.at[0], starts.at[1], core_sem.at[0], core_sem.at[1], other_core())
    pass_on.start()
    for k in range(CAP):
        at = pl.ds(me * SLOT_ROWS + k * TILE, TILE)
        values[at, :] = block[pl.ds(starts[0, me, k], TILE), :]
    mine = block[pl.ds(lax.axis_index("grp") * SHARE, SHARE), :]
    lane = lax.broadcasted_iota(jnp.int32, (SHARE, 128), 1)
    left = jnp.where(lane == 0, mine, pltpu.roll(mine, 1, 1))
    right = jnp.where(lane == 127, mine, pltpu.roll(mine, 127, 1))
    smooth[...] = BETA * (2.0 * mine - left - right)
    for copy in loads[1:]:
        copy.wait()
    arrange(source, observed, given)
    for d in NEAR_FIRST:
        answers[d].wait_recv()

    solve(place, lengths, values, given, by_layer, *fields)

    def fill(m, ref):
        for k in range(CAP):
            ref[m, pl.ds(k * TILE, TILE), :] = by_layer[pl.ds(holds[m * CAP + k], TILE), :]

    copies, forwards = {}, {}
    for dh, dx in NEAR_FIRST:
        to, m = partner(dh, dx)
        k = dh * NX + dx
        fill(m, slots)
        copies[dh, dx] = remote(slots.at[m], arrived.at[0, me], send.at[k], recv.at[k], to)
        copies[dh, dx].start()
    fill(me, arrived.at[0])
    pass_on.wait()

    def take(steps):
        for dh, dx in steps:
            _, m = partner(dh, dx)
            if (dh, dx) != (0, 0):
                copies[-dh % 2, -dx % NX].wait_recv()
            k = dh * NX + dx
            forwards[dh, dx] = remote(
                arrived.at[0, m], arrived.at[1, m], core_send.at[k], core_recv.at[k], other_core()
            )
            forwards[dh, dx].start()
        for d in steps:
            forwards[d].wait_recv()
        return [partner(*d)[1] for d in steps]

    shape = (OWN_ROWS // 8, 8, 128)
    at = lax.broadcasted_iota(jnp.int32, shape, 0) * 8 + lax.broadcasted_iota(jnp.int32, shape, 1)
    rows = (at // SHARE) * (2 * SHARE) + at % SHARE + c * SHARE
    found = targets(starts, arrived, vals, take(NEAR))

    def near(j, carry):
        dense[j] = placed_rows(found, vals, rows, j)
        return carry

    lax.fori_loop(0, NZ, near, 0, unroll=4)
    found_far = targets(starts, arrived, vals, take(FAR))

    def push(src, dst, sem, i, to):
        copy = remote(src, dst, sem.at[0, i], sem.at[1, i], to)
        copy.start()
        return copy

    low, high = pl.ds(0, CUT), pl.ds(CUT, SHARE - CUT)
    along_z, along_y, then_y, then_z = {}, {}, {}, {}
    for d in Z_ORDER + [0]:
        j = (z + d) % NZ
        dense[j] = dense[j] + placed_rows(found_far, vals, rows, j)
        for e in (2, 1, 3):
            along_y[d, e] = remote(
                dense.at[j, (y + e) % NY, high, :],
                y_box.at[d, e - 1],
                y_sem.at[0, d, e - 1],
                y_sem.at[1, d, e - 1],
                chip(0, e),
            )
            along_y[d, e].start()
        if d:
            along_z[d] = push(dense.at[j, :, low, :], z_box.at[d - 1], z_sem, d - 1, chip(d, 0))
    for d in Z_ORDER + [0]:
        for e in (2, 1, 3):
            along_y[d, e].wait_recv()
        y_sum[d] = dense[(z + d) % NZ, y, high, :] + sum(y_box[d, k] for k in range(NY - 1))
        if d:
            then_z[d] = push(y_sum.at[d], yz_box.at[d - 1], yz_sem, d - 1, chip(d, 0))
    for copy in along_z.values():
        copy.wait_recv()
    for d in (2, 1, 3, 0):
        j = (y + d) % NY
        z_sum[d] = dense[z, j, low, :] + sum(z_box[k, j] for k in range(NZ - 1))
        if d:
            then_y[d] = push(z_sum.at[d], zy_box.at[d - 1], zy_sem, d - 1, chip(0, d))
    for copy in then_z.values():
        copy.wait_recv()
    out[high, :] = smooth[high, :] + y_sum[0] + sum(yz_box[k] for k in range(NZ - 1))
    for copy in then_y.values():
        copy.wait_recv()
    out[low, :] = smooth[low, :] + z_sum[0] + sum(zy_box[k] for k in range(NY - 1))
    for sent in (asks, answers, copies, forwards, along_z, along_y, then_z, then_y):
        for copy in sent.values():
            copy.wait_send()


def per_device(model, source, observed, owner_ids, offsets, lengths):
    block = model.reshape(ROWS, 128)
    f32, i32 = jnp.float32, jnp.int32
    dma = pltpu.SemaphoreType.DMA
    field = (S_DEV, 3, TILE, 8, 128)
    plain = pltpu.VMEM((S_DEV, TILE * 8, 128), f32)
    gradient = pl.pallas_call(
        whole_kernel,
        out_shape=jax.ShapeDtypeStruct((SHARE, 128), f32),
        in_specs=[SMEM, SMEM, SMEM, HBM, HBM, HBM],
        out_specs=VMEM,
        scratch_shapes=[
            pltpu.SMEM((TILES,), i32),
            pltpu.SMEM((OWN * CAP,), i32),
            pltpu.SMEM((OWN, 128), i32),
            pltpu.SMEM((2, OWN, 128), i32),
            pltpu.VMEM((2, OWN, SLOT_ROWS, 128), f32),
            pltpu.VMEM((SHARE, 128), f32),
            pltpu.VMEM((2,) + field, f32),
            pltpu.VMEM((ROWS, 128), f32),
            pltpu.VMEM((S_DEV, 3, LZ, TILE * 128), f32),
            pltpu.VMEM((S_DEV, 3, LZ, TILE * 128), f32),
            pltpu.VMEM((OWN * SLOT_ROWS, 128), f32),
            pltpu.VMEM((OWN, SLOT_ROWS, 128), f32),
            pltpu.VMEM((OWN, SLOT_ROWS, 128), f32),
            pltpu.VMEM(((TILES + 1) * TILE, 128), f32),
            pltpu.VMEM((BLOCKS * SLOT_ROWS, 256), jnp.bfloat16),
            pltpu.VMEM((NZ, NY, SHARE, 128), f32),
            plain,
            pltpu.VMEM((S_DEV, TILE, 8, 128), f32),
            pltpu.VMEM((S_DEV, TILE, 8, 128), f32),
            pltpu.VMEM((3,) + field, f32),
            pltpu.VMEM(field, f32),
            plain,
            pltpu.VMEM((NZ - 1, NY, CUT, 128), f32),
            pltpu.VMEM((NZ, NY - 1, SHARE - CUT, 128), f32),
            pltpu.VMEM((NY, CUT, 128), f32),
            pltpu.VMEM((NZ, SHARE - CUT, 128), f32),
            pltpu.VMEM((NY - 1, CUT, 128), f32),
            pltpu.VMEM((NZ - 1, SHARE - CUT, 128), f32),
            dma((3,)),
        ]
        + [dma((OWN,))] * 8
        + [dma((2,)), dma((2, NZ - 1)), dma((2, NZ, NY - 1)), dma((2, NY - 1)), dma((2, NZ - 1))],
        compiler_params=pltpu.CompilerParams(
            collective_id=0, has_side_effects=True, vmem_limit_bytes=60 << 20
        ),
        name="whole",
    )(owner_ids.transpose(0, 2, 1), offsets, lengths, block, source, observed)
    return gradient[:, None, :]


def solution(mesh):
    placed = (
        P(None, "mdl", None),
        P(("grp", "mdl"), None, None, None),
        P(("grp", "mdl"), None, None, None),
        P(("grp", "mdl"), None, None),
        P(("grp", "mdl"), None),
        P(("grp", "mdl"), None),
    )
    return jax.shard_map(
        per_device, mesh=mesh, in_specs=placed, out_specs=P("grp", "mdl", None), check_vma=False
    )
```

```python
import functools

import jax
import jax.numpy as jnp
from jax import lax
from jax.experimental import pallas as pl
from jax.experimental.pallas import tpu as pltpu
from jax.sharding import PartitionSpec as P

LZ = 8
S_DEV = 2
TILES = S_DEV * LZ
TILE = 32
ROWS = 4096
CAP = 4
AIR = 0.05
BETA = 0.5

NZ, NY, NX = 8, 4, 4
OWN = 2 * NX
SLOT_ROWS = CAP * TILE
SHARE = ROWS // (NZ * NY * 2)

MESH = pl.DeviceIdType.MESH
SMEM = pl.BlockSpec(memory_space=pltpu.SMEM)
VMEM = pl.BlockSpec(memory_space=pltpu.VMEM)
HBM = pl.BlockSpec(memory_space=pl.ANY)
NEAR_FIRST = [(0, 2), (0, 1), (0, 3), (1, 2), (1, 1), (1, 3), (1, 0)]


def here():
    g, m = lax.axis_index("grp"), lax.axis_index("mdl")
    return g // (2 * NY), (g // 2) % NY, g % 2, m // NX, m % NX


def partner(dh, dx):
    z, y, c, h, x = here()
    y = NY - 1 - y if dh % 2 else y
    m = ((h + dh) % 2) * NX + (x + dx) % NX
    return ((z * NY + y) * 2 + c, m), m


def other_core():
    z, y, c, h, x = here()
    return ((z * NY + y) * 2 + 1 - c, h * NX + x)


def meet(ids):
    barrier = pltpu.get_barrier_semaphore()
    for i in ids:
        pl.semaphore_signal(barrier, inc=1, device_id=i, device_id_type=MESH)
    pl.semaphore_wait(barrier, len(ids))


def remote(src, dst, send, recv, to):
    return pltpu.make_async_remote_copy(
        src_ref=src, dst_ref=dst, send_sem=send, recv_sem=recv, device_id=to, device_id_type=MESH
    )


HALF = TILE // 2


def half(v):
    return pltpu.roll(v, 64, 1)


def split(a, b):
    low = lax.broadcasted_iota(jnp.int32, (8, 128), 1) < 64
    return jnp.where(low, a, half(b)), jnp.where(low, half(a), b)


def arrange(source, observed, given):
    def one(k, carry):
        places = [pl.ds(pl.multiple_of((k + d) * 128, 128), 128) for d in (0, HALF)]
        for s in range(S_DEV):
            for a in range(3):
                p, q = split(*[source[s, a, :, at] for at in places])
                given[0, s, a, 2 * k] = -p
                given[0, s, a, 2 * k + 1] = -q
                p, q = split(*[observed[s, a, :, at] for at in places])
                given[1, s, a, 2 * k] = p
                given[1, s, a, 2 * k + 1] = q
        return carry

    lax.fori_loop(0, HALF, one, 0, unroll=4)


def solve(place, lengths, values, given, by_layer, cond, weight, keeps, state, rhs, part):
    lane = lax.broadcasted_iota(jnp.int32, (8, 128), 1)
    layer = lax.broadcasted_iota(jnp.int32, (8, 128), 0)
    row = lax.broadcasted_iota(jnp.int32, (TILE, 128), 0)
    low = lane < 64

    def shift(mask, by, axis):
        def all_of(v):
            return jnp.stack([jnp.where(mask, pltpu.roll(v[i], by, axis), 0.0) for i in range(v.shape[0])])

        return all_of

    y_up, y_down = shift(lane % 64 != 63, 127, 1), shift(lane % 64 != 0, 1, 1)
    z_up, z_down = shift(layer != LZ - 1, LZ - 1, 0), shift(layer != 0, 1, 0)

    for t in range(TILES):
        s, z = t // LZ, t % LZ
        got = values[pl.ds(place[t], TILE), :]
        cond[s, pl.ds(z, TILE, stride=8), :] = jnp.where(row < lengths[s, z], jnp.exp(got), AIR)

    for k in range(HALF):
        for s in range(S_DEV):
            pair = split(*[cond[s, pl.ds((k + d) * 8, 8), :] for d in (0, HALF)])
            for i in range(2):
                w = 0.5 / (4.0 + pair[i])
                weight[s, 2 * k + i] = w
                keeps[s, 2 * k + i] = 0.5 + 4.0 * w

    state[0] = jnp.zeros_like(state[0])

    def phase(p, carry):
        for r in range(TILE):
            for s in range(S_DEV):
                for a in range(3):
                    b = weight[s, r] * (state[p, s, a, r] - given[p, s, a, r])
                    rhs[s, a, r] = b
                    state[p + 1, s, a, r] = b

        def sweep(i, carry):
            for s in range(S_DEV):
                ex, ey, ez = e = [state[p + 1, s, a] for a in range(3)]
                ey_x, ez_x = (jnp.concatenate([v[1:], jnp.where(low, half(v[0]), 0.0)[None]], 0) for v in (ey, ez))
                hx = (y_up(ez) - ez) - (z_up(ey) - ey)
                hy = (z_up(ex) - ex) - (ez_x - ez)
                hz = (ey_x - ey) - (y_up(ex) - ex)
                hy_x, hz_x = (
                    jnp.concatenate([jnp.where(low, 0.0, half(v[TILE - 1]))[None], v[:-1]], 0) for v in (hy, hz)
                )
                back = (
                    (z_down(hy) - hy) - (y_down(hz) - hz),
                    (hz_x - hz) - (z_down(hx) - hx),
                    (y_down(hx) - hx) - (hy_x - hy),
                )
                w, keep = weight[s], keeps[s]
                for a in range(3):
                    state[p + 1, s, a] = keep * e[a] + (rhs[s, a] - w * back[a])
            return carry

        lax.fori_loop(0, 3, sweep, 0)
        return carry

    lax.fori_loop(0, 2, phase, 0)

    for k in range(HALF):
        for s in range(S_DEV):
            pair = [sum(state[1, s, a, 2 * k + i] * state[2, s, a, 2 * k + i] for a in range(3)) for i in range(2)]
            for d, v in zip((0, HALF), split(*pair)):
                at = pl.ds((k + d) * 8, 8)
                part[s, at, :] = -cond[s, at, :] * v

    for t in range(TILES):
        s, z = t // LZ, t % LZ
        got = part[s, pl.ds(z, TILE, stride=8), :]
        by_layer[pl.ds(t * TILE, TILE), :] = jnp.where(row < lengths[s, z], got, 0.0)
    by_layer[pl.ds(TILES * TILE, TILE), :] = jnp.zeros((TILE, 128), jnp.float32)


NEAR = [(0, 0)] + [d for d in NEAR_FIRST if d[0] == 0]
FAR = [d for d in NEAR_FIRST if d[0] == 1]
OWN_ROWS = NY * SHARE
BLOCKS = 2 * NX


def targets(starts, arrived, vals, senders):
    lane = lax.broadcasted_iota(jnp.int32, (8, 128), 1)
    found = []
    for i, (side, m) in enumerate([(side, m) for m in senders for side in range(2)]):
        v = arrived[side, m]
        head = v.astype(jnp.bfloat16)
        at = pl.ds(i * SLOT_ROWS, SLOT_ROWS)
        vals[at, pl.ds(0, 128)] = head
        vals[at, pl.ds(128, 128)] = (v - head.astype(jnp.float32)).astype(jnp.bfloat16)
        s = [starts[side, m, k] for k in range(CAP)]
        t = jnp.where(lane < 2 * TILE, jnp.where(lane < TILE, s[0], s[1]), jnp.where(lane < 3 * TILE, s[2], s[3]))
        found.append(t + lane % TILE)
    return found


def placed_rows(found, vals, rows, j):
    picked = [
        jnp.where(rows == (t - j * (2 * OWN_ROWS))[None], 1.0, 0.0).astype(jnp.bfloat16).reshape(OWN_ROWS, 128)
        for t in found
    ]
    d = jnp.dot(jnp.concatenate(picked, 1), vals[...], preferred_element_type=jnp.float32)
    return (d[:, :128] + d[:, 128:]).reshape(NY, SHARE, 128)


CUT = SHARE // 2
Z_ORDER = [4, 3, 5, 2, 6, 1, 7]


def whole_kernel(
    owner,
    offset,
    lengths,
    block_hbm,
    source_hbm,
    observed_hbm,
    out,
    place,
    holds,
    request,
    starts,
    arrived,
    smooth,
    given,
    block,
    source,
    observed,
    values,
    outbox,
    slots,
    by_layer,
    vals,
    dense,
    *rest,
):
    fields, boxes, sems = rest[:6], rest[6:12], rest[12:]
    z_box, y_box, z_sum, y_sum, zy_box, yz_box = boxes
    (load_sem, ask_send, ask_recv, row_send, row_recv, send, recv, core_send, core_recv, core_sem) = sems[:10]
    z_sem, y_sem, zy_sem, yz_sem = sems[10:]
    z, y, c, h, x = here()
    me = lax.axis_index("mdl")

    def chip(dz, dy):
        return ((((z + dz) % NZ) * NY + (y + dy) % NY) * 2 + c, me)

    barrier = pltpu.get_barrier_semaphore()
    greeted = [partner(*d)[0] for d in NEAR_FIRST] + [other_core()]
    greeted += [chip(d, 0) for d in Z_ORDER] + [chip(0, d) for d in range(1, NY)]
    for i in greeted:
        pl.semaphore_signal(barrier, inc=1, device_id=i, device_id_type=MESH)
    pairs = ((block_hbm, block), (source_hbm, source), (observed_hbm, observed))
    loads = [pltpu.make_async_copy(a, b, load_sem.at[i]) for i, (a, b) in enumerate(pairs)]
    for copy in loads:
        copy.start()

    owners = [owner[t // LZ, 0, t % LZ] for t in range(TILES)]
    firsts = [offset[t // LZ, t % LZ] for t in range(TILES)]
    slot_of = []
    for t in range(TILES):
        slot = owners[t] * CAP
        for i in range(t):
            slot = jnp.where(owners[i] == owners[t], slot + 1, slot)
        slot_of.append(slot)
        place[t] = slot * TILE

    def ask(o, carry):
        for k in range(CAP):
            first = jnp.int32(0)
            for t in range(TILES):
                first = jnp.where(slot_of[t] == o * CAP + k, firsts[t], first)
            request[o, k] = first
        return carry

    lax.fori_loop(0, OWN, ask, 0)
    pl.semaphore_wait(barrier, len(greeted))

    asks, answers = {}, {}
    for dh, dx in NEAR_FIRST:
        to, m = partner(dh, dx)
        k = dh * NX + dx
        asks[dh, dx] = remote(request.at[m], starts.at[0, me], ask_send.at[k], ask_recv.at[k], to)
        asks[dh, dx].start()
    for k in range(CAP):
        starts[0, me, k] = request[me, k]
    loads[0].wait()
    for dh, dx in NEAR_FIRST:
        back = (-dh % 2, -dx % NX)
        asks[back].wait_recv()
        to, m = partner(dh, dx)
        k = dh * NX + dx
        for i in range(CAP):
            outbox[k, pl.ds(i * TILE, TILE), :] = block[pl.ds(starts[0, m, i], TILE), :]
        answers[dh, dx] = remote(
            outbox.at[k], values.at[pl.ds(me * SLOT_ROWS, SLOT_ROWS)], row_send.at[k], row_recv.at[k], to
        )
        answers[dh, dx].start()
    pass_on = remote(starts.at[0], starts.at[1], core_sem.at[0], core_sem.at[1], other_core())
    pass_on.start()
    for k in range(CAP):
        at = pl.ds(me * SLOT_ROWS + k * TILE, TILE)
        values[at, :] = block[pl.ds(starts[0, me, k], TILE), :]
    mine = block[pl.ds(lax.axis_index("grp") * SHARE, SHARE), :]
    lane = lax.broadcasted_iota(jnp.int32, (SHARE, 128), 1)
    left = jnp.where(lane == 0, mine, pltpu.roll(mine, 1, 1))
    right = jnp.where(lane == 127, mine, pltpu.roll(mine, 127, 1))
    smooth[...] = BETA * (2.0 * mine - left - right)
    for copy in loads[1:]:
        copy.wait()
    arrange(source, observed, given)

    def hold(o, carry):
        for k in range(CAP):
            held = jnp.int32(TILES * TILE)
            for t in range(TILES):
                held = jnp.where(place[t] == (o * CAP + k) * TILE, t * TILE, held)
            holds[o * CAP + k] = held
        return carry

    lax.fori_loop(0, OWN, hold, 0)
    for d in NEAR_FIRST:
        answers[d].wait_recv()

    solve(place, lengths, values, given, by_layer, *fields)

    def fill(m, ref):
        for k in range(CAP):
            ref[m, pl.ds(k * TILE, TILE), :] = by_layer[pl.ds(holds[m * CAP + k], TILE), :]

    copies, forwards = {}, {}
    for dh, dx in NEAR_FIRST:
        to, m = partner(dh, dx)
        k = dh * NX + dx
        fill(m, slots)
        copies[dh, dx] = remote(slots.at[m], arrived.at[0, me], send.at[k], recv.at[k], to)
        copies[dh, dx].start()
    fill(me, arrived.at[0])
    pass_on.wait()

    def take(steps):
        for dh, dx in steps:
            _, m = partner(dh, dx)
            if (dh, dx) != (0, 0):
                copies[-dh % 2, -dx % NX].wait_recv()
            k = dh * NX + dx
            forwards[dh, dx] = remote(
                arrived.at[0, m], arrived.at[1, m], core_send.at[k], core_recv.at[k], other_core()
            )
            forwards[dh, dx].start()
        for d in steps:
            forwards[d].wait_recv()
        return [partner(*d)[1] for d in steps]

    shape = (OWN_ROWS // 8, 8, 128)
    at = lax.broadcasted_iota(jnp.int32, shape, 0) * 8 + lax.broadcasted_iota(jnp.int32, shape, 1)
    rows = (at // SHARE) * (2 * SHARE) + at % SHARE + c * SHARE
    found = targets(starts, arrived, vals, take(NEAR))

    def near(j, carry):
        dense[j] = placed_rows(found, vals, rows, j)
        return carry

    lax.fori_loop(0, NZ, near, 0, unroll=4)
    found_far = targets(starts, arrived, vals, take(FAR))

    def push(src, dst, sem, i, to):
        copy = remote(src, dst, sem.at[0, i], sem.at[1, i], to)
        copy.start()
        return copy

    low, high = pl.ds(0, CUT), pl.ds(CUT, SHARE - CUT)
    along_z, along_y, then_y, then_z = {}, {}, {}, {}
    for d in Z_ORDER + [0]:
        j = (z + d) % NZ
        dense[j] = dense[j] + placed_rows(found_far, vals, rows, j)
        if d:
            along_z[d] = push(dense.at[j, :, low, :], z_box.at[d - 1], z_sem, d - 1, chip(d, 0))
    for d in (2, 1, 3):
        along_y[d] = push(dense.at[:, (y + d) % NY, high, :], y_box.at[d - 1], y_sem, d - 1, chip(0, d))
    for copy in along_y.values():
        copy.wait_recv()
    for d in Z_ORDER + [0]:
        j = (z + d) % NZ
        y_sum[d] = dense[j, y, high, :] + sum(y_box[k, j] for k in range(NY - 1))
        if d:
            then_z[d] = push(y_sum.at[d], yz_box.at[d - 1], yz_sem, d - 1, chip(d, 0))
    for copy in along_z.values():
        copy.wait_recv()
    for d in (2, 1, 3, 0):
        j = (y + d) % NY
        z_sum[d] = dense[z, j, low, :] + sum(z_box[k, j] for k in range(NZ - 1))
        if d:
            then_y[d] = push(z_sum.at[d], zy_box.at[d - 1], zy_sem, d - 1, chip(0, d))
    for copy in then_z.values():
        copy.wait_recv()
    out[high, :] = smooth[high, :] + y_sum[0] + sum(yz_box[k] for k in range(NZ - 1))
    for copy in then_y.values():
        copy.wait_recv()
    out[low, :] = smooth[low, :] + z_sum[0] + sum(zy_box[k] for k in range(NY - 1))
    for sent in (asks, answers, copies, forwards, along_z, along_y, then_z, then_y):
        for copy in sent.values():
            copy.wait_send()


def per_device(model, source, observed, owner_ids, offsets, lengths):
    block = model.reshape(ROWS, 128)
    f32, i32 = jnp.float32, jnp.int32
    dma = pltpu.SemaphoreType.DMA
    field = (S_DEV, 3, TILE, 8, 128)
    plain = pltpu.VMEM((S_DEV, TILE * 8, 128), f32)
    gradient = pl.pallas_call(
        whole_kernel,
        out_shape=jax.ShapeDtypeStruct((SHARE, 128), f32),
        in_specs=[SMEM, SMEM, SMEM, HBM, HBM, HBM],
        out_specs=VMEM,
        scratch_shapes=[
            pltpu.SMEM((TILES,), i32),
            pltpu.SMEM((OWN * CAP,), i32),
            pltpu.SMEM((OWN, 128), i32),
            pltpu.SMEM((2, OWN, 128), i32),
            pltpu.VMEM((2, OWN, SLOT_ROWS, 128), f32),
            pltpu.VMEM((SHARE, 128), f32),
            pltpu.VMEM((2,) + field, f32),
            pltpu.VMEM((ROWS, 128), f32),
            pltpu.VMEM((S_DEV, 3, LZ, TILE * 128), f32),
            pltpu.VMEM((S_DEV, 3, LZ, TILE * 128), f32),
            pltpu.VMEM((OWN * SLOT_ROWS, 128), f32),
            pltpu.VMEM((OWN, SLOT_ROWS, 128), f32),
            pltpu.VMEM((OWN, SLOT_ROWS, 128), f32),
            pltpu.VMEM(((TILES + 1) * TILE, 128), f32),
            pltpu.VMEM((BLOCKS * SLOT_ROWS, 256), jnp.bfloat16),
            pltpu.VMEM((NZ, NY, SHARE, 128), f32),
            plain,
            pltpu.VMEM((S_DEV, TILE, 8, 128), f32),
            pltpu.VMEM((S_DEV, TILE, 8, 128), f32),
            pltpu.VMEM((3,) + field, f32),
            pltpu.VMEM(field, f32),
            plain,
            pltpu.VMEM((NZ - 1, NY, CUT, 128), f32),
            pltpu.VMEM((NY - 1, NZ, SHARE - CUT, 128), f32),
            pltpu.VMEM((NY, CUT, 128), f32),
            pltpu.VMEM((NZ, SHARE - CUT, 128), f32),
            pltpu.VMEM((NY - 1, CUT, 128), f32),
            pltpu.VMEM((NZ - 1, SHARE - CUT, 128), f32),
            dma((3,)),
        ]
        + [dma((OWN,))] * 8
        + [dma((2,)), dma((2, NZ - 1)), dma((2, NY - 1)), dma((2, NY - 1)), dma((2, NZ - 1))],
        compiler_params=pltpu.CompilerParams(
            collective_id=0, has_side_effects=True, vmem_limit_bytes=60 << 20
        ),
        name="whole",
    )(owner_ids.transpose(0, 2, 1), offsets, lengths, block, source, observed)
    return gradient[:, None, :]


def solution(mesh):
    placed = (
        P(None, "mdl", None),
        P(("grp", "mdl"), None, None, None),
        P(("grp", "mdl"), None, None, None),
        P(("grp", "mdl"), None, None),
        P(("grp", "mdl"), None),
        P(("grp", "mdl"), None),
    )
    return jax.shard_map(
        per_device, mesh=mesh, in_specs=placed, out_specs=P("grp", "mdl", None), check_vma=False
    )
```

```python
import functools

import jax
import jax.numpy as jnp
from jax import lax
from jax.experimental import pallas as pl
from jax.experimental.pallas import tpu as pltpu
from jax.sharding import PartitionSpec as P

LZ = 8
S_DEV = 2
TILES = S_DEV * LZ
TILE = 32
ROWS = 4096
CAP = 4
AIR = 0.05
BETA = 0.5

NZ, NY, NX = 8, 4, 4
OWN = 2 * NX
SLOT_ROWS = CAP * TILE
SHARE = ROWS // (NZ * NY * 2)

MESH = pl.DeviceIdType.MESH
SMEM = pl.BlockSpec(memory_space=pltpu.SMEM)
VMEM = pl.BlockSpec(memory_space=pltpu.VMEM)
HBM = pl.BlockSpec(memory_space=pl.ANY)
NEAR_FIRST = [(0, 2), (0, 1), (0, 3), (1, 2), (1, 1), (1, 3), (1, 0)]


def here():
    g, m = lax.axis_index("grp"), lax.axis_index("mdl")
    return g // (2 * NY), (g // 2) % NY, g % 2, m // NX, m % NX


def partner(dh, dx):
    z, y, c, h, x = here()
    y = NY - 1 - y if dh % 2 else y
    m = ((h + dh) % 2) * NX + (x + dx) % NX
    return ((z * NY + y) * 2 + c, m), m


def other_core():
    z, y, c, h, x = here()
    return ((z * NY + y) * 2 + 1 - c, h * NX + x)


def meet(ids):
    barrier = pltpu.get_barrier_semaphore()
    for i in ids:
        pl.semaphore_signal(barrier, inc=1, device_id=i, device_id_type=MESH)
    pl.semaphore_wait(barrier, len(ids))


def remote(src, dst, send, recv, to):
    return pltpu.make_async_remote_copy(
        src_ref=src, dst_ref=dst, send_sem=send, recv_sem=recv, device_id=to, device_id_type=MESH
    )


HALF = TILE // 2


def half(v):
    return pltpu.roll(v, 64, 1)


def split(a, b):
    low = lax.broadcasted_iota(jnp.int32, (8, 128), 1) < 64
    return jnp.where(low, a, half(b)), jnp.where(low, half(a), b)


def arrange(source, observed, given):
    def one(k, carry):
        places = [pl.ds(pl.multiple_of((k + d) * 128, 128), 128) for d in (0, HALF)]
        for s in range(S_DEV):
            for a in range(3):
                p, q = split(*[source[s, a, :, at] for at in places])
                given[0, s, a, 2 * k] = -p
                given[0, s, a, 2 * k + 1] = -q
                p, q = split(*[observed[s, a, :, at] for at in places])
                given[1, s, a, 2 * k] = p
                given[1, s, a, 2 * k + 1] = q
        return carry

    lax.fori_loop(0, HALF, one, 0, unroll=4)


def solve(place, lengths, values, given, by_layer, cond, weight, keeps, state, rhs, part):
    lane = lax.broadcasted_iota(jnp.int32, (8, 128), 1)
    layer = lax.broadcasted_iota(jnp.int32, (8, 128), 0)
    row = lax.broadcasted_iota(jnp.int32, (TILE, 128), 0)
    low = lane < 64

    def shift(mask, by, axis):
        def all_of(v):
            return jnp.stack([jnp.where(mask, pltpu.roll(v[i], by, axis), 0.0) for i in range(v.shape[0])])

        return all_of

    y_up, y_down = shift(lane % 64 != 63, 127, 1), shift(lane % 64 != 0, 1, 1)
    z_up, z_down = shift(layer != LZ - 1, LZ - 1, 0), shift(layer != 0, 1, 0)

    for t in range(TILES):
        s, z = t // LZ, t % LZ
        got = values[pl.ds(place[t], TILE), :]
        cond[s, pl.ds(z, TILE, stride=8), :] = jnp.where(row < lengths[s, z], jnp.exp(got), AIR)

    for k in range(HALF):
        for s in range(S_DEV):
            pair = split(*[cond[s, pl.ds((k + d) * 8, 8), :] for d in (0, HALF)])
            for i in range(2):
                w = 0.5 / (4.0 + pair[i])
                weight[s, 2 * k + i] = w
                keeps[s, 2 * k + i] = 0.5 + 4.0 * w

    state[0] = jnp.zeros_like(state[0])

    def phase(p, carry):
        for r in range(TILE):
            for s in range(S_DEV):
                for a in range(3):
                    b = weight[s, r] * (state[p, s, a, r] - given[p, s, a, r])
                    rhs[s, a, r] = b
                    state[p + 1, s, a, r] = b

        def sweep(i, carry):
            for s in range(S_DEV):
                ex, ey, ez = e = [state[p + 1, s, a] for a in range(3)]
                ey_x, ez_x = (jnp.concatenate([v[1:], jnp.where(low, half(v[0]), 0.0)[None]], 0) for v in (ey, ez))
                hx = (y_up(ez) - ez) - (z_up(ey) - ey)
                hy = (z_up(ex) - ex) - (ez_x - ez)
                hz = (ey_x - ey) - (y_up(ex) - ex)
                hy_x, hz_x = (
                    jnp.concatenate([jnp.where(low, 0.0, half(v[TILE - 1]))[None], v[:-1]], 0) for v in (hy, hz)
                )
                back = (
                    (z_down(hy) - hy) - (y_down(hz) - hz),
                    (hz_x - hz) - (z_down(hx) - hx),
                    (y_down(hx) - hx) - (hy_x - hy),
                )
                w, keep = weight[s], keeps[s]
                for a in range(3):
                    state[p + 1, s, a] = keep * e[a] + (rhs[s, a] - w * back[a])
            return carry

        lax.fori_loop(0, 3, sweep, 0)
        return carry

    lax.fori_loop(0, 2, phase, 0)

    for k in range(HALF):
        for s in range(S_DEV):
            pair = [sum(state[1, s, a, 2 * k + i] * state[2, s, a, 2 * k + i] for a in range(3)) for i in range(2)]
            for d, v in zip((0, HALF), split(*pair)):
                at = pl.ds((k + d) * 8, 8)
                part[s, at, :] = -cond[s, at, :] * v

    for t in range(TILES):
        s, z = t // LZ, t % LZ
        got = part[s, pl.ds(z, TILE, stride=8), :]
        by_layer[pl.ds(t * TILE, TILE), :] = jnp.where(row < lengths[s, z], got, 0.0)
    by_layer[pl.ds(TILES * TILE, TILE), :] = jnp.zeros((TILE, 128), jnp.float32)


NEAR = [(0, 0)] + [d for d in NEAR_FIRST if d[0] == 0]
FAR = [d for d in NEAR_FIRST if d[0] == 1]
OWN_ROWS = NY * SHARE
BLOCKS = 2 * NX


def targets(starts, arrived, vals, senders):
    lane = lax.broadcasted_iota(jnp.int32, (8, 128), 1)
    found = []
    for i, (side, m) in enumerate([(side, m) for m in senders for side in range(2)]):
        v = arrived[side, m]
        head = v.astype(jnp.bfloat16)
        at = pl.ds(i * SLOT_ROWS, SLOT_ROWS)
        vals[at, pl.ds(0, 128)] = head
        vals[at, pl.ds(128, 128)] = (v - head.astype(jnp.float32)).astype(jnp.bfloat16)
        s = [starts[side, m, k] for k in range(CAP)]
        t = jnp.where(lane < 2 * TILE, jnp.where(lane < TILE, s[0], s[1]), jnp.where(lane < 3 * TILE, s[2], s[3]))
        found.append(t + lane % TILE)
    return found


def placed_rows(found, vals, rows, j):
    picked = [
        jnp.where(rows == (t - j * (2 * OWN_ROWS))[None], 1.0, 0.0).astype(jnp.bfloat16).reshape(OWN_ROWS, 128)
        for t in found
    ]
    d = jnp.dot(jnp.concatenate(picked, 1), vals[...], preferred_element_type=jnp.float32)
    return (d[:, :128] + d[:, 128:]).reshape(NY, SHARE, 128)


CUT = SHARE // 2
Z_ORDER = [4, 3, 5, 2, 6, 1, 7]


def whole_kernel(
    owner,
    offset,
    lengths,
    block_hbm,
    source_hbm,
    observed_hbm,
    out,
    place,
    holds,
    request,
    starts,
    arrived,
    smooth,
    given,
    block,
    source,
    observed,
    values,
    outbox,
    slots,
    by_layer,
    vals,
    dense,
    *rest,
):
    fields, boxes, sems = rest[:6], rest[6:12], rest[12:]
    z_box, y_box, z_sum, y_sum, zy_box, yz_box = boxes
    (load_sem, ask_send, ask_recv, row_send, row_recv, send, recv, core_send, core_recv, core_sem) = sems[:10]
    z_sem, y_sem, zy_sem, yz_sem = sems[10:]
    z, y, c, h, x = here()
    me = lax.axis_index("mdl")

    def chip(dz, dy):
        return ((((z + dz) % NZ) * NY + (y + dy) % NY) * 2 + c, me)

    barrier = pltpu.get_barrier_semaphore()
    greeted = [partner(*d)[0] for d in NEAR_FIRST] + [other_core()]
    greeted += [chip(d, 0) for d in Z_ORDER] + [chip(0, d) for d in range(1, NY)]
    for i in greeted:
        pl.semaphore_signal(barrier, inc=1, device_id=i, device_id_type=MESH)
    pairs = ((block_hbm, block), (source_hbm, source), (observed_hbm, observed))
    loads = [pltpu.make_async_copy(a, b, load_sem.at[i]) for i, (a, b) in enumerate(pairs)]
    for copy in loads:
        copy.start()

    owners = [owner[t // LZ, 0, t % LZ] for t in range(TILES)]
    firsts = [offset[t // LZ, t % LZ] for t in range(TILES)]
    slot_of = []
    for t in range(TILES):
        slot = owners[t] * CAP
        for i in range(t):
            slot = jnp.where(owners[i] == owners[t], slot + 1, slot)
        slot_of.append(slot)
        place[t] = slot * TILE

    def ask(o, carry):
        for k in range(CAP):
            first = jnp.int32(0)
            for t in range(TILES):
                first = jnp.where(slot_of[t] == o * CAP + k, firsts[t], first)
            request[o, k] = first
        return carry

    lax.fori_loop(0, OWN, ask, 0)
    pl.semaphore_wait(barrier, len(greeted))

    asks, answers = {}, {}
    for dh, dx in NEAR_FIRST:
        to, m = partner(dh, dx)
        k = dh * NX + dx
        asks[dh, dx] = remote(request.at[m], starts.at[0, me], ask_send.at[k], ask_recv.at[k], to)
        asks[dh, dx].start()
    for k in range(CAP):
        starts[0, me, k] = request[me, k]
    loads[0].wait()
    for dh, dx in NEAR_FIRST:
        back = (-dh % 2, -dx % NX)
        asks[back].wait_recv()
        to, m = partner(dh, dx)
        k = dh * NX + dx
        for i in range(CAP):
            outbox[k, pl.ds(i * TILE, TILE), :] = block[pl.ds(starts[0, m, i], TILE), :]
        answers[dh, dx] = remote(
            outbox.at[k], values.at[pl.ds(me * SLOT_ROWS, SLOT_ROWS)], row_send.at[k], row_recv.at[k], to
        )
        answers[dh, dx].start()
    pass_on = remote(starts.at[0], starts.at[1], core_sem.at[0], core_sem.at[1], other_core())
    pass_on.start()
    for k in range(CAP):
        at = pl.ds(me * SLOT_ROWS + k * TILE, TILE)
        values[at, :] = block[pl.ds(starts[0, me, k], TILE), :]
    mine = block[pl.ds(lax.axis_index("grp") * SHARE, SHARE), :]
    lane = lax.broadcasted_iota(jnp.int32, (SHARE, 128), 1)
    left = jnp.where(lane == 0, mine, pltpu.roll(mine, 1, 1))
    right = jnp.where(lane == 127, mine, pltpu.roll(mine, 127, 1))
    smooth[...] = BETA * (2.0 * mine - left - right)
    for copy in loads[1:]:
        copy.wait()
    arrange(source, observed, given)

    def hold(o, carry):
        for k in range(CAP):
            held = jnp.int32(TILES * TILE)
            for t in range(TILES):
                held = jnp.where(place[t] == (o * CAP + k) * TILE, t * TILE, held)
            holds[o * CAP + k] = held
        return carry

    lax.fori_loop(0, OWN, hold, 0)
    for d in NEAR_FIRST:
        answers[d].wait_recv()

    solve(place, lengths, values, given, by_layer, *fields)

    def fill(m, ref):
        for k in range(CAP):
            ref[m, pl.ds(k * TILE, TILE), :] = by_layer[pl.ds(holds[m * CAP + k], TILE), :]

    copies, forwards = {}, {}
    for dh, dx in NEAR_FIRST:
        to, m = partner(dh, dx)
        k = dh * NX + dx
        fill(m, slots)
        copies[dh, dx] = remote(slots.at[m], arrived.at[0, me], send.at[k], recv.at[k], to)
        copies[dh, dx].start()
    fill(me, arrived.at[0])
    pass_on.wait()

    def take(steps):
        for dh, dx in steps:
            _, m = partner(dh, dx)
            if (dh, dx) != (0, 0):
                copies[-dh % 2, -dx % NX].wait_recv()
            k = dh * NX + dx
            forwards[dh, dx] = remote(
                arrived.at[0, m], arrived.at[1, m], core_send.at[k], core_recv.at[k], other_core()
            )
            forwards[dh, dx].start()
        for d in steps:
            forwards[d].wait_recv()
        return [partner(*d)[1] for d in steps]

    shape = (OWN_ROWS // 8, 8, 128)
    at = lax.broadcasted_iota(jnp.int32, shape, 0) * 8 + lax.broadcasted_iota(jnp.int32, shape, 1)
    rows = (at // SHARE) * (2 * SHARE) + at % SHARE + c * SHARE
    found = targets(starts, arrived, vals, take(NEAR))

    def near(d, carry):
        dense[d] = placed_rows(found, vals, rows, (z + d) % NZ)
        return carry

    lax.fori_loop(0, NZ, near, 0, unroll=4)
    found_far = targets(starts, arrived, vals, take(FAR))

    def push(src, dst, sem, i, to):
        copy = remote(src, dst, sem.at[0, i], sem.at[1, i], to)
        copy.start()
        return copy

    low, high = pl.ds(0, CUT), pl.ds(CUT, SHARE - CUT)
    along_z, along_y, then_y, then_z = {}, {}, {}, {}
    parts = (4, 5, 6, 7), (3, 2, 1, 0)
    for part, steps in enumerate(parts):
        for d in steps:
            dense[d] = dense[d] + placed_rows(found_far, vals, rows, (z + d) % NZ)
            if d:
                along_z[d] = push(dense.at[d, :, low, :], z_box.at[d - 1], z_sem, d - 1, chip(d, 0))
        for e in (2, 1, 3):
            along_y[part, e] = push(
                dense.at[pl.ds(min(steps), 4), (y + e) % NY, high, :],
                y_box.at[part, e - 1],
                y_sem,
                part * (NY - 1) + e - 1,
                chip(0, e),
            )
    for part, steps in enumerate(parts):
        for e in (2, 1, 3):
            along_y[part, e].wait_recv()
        for d in steps:
            y_sum[d] = dense[d, y, high, :] + sum(y_box[part, k, d % 4] for k in range(NY - 1))
            if d:
                then_z[d] = push(y_sum.at[d], yz_box.at[d - 1], yz_sem, d - 1, chip(d, 0))
    for copy in along_z.values():
        copy.wait_recv()
    for d in (2, 1, 3, 0):
        j = (y + d) % NY
        z_sum[d] = dense[0, j, low, :] + sum(z_box[k, j] for k in range(NZ - 1))
        if d:
            then_y[d] = push(z_sum.at[d], zy_box.at[d - 1], zy_sem, d - 1, chip(0, d))
    for copy in then_z.values():
        copy.wait_recv()
    out[high, :] = smooth[high, :] + y_sum[0] + sum(yz_box[k] for k in range(NZ - 1))
    for copy in then_y.values():
        copy.wait_recv()
    out[low, :] = smooth[low, :] + z_sum[0] + sum(zy_box[k] for k in range(NY - 1))
    for sent in (asks, answers, copies, forwards, along_z, along_y, then_z, then_y):
        for copy in sent.values():
            copy.wait_send()


def per_device(model, source, observed, owner_ids, offsets, lengths):
    block = model.reshape(ROWS, 128)
    f32, i32 = jnp.float32, jnp.int32
    dma = pltpu.SemaphoreType.DMA
    field = (S_DEV, 3, TILE, 8, 128)
    plain = pltpu.VMEM((S_DEV, TILE * 8, 128), f32)
    gradient = pl.pallas_call(
        whole_kernel,
        out_shape=jax.ShapeDtypeStruct((SHARE, 128), f32),
        in_specs=[SMEM, SMEM, SMEM, HBM, HBM, HBM],
        out_specs=VMEM,
        scratch_shapes=[
            pltpu.SMEM((TILES,), i32),
            pltpu.SMEM((OWN * CAP,), i32),
            pltpu.SMEM((OWN, 128), i32),
            pltpu.SMEM((2, OWN, 128), i32),
            pltpu.VMEM((2, OWN, SLOT_ROWS, 128), f32),
            pltpu.VMEM((SHARE, 128), f32),
            pltpu.VMEM((2,) + field, f32),
            pltpu.VMEM((ROWS, 128), f32),
            pltpu.VMEM((S_DEV, 3, LZ, TILE * 128), f32),
            pltpu.VMEM((S_DEV, 3, LZ, TILE * 128), f32),
            pltpu.VMEM((OWN * SLOT_ROWS, 128), f32),
            pltpu.VMEM((OWN, SLOT_ROWS, 128), f32),
            pltpu.VMEM((OWN, SLOT_ROWS, 128), f32),
            pltpu.VMEM(((TILES + 1) * TILE, 128), f32),
            pltpu.VMEM((BLOCKS * SLOT_ROWS, 256), jnp.bfloat16),
            pltpu.VMEM((NZ, NY, SHARE, 128), f32),
            plain,
            pltpu.VMEM((S_DEV, TILE, 8, 128), f32),
            pltpu.VMEM((S_DEV, TILE, 8, 128), f32),
            pltpu.VMEM((3,) + field, f32),
            pltpu.VMEM(field, f32),
            plain,
            pltpu.VMEM((NZ - 1, NY, CUT, 128), f32),
            pltpu.VMEM((2, NY - 1, NZ // 2, SHARE - CUT, 128), f32),
            pltpu.VMEM((NY, CUT, 128), f32),
            pltpu.VMEM((NZ, SHARE - CUT, 128), f32),
            pltpu.VMEM((NY - 1, CUT, 128), f32),
            pltpu.VMEM((NZ - 1, SHARE - CUT, 128), f32),
            dma((3,)),
        ]
        + [dma((OWN,))] * 8
        + [dma((2,)), dma((2, NZ - 1)), dma((2, 2 * (NY - 1))), dma((2, NY - 1)), dma((2, NZ - 1))],
        compiler_params=pltpu.CompilerParams(
            collective_id=0, has_side_effects=True, vmem_limit_bytes=60 << 20
        ),
        name="whole",
    )(owner_ids.transpose(0, 2, 1), offsets, lengths, block, source, observed)
    return gradient[:, None, :]


def solution(mesh):
    placed = (
        P(None, "mdl", None),
        P(("grp", "mdl"), None, None, None),
        P(("grp", "mdl"), None, None, None),
        P(("grp", "mdl"), None, None),
        P(("grp", "mdl"), None),
        P(("grp", "mdl"), None),
    )
    return jax.shard_map(
        per_device, mesh=mesh, in_specs=placed, out_specs=P("grp", "mdl", None), check_vma=False
    )
```

```python
import functools

import jax
import jax.numpy as jnp
from jax import lax
from jax.experimental import pallas as pl
from jax.experimental.pallas import tpu as pltpu
from jax.sharding import PartitionSpec as P

LZ = 8
S_DEV = 2
TILES = S_DEV * LZ
TILE = 32
ROWS = 4096
CAP = 4
AIR = 0.05
BETA = 0.5

NZ, NY, NX = 8, 4, 4
OWN = 2 * NX
SLOT_ROWS = CAP * TILE
SHARE = ROWS // (NZ * NY * 2)

MESH = pl.DeviceIdType.MESH
SMEM = pl.BlockSpec(memory_space=pltpu.SMEM)
VMEM = pl.BlockSpec(memory_space=pltpu.VMEM)
HBM = pl.BlockSpec(memory_space=pl.ANY)
NEAR_FIRST = [(0, 2), (0, 1), (0, 3), (1, 2), (1, 1), (1, 3), (1, 0)]


def here():
    g, m = lax.axis_index("grp"), lax.axis_index("mdl")
    return g // (2 * NY), (g // 2) % NY, g % 2, m // NX, m % NX


def partner(dh, dx):
    z, y, c, h, x = here()
    y = NY - 1 - y if dh % 2 else y
    m = ((h + dh) % 2) * NX + (x + dx) % NX
    return ((z * NY + y) * 2 + c, m), m


def other_core():
    z, y, c, h, x = here()
    return ((z * NY + y) * 2 + 1 - c, h * NX + x)


def meet(ids):
    barrier = pltpu.get_barrier_semaphore()
    for i in ids:
        pl.semaphore_signal(barrier, inc=1, device_id=i, device_id_type=MESH)
    pl.semaphore_wait(barrier, len(ids))


def remote(src, dst, send, recv, to):
    return pltpu.make_async_remote_copy(
        src_ref=src, dst_ref=dst, send_sem=send, recv_sem=recv, device_id=to, device_id_type=MESH
    )


HALF = TILE // 2


def half(v):
    return pltpu.roll(v, 64, 1)


def split(a, b):
    low = lax.broadcasted_iota(jnp.int32, (8, 128), 1) < 64
    return jnp.where(low, a, half(b)), jnp.where(low, half(a), b)


def arrange(source, observed, given):
    def one(k, carry):
        places = [pl.ds(pl.multiple_of((k + d) * 128, 128), 128) for d in (0, HALF)]
        for s in range(S_DEV):
            for a in range(3):
                p, q = split(*[source[s, a, :, at] for at in places])
                given[0, s, a, 2 * k] = -p
                given[0, s, a, 2 * k + 1] = -q
                p, q = split(*[observed[s, a, :, at] for at in places])
                given[1, s, a, 2 * k] = p
                given[1, s, a, 2 * k + 1] = q
        return carry

    lax.fori_loop(0, HALF, one, 0, unroll=4)


def solve(place, lengths, values, given, by_layer, cond, weight, keeps, state, rhs, part):
    lane = lax.broadcasted_iota(jnp.int32, (8, 128), 1)
    layer = lax.broadcasted_iota(jnp.int32, (8, 128), 0)
    row = lax.broadcasted_iota(jnp.int32, (TILE, 128), 0)
    low = lane < 64

    def shift(mask, by, axis):
        def all_of(v):
            return jnp.stack([jnp.where(mask, pltpu.roll(v[i], by, axis), 0.0) for i in range(v.shape[0])])

        return all_of

    y_up, y_down = shift(lane % 64 != 63, 127, 1), shift(lane % 64 != 0, 1, 1)
    z_up, z_down = shift(layer != LZ - 1, LZ - 1, 0), shift(layer != 0, 1, 0)

    for t in range(TILES):
        s, z = t // LZ, t % LZ
        got = values[pl.ds(place[t], TILE), :]
        cond[s, pl.ds(z, TILE, stride=8), :] = jnp.where(row < lengths[s, z], jnp.exp(got), AIR)

    for k in range(HALF):
        for s in range(S_DEV):
            pair = split(*[cond[s, pl.ds((k + d) * 8, 8), :] for d in (0, HALF)])
            for i in range(2):
                w = 0.5 / (4.0 + pair[i])
                weight[s, 2 * k + i] = w
                keeps[s, 2 * k + i] = 0.5 + 4.0 * w

    state[0] = jnp.zeros_like(state[0])

    def phase(p, carry):
        for r in range(TILE):
            for s in range(S_DEV):
                for a in range(3):
                    b = weight[s, r] * (state[p, s, a, r] - given[p, s, a, r])
                    rhs[s, a, r] = b
                    state[p + 1, s, a, r] = b

        def sweep(i, carry):
            for s in range(S_DEV):
                ex, ey, ez = e = [state[p + 1, s, a] for a in range(3)]
                ey_x, ez_x = (jnp.concatenate([v[1:], jnp.where(low, half(v[0]), 0.0)[None]], 0) for v in (ey, ez))
                hx = (y_up(ez) - ez) - (z_up(ey) - ey)
                hy = (z_up(ex) - ex) - (ez_x - ez)
                hz = (ey_x - ey) - (y_up(ex) - ex)
                hy_x, hz_x = (
                    jnp.concatenate([jnp.where(low, 0.0, half(v[TILE - 1]))[None], v[:-1]], 0) for v in (hy, hz)
                )
                back = (
                    (z_down(hy) - hy) - (y_down(hz) - hz),
                    (hz_x - hz) - (z_down(hx) - hx),
                    (y_down(hx) - hx) - (hy_x - hy),
                )
                w, keep = weight[s], keeps[s]
                for a in range(3):
                    state[p + 1, s, a] = keep * e[a] + (rhs[s, a] - w * back[a])
            return carry

        lax.fori_loop(0, 3, sweep, 0)
        return carry

    lax.fori_loop(0, 2, phase, 0)

    for k in range(HALF):
        for s in range(S_DEV):
            pair = [sum(state[1, s, a, 2 * k + i] * state[2, s, a, 2 * k + i] for a in range(3)) for i in range(2)]
            for d, v in zip((0, HALF), split(*pair)):
                at = pl.ds((k + d) * 8, 8)
                part[s, at, :] = -cond[s, at, :] * v

    for t in range(TILES):
        s, z = t // LZ, t % LZ
        got = part[s, pl.ds(z, TILE, stride=8), :]
        by_layer[pl.ds(t * TILE, TILE), :] = jnp.where(row < lengths[s, z], got, 0.0)
    by_layer[pl.ds(TILES * TILE, TILE), :] = jnp.zeros((TILE, 128), jnp.float32)


NEAR = [(0, 0)] + [d for d in NEAR_FIRST if d[0] == 0]
FAR = [d for d in NEAR_FIRST if d[0] == 1]
OWN_ROWS = NY * SHARE
BLOCKS = 2 * NX


def targets(starts, arrived, vals, senders):
    lane = lax.broadcasted_iota(jnp.int32, (8, 128), 1)
    found = []
    for i, (side, m) in enumerate([(side, m) for m in senders for side in range(2)]):
        v = arrived[side, m]
        head = v.astype(jnp.bfloat16)
        at = pl.ds(i * SLOT_ROWS, SLOT_ROWS)
        vals[at, pl.ds(0, 128)] = head
        vals[at, pl.ds(128, 128)] = (v - head.astype(jnp.float32)).astype(jnp.bfloat16)
        s = [starts[side, m, k] for k in range(CAP)]
        t = jnp.where(lane < 2 * TILE, jnp.where(lane < TILE, s[0], s[1]), jnp.where(lane < 3 * TILE, s[2], s[3]))
        found.append(t + lane % TILE)
    return found


def placed_rows(found, vals, rows, j):
    picked = [
        jnp.where(rows == (t - j * (2 * OWN_ROWS))[None], 1.0, 0.0).astype(jnp.bfloat16).reshape(OWN_ROWS, 128)
        for t in found
    ]
    d = jnp.dot(jnp.concatenate(picked, 1), vals[...], preferred_element_type=jnp.float32)
    return (d[:, :128] + d[:, 128:]).reshape(NY, SHARE, 128)


CUT = SHARE // 2
Z_ORDER = [4, 3, 5, 2, 6, 1, 7]


def whole_kernel(
    owner,
    offset,
    lengths,
    block_hbm,
    source_hbm,
    observed_hbm,
    out,
    place,
    holds,
    request,
    starts,
    arrived,
    smooth,
    given,
    block,
    source,
    observed,
    values,
    outbox,
    slots,
    by_layer,
    vals,
    dense,
    *rest,
):
    fields, boxes, sems = rest[:6], rest[6:12], rest[12:]
    z_box, y_box, z_sum, y_sum, zy_box, yz_box = boxes
    (load_sem, ask_send, ask_recv, row_send, row_recv, send, recv, core_send, core_recv, core_sem) = sems[:10]
    z_sem, y_sem, zy_sem, yz_sem = sems[10:]
    z, y, c, h, x = here()
    me = lax.axis_index("mdl")

    def chip(dz, dy):
        return ((((z + dz) % NZ) * NY + (y + dy) % NY) * 2 + c, me)

    barrier = pltpu.get_barrier_semaphore()
    greeted = [partner(*d)[0] for d in NEAR_FIRST] + [other_core()]
    greeted += [chip(d, 0) for d in Z_ORDER] + [chip(0, d) for d in range(1, NY)]
    for i in greeted:
        pl.semaphore_signal(barrier, inc=1, device_id=i, device_id_type=MESH)
    pairs = ((block_hbm, block), (source_hbm, source), (observed_hbm, observed))
    loads = [pltpu.make_async_copy(a, b, load_sem.at[i]) for i, (a, b) in enumerate(pairs)]
    for copy in loads:
        copy.start()

    owners = [owner[t // LZ, 0, t % LZ] for t in range(TILES)]
    firsts = [offset[t // LZ, t % LZ] for t in range(TILES)]
    slot_of = []
    for t in range(TILES):
        slot = owners[t] * CAP
        for i in range(t):
            slot = jnp.where(owners[i] == owners[t], slot + 1, slot)
        slot_of.append(slot)
        place[t] = slot * TILE

    def ask(o, carry):
        for k in range(CAP):
            first = jnp.int32(0)
            for t in range(TILES):
                first = jnp.where(slot_of[t] == o * CAP + k, firsts[t], first)
            request[o, k] = first
        return carry

    lax.fori_loop(0, OWN, ask, 0)
    pl.semaphore_wait(barrier, len(greeted))

    asks, answers = {}, {}
    for dh, dx in NEAR_FIRST:
        to, m = partner(dh, dx)
        k = dh * NX + dx
        asks[dh, dx] = remote(request.at[m], starts.at[0, me], ask_send.at[k], ask_recv.at[k], to)
        asks[dh, dx].start()
    for k in range(CAP):
        starts[0, me, k] = request[me, k]
    loads[0].wait()
    for dh, dx in NEAR_FIRST:
        back = (-dh % 2, -dx % NX)
        asks[back].wait_recv()
        to, m = partner(dh, dx)
        k = dh * NX + dx
        for i in range(CAP):
            outbox[k, pl.ds(i * TILE, TILE), :] = block[pl.ds(starts[0, m, i], TILE), :]
        answers[dh, dx] = remote(
            outbox.at[k], values.at[pl.ds(me * SLOT_ROWS, SLOT_ROWS)], row_send.at[k], row_recv.at[k], to
        )
        answers[dh, dx].start()
    pass_on = remote(starts.at[0], starts.at[1], core_sem.at[0], core_sem.at[1], other_core())
    pass_on.start()
    for k in range(CAP):
        at = pl.ds(me * SLOT_ROWS + k * TILE, TILE)
        values[at, :] = block[pl.ds(starts[0, me, k], TILE), :]
    mine = block[pl.ds(lax.axis_index("grp") * SHARE, SHARE), :]
    lane = lax.broadcasted_iota(jnp.int32, (SHARE, 128), 1)
    left = jnp.where(lane == 0, mine, pltpu.roll(mine, 1, 1))
    right = jnp.where(lane == 127, mine, pltpu.roll(mine, 127, 1))
    smooth[...] = BETA * (2.0 * mine - left - right)
    for copy in loads[1:]:
        copy.wait()
    arrange(source, observed, given)

    def hold(o, carry):
        for k in range(CAP):
            held = jnp.int32(TILES * TILE)
            for t in range(TILES):
                held = jnp.where(place[t] == (o * CAP + k) * TILE, t * TILE, held)
            holds[o * CAP + k] = held
        return carry

    lax.fori_loop(0, OWN, hold, 0)
    for d in NEAR_FIRST:
        answers[d].wait_recv()

    solve(place, lengths, values, given, by_layer, *fields)

    def fill(m, ref):
        for k in range(CAP):
            ref[m, pl.ds(k * TILE, TILE), :] = by_layer[pl.ds(holds[m * CAP + k], TILE), :]

    copies, forwards = {}, {}
    for dh, dx in NEAR_FIRST:
        to, m = partner(dh, dx)
        k = dh * NX + dx
        fill(m, slots)
        copies[dh, dx] = remote(slots.at[m], arrived.at[0, me], send.at[k], recv.at[k], to)
        copies[dh, dx].start()
    fill(me, arrived.at[0])
    pass_on.wait()

    def take(steps):
        for dh, dx in steps:
            _, m = partner(dh, dx)
            if (dh, dx) != (0, 0):
                copies[-dh % 2, -dx % NX].wait_recv()
            k = dh * NX + dx
            forwards[dh, dx] = remote(
                arrived.at[0, m], arrived.at[1, m], core_send.at[k], core_recv.at[k], other_core()
            )
            forwards[dh, dx].start()
        for d in steps:
            forwards[d].wait_recv()
        return [partner(*d)[1] for d in steps]

    shape = (OWN_ROWS // 8, 8, 128)
    at = lax.broadcasted_iota(jnp.int32, shape, 0) * 8 + lax.broadcasted_iota(jnp.int32, shape, 1)
    rows = (at // SHARE) * (2 * SHARE) + at % SHARE + c * SHARE
    found = targets(starts, arrived, vals, take(NEAR))

    def near(d, carry):
        dense[d] = placed_rows(found, vals, rows, (z + d + 2) % NZ)
        return carry

    lax.fori_loop(0, NZ, near, 0, unroll=4)
    found_far = targets(starts, arrived, vals, take(FAR))

    def push(src, dst, sem, i, to):
        copy = remote(src, dst, sem.at[0, i], sem.at[1, i], to)
        copy.start()
        return copy

    low, high = pl.ds(0, CUT), pl.ds(CUT, SHARE - CUT)
    along_z, along_y, then_y, then_z = {}, {}, {}, {}
    parts = (4, 3, 5, 2), (6, 1, 7, 0)
    for part, steps in enumerate(parts):
        for d in steps:
            n = (d - 2) % NZ
            dense[n] = dense[n] + placed_rows(found_far, vals, rows, (z + d) % NZ)
            if d:
                along_z[d] = push(dense.at[n, :, low, :], z_box.at[d - 1], z_sem, d - 1, chip(d, 0))
        for e in (2, 1, 3):
            along_y[part, e] = push(
                dense.at[pl.ds(part * 4, 4), (y + e) % NY, high, :],
                y_box.at[part, e - 1],
                y_sem,
                part * (NY - 1) + e - 1,
                chip(0, e),
            )
    for part, steps in enumerate(parts):
        for e in (2, 1, 3):
            along_y[part, e].wait_recv()
        for d in steps:
            y_sum[d] = dense[(d - 2) % NZ, y, high, :] + sum(y_box[part, k, (d - 2) % 4] for k in range(NY - 1))
            if d:
                then_z[d] = push(y_sum.at[d], yz_box.at[d - 1], yz_sem, d - 1, chip(d, 0))
    for copy in along_z.values():
        copy.wait_recv()
    for d in (2, 1, 3, 0):
        j = (y + d) % NY
        z_sum[d] = dense[NZ - 2, j, low, :] + sum(z_box[k, j] for k in range(NZ - 1))
        if d:
            then_y[d] = push(z_sum.at[d], zy_box.at[d - 1], zy_sem, d - 1, chip(0, d))
    for copy in then_z.values():
        copy.wait_recv()
    out[high, :] = smooth[high, :] + y_sum[0] + sum(yz_box[k] for k in range(NZ - 1))
    for copy in then_y.values():
        copy.wait_recv()
    out[low, :] = smooth[low, :] + z_sum[0] + sum(zy_box[k] for k in range(NY - 1))
    for sent in (asks, answers, copies, forwards, along_z, along_y, then_z, then_y):
        for copy in sent.values():
            copy.wait_send()


def per_device(model, source, observed, owner_ids, offsets, lengths):
    block = model.reshape(ROWS, 128)
    f32, i32 = jnp.float32, jnp.int32
    dma = pltpu.SemaphoreType.DMA
    field = (S_DEV, 3, TILE, 8, 128)
    plain = pltpu.VMEM((S_DEV, TILE * 8, 128), f32)
    gradient = pl.pallas_call(
        whole_kernel,
        out_shape=jax.ShapeDtypeStruct((SHARE, 128), f32),
        in_specs=[SMEM, SMEM, SMEM, HBM, HBM, HBM],
        out_specs=VMEM,
        scratch_shapes=[
            pltpu.SMEM((TILES,), i32),
            pltpu.SMEM((OWN * CAP,), i32),
            pltpu.SMEM((OWN, 128), i32),
            pltpu.SMEM((2, OWN, 128), i32),
            pltpu.VMEM((2, OWN, SLOT_ROWS, 128), f32),
            pltpu.VMEM((SHARE, 128), f32),
            pltpu.VMEM((2,) + field, f32),
            pltpu.VMEM((ROWS, 128), f32),
            pltpu.VMEM((S_DEV, 3, LZ, TILE * 128), f32),
            pltpu.VMEM((S_DEV, 3, LZ, TILE * 128), f32),
            pltpu.VMEM((OWN * SLOT_ROWS, 128), f32),
            pltpu.VMEM((OWN, SLOT_ROWS, 128), f32),
            pltpu.VMEM((OWN, SLOT_ROWS, 128), f32),
            pltpu.VMEM(((TILES + 1) * TILE, 128), f32),
            pltpu.VMEM((BLOCKS * SLOT_ROWS, 256), jnp.bfloat16),
            pltpu.VMEM((NZ, NY, SHARE, 128), f32),
            plain,
            pltpu.VMEM((S_DEV, TILE, 8, 128), f32),
            pltpu.VMEM((S_DEV, TILE, 8, 128), f32),
            pltpu.VMEM((3,) + field, f32),
            pltpu.VMEM(field, f32),
            plain,
            pltpu.VMEM((NZ - 1, NY, CUT, 128), f32),
            pltpu.VMEM((2, NY - 1, NZ // 2, SHARE - CUT, 128), f32),
            pltpu.VMEM((NY, CUT, 128), f32),
            pltpu.VMEM((NZ, SHARE - CUT, 128), f32),
            pltpu.VMEM((NY - 1, CUT, 128), f32),
            pltpu.VMEM((NZ - 1, SHARE - CUT, 128), f32),
            dma((3,)),
        ]
        + [dma((OWN,))] * 8
        + [dma((2,)), dma((2, NZ - 1)), dma((2, 2 * (NY - 1))), dma((2, NY - 1)), dma((2, NZ - 1))],
        compiler_params=pltpu.CompilerParams(
            collective_id=0, has_side_effects=True, vmem_limit_bytes=60 << 20
        ),
        name="whole",
    )(owner_ids.transpose(0, 2, 1), offsets, lengths, block, source, observed)
    return gradient[:, None, :]


def solution(mesh):
    placed = (
        P(None, "mdl", None),
        P(("grp", "mdl"), None, None, None),
        P(("grp", "mdl"), None, None, None),
        P(("grp", "mdl"), None, None),
        P(("grp", "mdl"), None),
        P(("grp", "mdl"), None),
    )
    return jax.shard_map(
        per_device, mesh=mesh, in_specs=placed, out_specs=P("grp", "mdl", None), check_vma=False
    )
```
